32 devices in a mesh: dp: 16 (over z, y, core), mp: 2 (over x).
Axes of the slice: x: 2, y: 2, z: 4, core: 2. Of those that a mesh axis runs over, the one named last changes fastest.
Arguments:
- inputs: bfloat16 [32, 512, 768], P('dp', 'mp'), may hold values from -6 to 6
- pad_counts: int32 [32], P('dp'), may hold values from 0 to 32, as said below
- gainmix_one: bfloat16 [768], replicated, may hold values from 0.099609375 to 1.8984375
- shiftmix_one: bfloat16 [768], replicated, may hold values from -4 to 4
- upweight_one: bfloat16 [768, 3072], P(None, 'mp'), may hold values from -0.21875 to 0.21875
- upbias_one: bfloat16 [3072], P('mp'), may hold values from -6 to 6
- downweight_one: bfloat16 [3072, 768], P('mp'), may hold values from -0.109375 to 0.109375
- downbias_one: bfloat16 [768], replicated, may hold values from -6 to 6
- gainout_one: bfloat16 [768], replicated, may hold values from 0.099609375 to 1.8984375
- shiftout_one: bfloat16 [768], replicated, may hold values from -4 to 4
- gainmix_two: bfloat16 [768], replicated, may hold values from 0.099609375 to 1.8984375
- shiftmix_two: bfloat16 [768], replicated, may hold values from -4 to 4
- upweight_two: bfloat16 [768, 3072], P(None, 'mp'), may hold values from -0.21875 to 0.21875
- upbias_two: bfloat16 [3072], P('mp'), may hold values from -6 to 6
- downweight_two: bfloat16 [3072, 768], P('mp'), may hold values from -0.109375 to 0.109375
- downbias_two: bfloat16 [768], replicated, may hold values from -6 to 6
- gainout_two: bfloat16 [768], replicated, may hold values from 0.099609375 to 1.8984375
- shiftout_two: bfloat16 [768], replicated, may hold values from -4 to 4
- cotangent: bfloat16 [32, 512, 768], P('dp', 'mp'), may hold values from -6 to 6
Outputs:
- outputs: bfloat16 [32, 512, 768], P('dp', 'mp')
- input_grad: float32 [32, 512, 768], P('dp', 'mp')
- gradgainmix_one: float32 [768], replicated
- gradshiftmix_one: float32 [768], replicated
- gradupweight_one: float32 [768, 3072], P(None, 'mp')
- gradupbias_one: float32 [3072], P('mp')
- graddownweight_one: float32 [3072, 768], P('mp')
- graddownbias_one: float32 [768], replicated
- gradgainout_one: float32 [768], replicated
- gradshiftout_one: float32 [768], replicated
- gradgainmix_two: float32 [768], replicated
- gradshiftmix_two: float32 [768], replicated
- gradupweight_two: float32 [768, 3072], P(None, 'mp')
- gradupbias_two: float32 [3072], P('mp')
- graddownweight_two: float32 [3072, 768], P('mp')
- graddownbias_two: float32 [768], replicated
- gradgainout_two: float32 [768], replicated
- gradshiftout_two: float32 [768], replicated
The draws below stay inside these ranges and needn't reach their ends.
Inputs may be any that keep to these rules, and one draw needn't show every extreme that they name: `pad_counts`: some row has exactly 32 pad slots and some row has none.
All inputs are finite; a program needn't handle non-finite values.
Results may differ from the reference program's by a relative error of at most 0.023.
Values may be sent and summed in bfloat16 or wider, within the bound.
No kernel may reach another device: no remote copies, remote signals or barrier semaphores. Data moves between devices by JAX's collectives and lax.ppermute only.
A program may use at most 128 MiB of HBM per device.

```python
import math
import jax
import jax.numpy as jnp
from jax import lax

D = 768
FF = 3072
LEN = 512
ROWS = 32
PADS = 32


def draw_pad_counts(key, part):
    key = jax.random.fold_in(key, 7)
    key_counts, key_full, key_empty = jax.random.split(key, 3)
    counts_drawn = jax.random.randint(key_counts, (ROWS,), 0, PADS + 1)
    indices = jnp.arange(ROWS, dtype=jnp.int32)
    full_row = jax.random.randint(key_full, (), 0, ROWS)
    empty_row = (full_row + 1 + jax.random.randint(key_empty, (), 0, ROWS - 1)) % ROWS
    counts_drawn = jnp.where(indices == full_row, PADS, counts_drawn)
    counts_drawn = jnp.where(indices == empty_row, 0, counts_drawn)
    return counts_drawn.astype(jnp.int32)


def level_of(key, dims, cuts, smallest, high):
    factor_of, own = 1.0, jax.random.fold_in(key, 6)
    for dim, shards_of in cuts:
        steps = jnp.exp(jax.random.uniform(jax.random.fold_in(own, dim), (shards_of,), jnp.float32, smallest / len(cuts), high / len(cuts)))
        factor_of = factor_of * jnp.repeat(steps, dims[dim] // shards_of).reshape([-1 if axis == dim else 1 for axis in range(len(dims))])
    return factor_of


def bell_draw(rng, dims, scale, reach, cuts=(), held_as=jnp.bfloat16):
    level = level_of(rng, dims, cuts, -0.22, 0.18) if cuts else 1.0
    array = jax.random.normal(rng, dims, jnp.float32) * scale * level
    return jnp.minimum(jnp.maximum(array, -reach), reach).astype(held_as)


def setup_inputs(seed: int = 0) -> dict:
    arg_keys = jax.random.split(jax.random.key(seed), 20)
    return {
        "inputs": bell_draw(arg_keys[0], (ROWS, LEN, D), 1.0, 6.0, ((0, 16), (1, 2))),
        "pad_counts": draw_pad_counts(jax.random.fold_in(arg_keys[19], 71), 0),
        "gainmix_one": jnp.clip(1.0 + 0.18 * jax.random.normal(arg_keys[2], (D,), jnp.float32), 0.099609375, 1.8984375).astype(jnp.bfloat16),
        "shiftmix_one": bell_draw(arg_keys[3], (D,), 0.3, 4.0),
        "upweight_one": bell_draw(arg_keys[4], (D, FF), D ** -0.5, 0.21875, ((1, 2),)),
        "upbias_one": bell_draw(arg_keys[5], (FF,), 0.5, 6.0, ((0, 2),)),
        "downweight_one": bell_draw(arg_keys[6], (FF, D), FF ** -0.5, 0.109375, ((0, 2),)),
        "downbias_one": bell_draw(arg_keys[7], (D,), 0.5, 6.0),
        "gainout_one": jnp.clip(1.0 + 0.18 * jax.random.normal(arg_keys[8], (D,), jnp.float32), 0.099609375, 1.8984375).astype(jnp.bfloat16),
        "shiftout_one": bell_draw(arg_keys[9], (D,), 0.3, 4.0),
        "gainmix_two": jnp.clip(1.0 + 0.18 * jax.random.normal(arg_keys[10], (D,), jnp.float32), 0.099609375, 1.8984375).astype(jnp.bfloat16),
        "shiftmix_two": bell_draw(arg_keys[11], (D,), 0.3, 4.0),
        "upweight_two": bell_draw(arg_keys[12], (D, FF), D ** -0.5, 0.21875, ((1, 2),)),
        "upbias_two": bell_draw(arg_keys[13], (FF,), 0.5, 6.0, ((0, 2),)),
        "downweight_two": bell_draw(arg_keys[14], (FF, D), FF ** -0.5, 0.109375, ((0, 2),)),
        "downbias_two": bell_draw(arg_keys[15], (D,), 0.5, 6.0),
        "gainout_two": jnp.clip(1.0 + 0.18 * jax.random.normal(arg_keys[16], (D,), jnp.float32), 0.099609375, 1.8984375).astype(jnp.bfloat16),
        "shiftout_two": bell_draw(arg_keys[17], (D,), 0.3, 4.0),
        "cotangent": bell_draw(arg_keys[18], (ROWS, LEN, D), 1.0, 6.0, ((0, 16), (1, 2))),
    }


norm_eps = 1e-05

@jax.custom_vjp
def low(v):
    return lax.optimization_barrier(v.astype(jnp.bfloat16)).astype(jnp.float32)

@jax.custom_vjp
def low_back(v):
    return v

def low_keep(v):
    return (low(v), None)

def low_pass(kept, grad):
    return (grad,)

def back_keep(v):
    return (v, None)

def back_low(kept, grad):
    return (low(grad),)
low.defvjp(low_keep, low_pass)
low_back.defvjp(back_keep, back_low)

def fourier_table(points):
    indices = jnp.arange(points, dtype=jnp.int32)
    phases = indices[:, None] * indices[None, :] % points
    angles = phases.astype(jnp.float32) * (2.0 * math.pi / points)
    factor = points ** (-0.5)
    return (jnp.cos(angles) * factor, jnp.sin(angles) * factor)

def matmul(left_op, right_op):
    return jnp.matmul(left_op, right_op, precision=lax.Precision.HIGHEST)

def layer_norm(activity, gain_vec, shift_vec):
    center = lax.optimization_barrier(jnp.mean(activity, axis=-1, keepdims=True))
    centered = activity - center
    spread = lax.optimization_barrier(jnp.mean(centered * centered, axis=-1, keepdims=True))
    return centered * lax.rsqrt(spread + norm_eps) * gain_vec + shift_vec

def spectral_mix(masked, tables):
    cos_seq, sin_seq, cos_wid, sin_wid = tables
    rounded = low(masked)
    spectra_cos = low_back(low(matmul(rounded, cos_wid)))
    spectra_sin = low_back(low(matmul(rounded, sin_wid)))
    return matmul(cos_seq, spectra_cos) - matmul(sin_seq, spectra_sin)

def fnet_layer(layer_in, live_mask, params, tables):
    gain_mix, shift_mix, up_weight, up_bias, down_weight, down_bias, gain_out, shift_out = params
    masked = layer_in * live_mask
    mixed = low_back(spectral_mix(masked, tables))
    normed = layer_norm(masked + mixed, gain_mix, shift_mix)
    preact = low_back(matmul(low(normed), up_weight) + up_bias)
    hidden = low(jax.nn.gelu(preact, approximate=True))
    branch = low_back(matmul(hidden, down_weight) + down_bias)
    return layer_norm(normed + branch, gain_out, shift_out) * live_mask

def reference(inputs, pad_counts, gainmix_one, shiftmix_one, upweight_one, upbias_one, downweight_one, downbias_one, gainout_one, shiftout_one, gainmix_two, shiftmix_two, upweight_two, upbias_two, downweight_two, downbias_two, gainout_two, shiftout_two, cotangent):
    first_params = tuple((member.astype(jnp.float32) for member in (gainmix_one, shiftmix_one, upweight_one, upbias_one, downweight_one, downbias_one, gainout_one, shiftout_one)))
    second_params = tuple((member.astype(jnp.float32) for member in (gainmix_two, shiftmix_two, upweight_two, upbias_two, downweight_two, downbias_two, gainout_two, shiftout_two)))
    cos_seq, sin_seq = fourier_table(LEN)
    cos_wid, sin_wid = fourier_table(D)
    tables = (low(cos_seq), low(sin_seq), low(cos_wid), low(sin_wid))
    position = jnp.arange(LEN, dtype=jnp.int32)

    def row_step(totals, row_data):
        row_in, row_pad, row_cot = row_data
        live_mask = (position < LEN - row_pad).astype(jnp.float32)[:, None]

        def forward(layer_in, first_set, second_set):
            middle = fnet_layer(layer_in, live_mask, first_set, tables)
            return fnet_layer(middle, live_mask, second_set, tables)
        row_out, pullback = jax.vjp(forward, row_in.astype(jnp.float32), first_params, second_params)
        row_grad, first_grad, second_grad = pullback(row_cot.astype(jnp.float32))
        totals = jax.tree.map(jnp.add, totals, (first_grad, second_grad))
        return (totals, (row_out.astype(jnp.bfloat16), row_grad))
    initial = jax.tree.map(jnp.zeros_like, (first_params, second_params))
    totals, (outputs, input_grad) = lax.scan(row_step, initial, (inputs, pad_counts, cotangent))
    first_grad, second_grad = totals
    return (outputs, input_grad, first_grad[0], first_grad[1], first_grad[2], first_grad[3], first_grad[4], first_grad[5], first_grad[6], first_grad[7], second_grad[0], second_grad[1], second_grad[2], second_grad[3], second_grad[4], second_grad[5], second_grad[6], second_grad[7])
```

```python
import math

import jax
import jax.numpy as jnp
import numpy as np
from jax import lax
from jax.sharding import PartitionSpec as P

norm_eps = 1e-05
low_type = jnp.bfloat16
wide_type = jnp.float32


def fourier_table(points):
    indices = np.arange(points, dtype=np.int64)
    phases = (indices[:, None] * indices[None, :]) % points
    angles = phases.astype(np.float32) * np.float32(2.0 * math.pi / points)
    factor = np.float32(points ** (-0.5))
    return (np.cos(angles) * factor, np.sin(angles) * factor)


def dot(left, right):
    return jnp.dot(left, right, preferred_element_type=wide_type)


def dot_tn(left, right):
    return lax.dot_general(left, right, (((0,), (0,)), ((), ())), preferred_element_type=wide_type)


def dot_nt(left, right):
    return lax.dot_general(left, right, (((1,), (1,)), ((), ())), preferred_element_type=wide_type)


def normalize(activity):
    center = jnp.mean(activity, axis=-1, keepdims=True)
    centered = activity - center
    spread = jnp.mean(centered * centered, axis=-1, keepdims=True)
    inverse = lax.rsqrt(spread + norm_eps)
    return centered * inverse, inverse


def norm_backward(grad, normal, inverse, gain):
    pulled = grad * gain
    first = jnp.mean(pulled, axis=-1, keepdims=True)
    second = jnp.mean(pulled * normal, axis=-1, keepdims=True)
    return inverse * (pulled - first - normal * second)


def gate_pair(preact):
    scale = math.sqrt(2.0 / math.pi)
    square = preact * preact
    turn = jnp.tanh(scale * (preact + 0.044715 * preact * square))
    half = 0.5 * (1.0 + turn)
    slope = half + (0.5 * scale) * preact * (1.0 - turn * turn) * (1.0 + 3 * 0.044715 * square)
    return (preact * half).astype(low_type), slope.astype(low_type)


def flip_pairs(size, bit):
    return [(index, index ^ bit) for index in range(size)]


def order_halves(bit_value, mine, theirs):
    return jnp.where(
        bit_value == 0,
        jnp.concatenate([mine, theirs], axis=0),
        jnp.concatenate([theirs, mine], axis=0),
    )


def take_half(array, which):
    half = array.shape[0] // 2
    return lax.dynamic_slice_in_dim(array, which * half, half, 0)


def dp_bits():
    return [1 << level for level in range(lax.axis_size("dp").bit_length() - 1)]


def bit_of(bit):
    return (lax.axis_index("dp") // bit) % 2


def dp_swap(array, bit):
    return lax.ppermute(array, "dp", flip_pairs(lax.axis_size("dp"), bit))


def mp_swap(array):
    return lax.ppermute(array, "mp", [(0, 1), (1, 0)])


def add_low(left, right):
    return (left.astype(wide_type) + right.astype(wide_type)).astype(low_type)


def halve_over(array, bit):
    own_bit = bit_of(bit)
    received = dp_swap(take_half(array, 1 - own_bit), bit)
    return add_low(take_half(array, own_bit), received)


def gather_over(array, bit):
    return order_halves(bit_of(bit), array, dp_swap(array, bit))


def fetch_other(weight):
    bits = dp_bits()[:2]
    piece = weight
    for bit in bits:
        piece = take_half(piece, bit_of(bit))
    piece = mp_swap(piece)
    for bit in bits[::-1]:
        piece = gather_over(piece, bit)
    return piece


def gathered_weights(up_weight, up_bias, down_weight):
    if lax.axis_size("mp") == 2:
        return (
            (up_weight, up_bias, down_weight),
            (fetch_other(up_weight), mp_swap(up_bias), fetch_other(down_weight)),
        )
    return (
        (
            lax.all_gather(up_weight, "mp", axis=1, tiled=True),
            lax.all_gather(up_bias, "mp", axis=0, tiled=True),
            lax.all_gather(down_weight, "mp", axis=0, tiled=True),
        ),
    )


def total_large(parts, hidden_axis):
    bits = dp_bits()
    if len(parts) == 2:
        own, other = parts
        other = halve_over(other, bits[0])
        own = halve_over(own, bits[0])
        own = add_low(own, mp_swap(other))
    else:
        own = lax.psum_scatter(parts[0], "mp", scatter_dimension=hidden_axis, tiled=True)
        own = halve_over(own, bits[0])
    for bit in bits[1:]:
        own = halve_over(own, bit)
    for bit in bits[::-1]:
        own = gather_over(own, bit)
    return own.astype(wide_type)


def total_small(vector):
    for bit in dp_bits():
        vector = vector + dp_swap(vector, bit)
    if lax.axis_size("mp") == 2:
        return vector + mp_swap(vector)
    return lax.psum(vector, "mp")


def exchange_rows(array):
    if lax.axis_size("mp") == 2:
        mine = lax.axis_index("mp")
        own = lax.dynamic_index_in_dim(array, mine, 0, keepdims=False)
        given = lax.dynamic_index_in_dim(array, 1 - mine, 0, keepdims=False)
        return jnp.concatenate([own, mp_swap(given)], axis=0)
    return lax.all_to_all(array, "mp", split_axis=0, concat_axis=1, tiled=True)[0]


def return_rows(array):
    if lax.axis_size("mp") == 2:
        mine = lax.axis_index("mp")
        half = array.shape[0] // 2
        own, received = array[:half], mp_swap(array[half:])
        return jnp.where(mine == 0, jnp.stack([own, received]), jnp.stack([received, own]))
    return lax.all_to_all(array[None], "mp", split_axis=1, concat_axis=0, tiled=True)


def layer_forward(layer_in, live_mask, params, weights, tables):
    gain_mix, shift_mix, down_bias, gain_out, shift_out = params
    pair_table, wide_table = tables
    width = layer_in.shape[1]
    masked = layer_in * live_mask
    spectra = dot(masked.astype(low_type), wide_table).astype(low_type)
    stacked = jnp.concatenate([spectra[:, :width], spectra[:, width:]], axis=0)
    summed = masked + dot(pair_table, stacked)
    normal, inverse = normalize(summed)
    normed = normal * gain_mix + shift_mix
    normed_low = normed.astype(low_type)
    branch = down_bias
    kept = []
    for up_weight, up_bias, down_weight in weights:
        hidden, slope = gate_pair(dot(normed_low, up_weight) + up_bias.astype(wide_type))
        branch = branch + dot(hidden, down_weight)
        kept.append((hidden, slope))
    residual = normed + branch
    out_normal, out_inverse = normalize(residual)
    result = (out_normal * gain_out + shift_out) * live_mask
    return result, (summed, normed_low, residual, kept)


def layer_backward(result_cot, live_mask, params, weights, tables, saved):
    gain_mix, shift_mix, down_bias, gain_out, shift_out = params
    pair_table, wide_table = tables
    summed, normed_low, residual, kept = saved
    length = summed.shape[0]
    out_grad = result_cot * live_mask
    out_normal, out_inverse = normalize(residual)
    resid_grad = norm_backward(out_grad, out_normal, out_inverse, gain_out)
    gainout_grad = jnp.sum(out_grad * out_normal, axis=0)
    shiftout_grad = jnp.sum(out_grad, axis=0)
    branch_cot = resid_grad.astype(low_type)
    downbias_grad = jnp.sum(branch_cot, axis=0, dtype=wide_type)
    normed_grad = resid_grad
    up_parts, bias_parts, down_parts = [], [], []
    for (up_weight, up_bias, down_weight), (hidden, slope) in zip(weights[::-1], kept[::-1]):
        preact_cot = (dot_nt(branch_cot, down_weight) * slope.astype(wide_type)).astype(low_type)
        down_parts.append(dot_tn(hidden, branch_cot).astype(low_type))
        up_parts.append(dot_tn(normed_low, preact_cot).astype(low_type))
        bias_parts.append(jnp.sum(preact_cot, axis=0, dtype=wide_type))
        normed_grad = normed_grad + dot_nt(preact_cot, up_weight)
    normal, inverse = normalize(summed)
    summed_grad = norm_backward(normed_grad, normal, inverse, gain_mix)
    gainmix_grad = jnp.sum(normed_grad * normal, axis=0)
    shiftmix_grad = jnp.sum(normed_grad, axis=0)
    summed_low = summed_grad.astype(low_type)
    flat_grad = jnp.concatenate(
        [
            dot_tn(pair_table[:, :length], summed_low).astype(low_type),
            dot_tn(pair_table[:, length:], summed_low).astype(low_type),
        ],
        axis=1,
    )
    masked_grad = (summed_grad + dot_nt(flat_grad, wide_table)) * live_mask
    small = [gainmix_grad, shiftmix_grad, downbias_grad, gainout_grad, shiftout_grad]
    return masked_grad, (up_parts[::-1], down_parts[::-1]), small, bias_parts[::-1]


def on_device(*arguments):
    inputs, pad_counts = arguments[:2]
    layer_args = (arguments[2:10], arguments[10:18])
    cotangent = arguments[18]
    mp_count = lax.axis_size("mp")
    mine = lax.axis_index("mp")
    feature_width = inputs.shape[2]
    row_length = inputs.shape[1] * mp_count
    cos_seq, sin_seq = fourier_table(row_length)
    pair_full = np.concatenate([cos_seq, -sin_seq], axis=1)
    turned = 1 - 2 * ((np.arange(row_length)[:, None] + np.arange(2 * row_length)[None, :]) % 2)
    position = jnp.arange(row_length, dtype=jnp.int32)
    if mp_count == 2:
        pair_table = lax.dynamic_index_in_dim(
            jnp.asarray(np.stack([pair_full, pair_full * turned]), low_type), mine, 0, False
        )
        position = (position + mine * inputs.shape[1]) % row_length
    else:
        pair_table = jnp.asarray(pair_full, low_type)
    wide_table = jnp.asarray(np.concatenate(fourier_table(feature_width), axis=1), low_type)
    tables = (pair_table, wide_table)
    pads = lax.dynamic_index_in_dim(pad_counts, mine, 0, False)
    live_mask = (position < row_length - pads).astype(wide_type)[:, None]
    row_in = exchange_rows(inputs)
    row_cot = exchange_rows(cotangent)
    weights, params = [], []
    for gain_mix, shift_mix, up_weight, up_bias, down_weight, down_bias, gain_out, shift_out in (
        layer_args
    ):
        weights.append(gathered_weights(up_weight, up_bias, down_weight))
        params.append(
            tuple(
                member.astype(wide_type)
                for member in (gain_mix, shift_mix, down_bias, gain_out, shift_out)
            )
        )
    current = row_in.astype(wide_type)
    saved = []
    for level in range(2):
        current, kept = layer_forward(current, live_mask, params[level], weights[level], tables)
        saved.append(kept)
    final_out = return_rows(current.astype(low_type))
    grad = row_cot.astype(wide_type)
    large, small, bias = [None] * 2, [None] * 2, [None] * 2
    for level in (1, 0):
        grad, parts, small[level], bias[level] = layer_backward(
            grad, live_mask, params[level], weights[level], tables, saved[level]
        )
        large[level] = (total_large(parts[0], 1), total_large(parts[1], 0))
    input_grad = return_rows(grad.astype(low_type)).astype(wide_type)
    hidden_own = layer_args[0][3].shape[0]
    pieces = []
    for level in range(2):
        pieces.extend(small[level])
        absolute = (
            bias[level][0]
            if mp_count != 2
            else order_halves(mine, bias[level][0], bias[level][1])
        )
        pieces.append(absolute)
    vector = total_small(jnp.concatenate(pieces))
    results = [final_out, input_grad]
    offset = 0
    for level in range(2):
        vectors = []
        for _ in range(5):
            vectors.append(vector[offset : offset + feature_width])
            offset += feature_width
        bias_total = lax.dynamic_slice_in_dim(
            vector, offset + mine * hidden_own, hidden_own, 0
        )
        offset += hidden_own * mp_count
        gainmix, shiftmix, downbias, gainout, shiftout = vectors
        up_total, down_total = large[level]
        results += [gainmix, shiftmix, up_total, bias_total, down_total, downbias, gainout, shiftout]
    return tuple(results)


def solution(mesh):
    layer_specs = (P(), P(), P(None, "mp"), P("mp"), P("mp", None), P(), P(), P())
    rows = P("dp", "mp", None)
    return jax.shard_map(
        on_device,
        mesh=mesh,
        in_specs=(rows, P("dp"), *layer_specs, *layer_specs, rows),
        out_specs=(rows, rows, *layer_specs, *layer_specs),
        check_vma=False,
    )
```

```python
import math

import jax
import jax.numpy as jnp
import numpy as np
from jax import lax
from jax.experimental import pallas as pl
from jax.sharding import PartitionSpec as P

norm_eps = 1e-05
low_type = jnp.bfloat16
wide_type = jnp.float32


def fourier_table(points):
    indices = np.arange(points, dtype=np.int64)
    phases = (indices[:, None] * indices[None, :]) % points
    angles = phases.astype(np.float32) * np.float32(2.0 * math.pi / points)
    factor = np.float32(points ** (-0.5))
    return (np.cos(angles) * factor, np.sin(angles) * factor)


def dot(left, right):
    return jnp.dot(left, right, preferred_element_type=wide_type)


def dot_tn(left, right):
    return lax.dot_general(left, right, (((0,), (0,)), ((), ())), preferred_element_type=wide_type)


def dot_nt(left, right):
    return lax.dot_general(left, right, (((1,), (1,)), ((), ())), preferred_element_type=wide_type)


def normalize(activity):
    center = jnp.mean(activity, axis=-1, keepdims=True)
    centered = activity - center
    spread = jnp.mean(centered * centered, axis=-1, keepdims=True)
    inverse = lax.rsqrt(spread + norm_eps)
    return centered * inverse, inverse


def norm_backward(grad, normal, inverse, gain):
    pulled = grad * gain
    first = jnp.mean(pulled, axis=-1, keepdims=True)
    second = jnp.mean(pulled * normal, axis=-1, keepdims=True)
    return inverse * (pulled - first - normal * second)


def gate_pair(preact):
    scale = math.sqrt(2.0 / math.pi)
    square = preact * preact
    turn = jnp.tanh(scale * (preact + 0.044715 * preact * square))
    half = 0.5 * (1.0 + turn)
    slope = half + (0.5 * scale) * preact * (1.0 - turn * turn) * (1.0 + 3 * 0.044715 * square)
    return (preact * half).astype(low_type), slope.astype(low_type)


def flip_pairs(size, bit):
    return [(index, index ^ bit) for index in range(size)]


def order_halves(bit_value, mine, theirs, axis=0):
    return jnp.where(
        bit_value == 0,
        jnp.concatenate([mine, theirs], axis=axis),
        jnp.concatenate([theirs, mine], axis=axis),
    )


def take_block(array, which, count=2, axis=0):
    size = array.shape[axis] // count
    return lax.dynamic_slice_in_dim(array, which * size, size, axis)


def dp_bits():
    return [1 << level for level in range(lax.axis_size("dp").bit_length() - 1)]


def bit_of(bit):
    return (lax.axis_index("dp") // bit) % 2


def dp_swap(array, bit):
    return lax.ppermute(array, "dp", flip_pairs(lax.axis_size("dp"), bit))


def mp_swap(array):
    return lax.ppermute(array, "mp", [(0, 1), (1, 0)])


def add_low(left, right):
    return (left.astype(wide_type) + right.astype(wide_type)).astype(low_type)


def gate(value, *earlier):
    def kernel(*refs):
        pass

    anywhere = pl.BlockSpec(memory_space=pl.ANY)
    return pl.pallas_call(
        kernel,
        out_shape=jax.ShapeDtypeStruct(value.shape, value.dtype),
        in_specs=[anywhere] * (1 + len(earlier)),
        out_specs=anywhere,
        input_output_aliases={0: 0},
        name="gate",
    )(value, *earlier)


def fetch_pieces(weight, bits):
    piece = weight
    for bit in bits:
        piece = take_block(piece, bit_of(bit))
    return piece


def fetch_join(piece, bit):
    return order_halves(bit_of(bit), piece, dp_swap(piece, bit))


def far_piece(up_weight, down_weight):
    core = dp_bits()[0]
    place, count = lax.axis_index("dp") // 2, lax.axis_size("dp") // 2
    return jnp.concatenate(
        [
            take_block(take_block(up_weight, bit_of(core), axis=1), place, count),
            take_block(take_block(down_weight, bit_of(core)), place, count),
        ]
    )


def far_weights(pieces):
    half = pieces.shape[1] // 2
    width = pieces.shape[2]
    return pieces[:, :half].reshape(-1, width), pieces[:, half:].reshape(-1, width)


def core_groups():
    return [
        [place for place in range(lax.axis_size("dp")) if place % 2 == which] for which in (0, 1)
    ]


def total_plain(part, hidden_axis):
    own = lax.psum_scatter(part, "mp", scatter_dimension=hidden_axis, tiled=True)
    return lax.psum(own, "dp").astype(wide_type)


def total_small(vector):
    for bit in dp_bits():
        vector = vector + dp_swap(vector, bit)
    if lax.axis_size("mp") == 2:
        return vector + mp_swap(vector)
    return lax.psum(vector, "mp")


def given_row(array):
    return lax.dynamic_index_in_dim(array, 1 - lax.axis_index("mp"), 0, keepdims=False)


def joined_row(array, received):
    own = lax.dynamic_index_in_dim(array, lax.axis_index("mp"), 0, keepdims=False)
    return jnp.concatenate([own, received], axis=0)


def gathered_row(array):
    return lax.all_to_all(array, "mp", split_axis=0, concat_axis=1, tiled=True)[0]


def return_rows(array):
    if lax.axis_size("mp") == 2:
        half = array.shape[0] // 2
        own, received = array[None, :half], mp_swap(array[None, half:])
        return order_halves(lax.axis_index("mp"), own, received)
    return lax.all_to_all(array[None], "mp", split_axis=1, concat_axis=0, tiled=True)


def layer_mix(layer_in, live_mask, params, tables, *earlier):
    gain_mix, shift_mix = params[:2]
    pair_table, wide_table, stack_table = tables
    width = layer_in.shape[1]
    masked = layer_in * live_mask
    spectra = dot(masked.astype(low_type), wide_table).astype(low_type)
    if earlier:
        spectra = gate(spectra, *earlier)
    stacked = jnp.concatenate([spectra[:, :width], spectra[:, width:]], axis=0)
    summed = masked + dot(pair_table, stacked)
    normal, inverse = normalize(summed)
    normed = normal * gain_mix + shift_mix
    return summed, normed, normed.astype(low_type)


def layer_hidden(normed_low, up_weight, up_bias):
    return gate_pair(dot(normed_low, up_weight) + up_bias.astype(wide_type))


def layer_out(normed, branch, live_mask, params):
    down_bias, gain_out, shift_out = params[2:]
    residual = normed + branch + down_bias
    out_normal, out_inverse = normalize(residual)
    result = (out_normal * gain_out + shift_out) * live_mask
    return result, residual


def out_backward(result_cot, live_mask, gain_out, residual):
    out_grad = result_cot * live_mask
    out_normal, out_inverse = normalize(residual)
    resid_grad = norm_backward(out_grad, out_normal, out_inverse, gain_out)
    gainout_grad = jnp.sum(out_grad * out_normal, axis=0)
    shiftout_grad = jnp.sum(out_grad, axis=0)
    branch_cot = resid_grad.astype(low_type)
    downbias_grad = jnp.sum(branch_cot, axis=0, dtype=wide_type)
    return resid_grad, branch_cot, (downbias_grad, gainout_grad, shiftout_grad)


def cot_of(branch_cot, down_weight, slope):
    return (dot_nt(branch_cot, down_weight) * slope.astype(wide_type)).astype(low_type)


def mix_backward(normed_grad, live_mask, gain_mix, summed, tables):
    pair_table, wide_table, stack_table = tables
    length = summed.shape[0]
    normal, inverse = normalize(summed)
    summed_grad = norm_backward(normed_grad, normal, inverse, gain_mix)
    gainmix_grad = jnp.sum(normed_grad * normal, axis=0)
    shiftmix_grad = jnp.sum(normed_grad, axis=0)
    summed_low = summed_grad.astype(low_type)
    flat_grad = jnp.concatenate(
        [
            dot(pair_table[:, :length], summed_low).astype(low_type),
            dot(pair_table[:, length:], summed_low).astype(low_type),
        ],
        axis=1,
    )
    masked_grad = (summed_grad + dot(flat_grad, stack_table)) * live_mask
    return masked_grad, (gainmix_grad, shiftmix_grad)


def paired(first, second):
    return dot_tn(*first) + dot_tn(*second)


def core_swap(array):
    return dp_swap(array, dp_bits()[0])


def shared_forward(normed_low, weights, biases):
    normed_near = core_swap(normed_low)
    kept = []
    for (up_weight, down_weight), bias in zip(weights, biases):
        kept.append(
            (
                layer_hidden(normed_low, up_weight, bias),
                layer_hidden(normed_near, up_weight, bias),
            )
        )
    near_branch = sum(
        dot(near[0], down_weight) for (_, near), (_, down_weight) in zip(kept, weights)
    )
    received = core_swap(near_branch.astype(low_type))
    branch = sum(dot(own[0], down_weight) for (own, _), (_, down_weight) in zip(kept, weights))
    return branch + received.astype(wide_type), normed_near, kept


def far_shape(array):
    bits = len(dp_bits()) - 1
    return array.reshape((2,) * bits + (-1, array.shape[-1]))


def far_scatter(total):
    total = far_shape(total)
    bits = dp_bits()[1:]
    for level, bit in enumerate(bits):
        axis = len(bits) - 1 - level
        which = bit_of(bit)
        given = lax.dynamic_index_in_dim(total, 1 - which, axis, False)
        own = lax.dynamic_index_in_dim(total, which, axis, False)
        total = add_low(own, dp_swap(given, bit))
    return total


def far_gather(piece):
    bits = dp_bits()[1:]
    total = piece
    for level, bit in list(enumerate(bits))[::-1]:
        theirs = dp_swap(total, bit)
        axis = len(bits) - 1 - level
        total = order_halves(
            bit_of(bit), jnp.expand_dims(total, axis), jnp.expand_dims(theirs, axis), axis
        )
    return total.reshape(-1, piece.shape[-1])


def shared_backward(resid_grad, branch_cot, normed_pair, weights, kept, *earlier):
    normed_low, normed_near = normed_pair
    cot_near = core_swap(branch_cot)
    downs, ups, bias = [None] * 2, [None] * 2, [None] * 2
    own_cots, near_cots = [None] * 2, [None] * 2
    for step in (1, 0):
        (hidden, slope), (hidden_near, slope_near) = kept[step]
        downs[step] = paired((hidden, branch_cot), (hidden_near, cot_near)).astype(low_type)
        down_weight = weights[step][1]
        own_cots[step] = cot_of(branch_cot, down_weight, slope)
        near_cots[step] = cot_of(cot_near, down_weight, slope_near)
        bias[step] = jnp.sum(own_cots[step], axis=0, dtype=wide_type) + jnp.sum(
            near_cots[step], axis=0, dtype=wide_type
        )
    for step in (1, 0):
        ups[step] = paired(
            (normed_low, own_cots[step]), (normed_near, near_cots[step])
        ).astype(low_type)
    near_grad = sum(dot_nt(cot, weight[0]) for cot, weight in zip(near_cots, weights))
    near_grad = near_grad.astype(low_type)
    if earlier:
        near_grad = gate(near_grad, *earlier)
    received = core_swap(near_grad)
    normed_grad = resid_grad + sum(dot_nt(cot, weight[0]) for cot, weight in zip(own_cots, weights))
    return normed_grad + received.astype(wide_type), downs, ups, bias


def backward_overlapped(grad, live_mask, params, weights, tables, saved):
    bits = dp_bits()
    core = bit_of(bits[0])
    gain_mix, _, _, gain_out, _ = params[1]
    summed, normed_pair, residual, kept = saved[1]
    width = summed.shape[1]
    resid_grad, branch_cot, small_out = out_backward(grad, live_mask, gain_out, residual)
    normed_grad, downs_two, ups_two, bias_two = shared_backward(
        resid_grad, branch_cot, normed_pair, weights[1], kept
    )
    scattered = lax.psum_scatter(
        jnp.concatenate(
            [
                downs_two[0].reshape(lax.axis_size("dp") // 2, -1, width),
                downs_two[1].reshape(lax.axis_size("dp") // 2, -1, width),
            ],
            axis=1,
        ),
        "dp",
        scatter_dimension=0,
        axis_index_groups=core_groups(),
        tiled=False,
    )
    up_two_other = mp_swap(ups_two[1])
    grad, small_mix = mix_backward(normed_grad, live_mask, gain_mix, summed, tables)
    small_two = small_mix + small_out
    gain_mix, _, _, gain_out, _ = params[0]
    summed, normed_pair, residual, kept = saved[0]
    resid_grad, branch_cot, small_out = out_backward(grad, live_mask, gain_out, residual)
    up_two = add_low(ups_two[0], up_two_other)
    normed_grad, downs_one, ups_one, bias_one = shared_backward(
        resid_grad, branch_cot, normed_pair, weights[0], kept, up_two
    )
    down_one_other = mp_swap(gate(downs_one[1], up_two))
    grad, small_mix = mix_backward(normed_grad, live_mask, gain_mix, summed, tables)
    small_one = small_mix + small_out
    up_two_piece = far_scatter(up_two)
    half = scattered.shape[0] // 2
    down_two_piece = add_low(scattered[:half], mp_swap(scattered[half:]))
    both = lax.all_gather(
        jnp.concatenate([up_two_piece, down_two_piece], axis=0), "dp", axis=0, tiled=False
    )
    down_one = add_low(downs_one[0], down_one_other)
    up_one_other = mp_swap(gate(ups_one[1], down_one))
    down_one = far_gather(far_scatter(down_one))
    up_one = add_low(ups_one[0], up_one_other)
    up_one = far_gather(far_scatter(up_one))
    up_one = order_halves(core, up_one, core_swap(up_one), 1).astype(wide_type)
    down_one = order_halves(core, down_one, core_swap(down_one), 0).astype(wide_type)
    both = both.reshape(lax.axis_size("dp") // 2, 2, 2, -1, width)
    up_two = both[:, :, 0].transpose(0, 2, 1, 3).reshape(-1, 2 * width).astype(wide_type)
    down_two = both[:, :, 1].transpose(1, 0, 2, 3).reshape(-1, width).astype(wide_type)
    large = ((up_one, down_one), (up_two, down_two))
    return grad, large, (small_one, small_two), (bias_one, bias_two)


def backward_plain(grad, live_mask, params, weights, tables, saved):
    large, small, bias = [None] * 2, [None] * 2, [None] * 2
    for level in (1, 0):
        gain_mix, _, _, gain_out, _ = params[level]
        summed, normed_low, residual, kept = saved[level]
        ((up_weight, down_weight),) = weights[level]
        ((hidden, slope),) = kept
        resid_grad, branch_cot, small_out = out_backward(grad, live_mask, gain_out, residual)
        down_grad = dot_tn(hidden, branch_cot).astype(low_type)
        cot = cot_of(branch_cot, down_weight, slope)
        up_grad = dot_tn(normed_low, cot).astype(low_type)
        bias[level] = [jnp.sum(cot, axis=0, dtype=wide_type)]
        grad, small_mix = mix_backward(
            resid_grad + dot_nt(cot, up_weight), live_mask, gain_mix, summed, tables
        )
        small[level] = small_mix + small_out
        large[level] = (total_plain(up_grad, 1), total_plain(down_grad, 0))
    return grad, large, small, bias


def whole_bias(parts):
    if len(parts) == 1:
        return parts[0]
    core, mine = bit_of(dp_bits()[0]), lax.axis_index("mp")
    index = jnp.arange(4, dtype=jnp.int32)[:, None]
    own = jnp.where(index == 2 * mine + core, parts[0][None], 0.0)
    other = jnp.where(index == 2 * (1 - mine) + core, parts[1][None], 0.0)
    return (own + other).reshape(-1)


def on_device(*arguments):
    inputs, pad_counts = arguments[:2]
    layer_args = (arguments[2:10], arguments[10:18])
    cotangent = arguments[18]
    mp_count = lax.axis_size("mp")
    mine = lax.axis_index("mp")
    feature_width = inputs.shape[2]
    row_length = inputs.shape[1] * mp_count
    cos_seq, sin_seq = fourier_table(row_length)
    pair_full = np.concatenate([cos_seq, -sin_seq], axis=1)
    turned = 1 - 2 * ((np.arange(row_length)[:, None] + np.arange(2 * row_length)[None, :]) % 2)
    position = jnp.arange(row_length, dtype=jnp.int32)
    if mp_count == 2:
        pair_table = lax.dynamic_index_in_dim(
            jnp.asarray(np.stack([pair_full, pair_full * turned]), low_type), mine, 0, False
        )
        position = (position + mine * inputs.shape[1]) % row_length
    else:
        pair_table = jnp.asarray(pair_full, low_type)
    wide_table = jnp.asarray(np.concatenate(fourier_table(feature_width), axis=1), low_type)
    stack_table = jnp.asarray(np.concatenate(fourier_table(feature_width), axis=0), low_type)
    tables = (pair_table, wide_table, stack_table)
    pads = lax.dynamic_index_in_dim(pad_counts, mine, 0, False)
    live_mask = (position < row_length - pads).astype(wide_type)[:, None]
    vectors = jnp.stack(
        [member for args in layer_args for member in (args[0], args[1], args[5], args[6], args[7])]
    )
    if mp_count == 2:
        vectors = gate(vectors)
    vectors = vectors.astype(wide_type)
    params = [tuple(vectors[5 * level + step] for step in range(5)) for level in range(2)]
    (up_one, down_one), (up_two, down_two) = [(args[2], args[4]) for args in layer_args]
    biases = jnp.stack([args[3] for args in layer_args])
    saved = []
    if mp_count == 2:
        core, near, far = dp_bits()[:3]
        core_bit = bit_of(core)
        there = lambda array, bits, axis: fetch_pieces(take_block(array, core_bit, axis=axis), bits)
        far_part = mp_swap(far_piece(up_two, down_two))
        received = mp_swap(given_row(inputs))
        up_part = mp_swap(there(up_one, (near, far), 1))
        other_biases = mp_swap(biases)
        down_part = mp_swap(gate(there(down_one, (far, near), 0), received))
        received_cot = mp_swap(gate(given_row(cotangent), down_part))
        far_parts = lax.all_gather(
            far_part, "dp", axis=0, tiled=False, axis_index_groups=core_groups()
        )
        biases = [
            [take_block(array, core_bit, axis=1)[level] for array in (biases, other_biases)]
            for level in range(2)
        ]
        row_in = joined_row(inputs, received).astype(wide_type)
        up_part = fetch_join(up_part, far)
        summed, normed, normed_low = layer_mix(row_in, live_mask, params[0], tables, up_part)
        down_part = fetch_join(down_part, near)
        up_part = fetch_join(up_part, near)
        down_part = fetch_join(down_part, far)
        own_blocks = lambda up, down: (take_block(up, core_bit, axis=1), take_block(down, core_bit))
        weights = [
            (own_blocks(up_one, down_one), (up_part, down_part)),
            (own_blocks(up_two, down_two), far_weights(far_parts)),
        ]
        current = row_in
        for level in range(2):
            if level:
                summed, normed, normed_low = layer_mix(current, live_mask, params[1], tables)
            branch, normed_near, kept = shared_forward(normed_low, weights[level], biases[level])
            current, residual = layer_out(normed, branch, live_mask, params[level])
            saved.append((summed, (normed_low, normed_near), residual, kept))
        row_cot = joined_row(cotangent, received_cot)
    else:
        weights = []
        biases = lax.all_gather(biases, "mp", axis=1, tiled=True)
        current = gathered_row(inputs).astype(wide_type)
        for level, (up_weight, down_weight) in enumerate(((up_one, down_one), (up_two, down_two))):
            up_weight = lax.all_gather(up_weight, "mp", axis=1, tiled=True)
            down_weight = lax.all_gather(down_weight, "mp", axis=0, tiled=True)
            weights.append(((up_weight, down_weight),))
            summed, normed, normed_low = layer_mix(current, live_mask, params[level], tables)
            kept = layer_hidden(normed_low, up_weight, biases[level])
            current, residual = layer_out(
                normed, dot(kept[0], down_weight), live_mask, params[level]
            )
            saved.append((summed, normed_low, residual, (kept,)))
        row_cot = gathered_row(cotangent)
    final_out = return_rows(current.astype(low_type))
    backward = backward_overlapped if mp_count == 2 else backward_plain
    grad, large, small, bias = backward(
        row_cot.astype(wide_type), live_mask, params, weights, tables, saved
    )
    input_grad = return_rows(grad.astype(low_type)).astype(wide_type)
    hidden_own = layer_args[0][3].shape[0]
    pieces = []
    for level in range(2):
        pieces.extend(small[level])
        pieces.append(whole_bias(bias[level]))
    vector = total_small(jnp.concatenate(pieces))
    results = [final_out, input_grad]
    offset = 0
    for level in range(2):
        vectors = []
        for _ in range(5):
            vectors.append(vector[offset : offset + feature_width])
            offset += feature_width
        bias_total = lax.dynamic_slice_in_dim(
            vector, offset + mine * hidden_own, hidden_own, 0
        )
        offset += hidden_own * mp_count
        gainmix, shiftmix, downbias, gainout, shiftout = vectors
        up_total, down_total = large[level]
        results += [gainmix, shiftmix, up_total, bias_total, down_total, downbias, gainout, shiftout]
    return tuple(results)


def solution(mesh):
    layer_specs = (P(), P(), P(None, "mp"), P("mp"), P("mp", None), P(), P(), P())
    rows = P("dp", "mp", None)
    return jax.shard_map(
        on_device,
        mesh=mesh,
        in_specs=(rows, P("dp"), *layer_specs, *layer_specs, rows),
        out_specs=(rows, rows, *layer_specs, *layer_specs),
        check_vma=False,
    )
```

```python
import functools
import math

import jax
import jax.numpy as jnp
import numpy as np
from jax import lax
from jax.experimental import pallas as pl
from jax.experimental.pallas import tpu as pltpu
from jax.sharding import PartitionSpec as P

norm_eps = 1e-05
low_type = jnp.bfloat16
wide_type = jnp.float32
vmem_bytes = 62 * 2**20
window = 4
heavy = 6 * 10**9
weight = [1]


def fourier_table(points):
    indices = np.arange(points, dtype=np.int64)
    phases = (indices[:, None] * indices[None, :]) % points
    angles = phases.astype(np.float32) * np.float32(2.0 * math.pi / points)
    factor = np.float32(points ** (-0.5))
    return (np.cos(angles) * factor, np.sin(angles) * factor)


def dot(left, right):
    return jnp.dot(left, right, preferred_element_type=wide_type)


def dot_tn(left, right):
    return lax.dot_general(left, right, (((0,), (0,)), ((), ())), preferred_element_type=wide_type)


def dot_nt(left, right):
    return lax.dot_general(left, right, (((1,), (1,)), ((), ())), preferred_element_type=wide_type)


def normalize(activity):
    center = jnp.mean(activity, axis=-1, keepdims=True)
    centered = activity - center
    spread = jnp.mean(centered * centered, axis=-1, keepdims=True)
    inverse = lax.rsqrt(spread + norm_eps)
    return centered * inverse, inverse


def norm_backward(grad, normal, inverse, gain):
    pulled = grad * gain
    first = jnp.mean(pulled, axis=-1, keepdims=True)
    second = jnp.mean(pulled * normal, axis=-1, keepdims=True)
    return inverse * (pulled - first - normal * second)


def gate_pair(preact):
    scale = math.sqrt(2.0 / math.pi)
    square = preact * preact
    turn = jnp.tanh(preact * (scale + (0.044715 * scale) * square))
    half = 0.5 + 0.5 * turn
    hidden = preact * half
    slope = half + hidden * (1.0 - turn) * (scale + (3 * 0.044715 * scale) * square)
    return hidden.astype(low_type), slope.astype(low_type)


def flip_pairs(size, bit):
    return [(index, index ^ bit) for index in range(size)]


def order_halves(bit_value, mine, theirs, axis=0):
    return jnp.where(
        bit_value == 0,
        jnp.concatenate([mine, theirs], axis=axis),
        jnp.concatenate([theirs, mine], axis=axis),
    )


def take_block(array, which, count=2, axis=0):
    size = array.shape[axis] // count
    return lax.dynamic_slice_in_dim(array, which * size, size, axis)


def dp_bits():
    return [1 << level for level in range(lax.axis_size("dp").bit_length() - 1)]


def bit_of(bit):
    return (lax.axis_index("dp") // bit) % 2


def dp_swap(array, bit):
    return lax.ppermute(array, "dp", flip_pairs(lax.axis_size("dp"), bit))


def mp_swap(array):
    return lax.ppermute(array, "mp", [(0, 1), (1, 0)])


def add_low(left, right):
    return (left.astype(wide_type) + right.astype(wide_type)).astype(low_type)


def gate(value, *earlier):
    def kernel(*refs):
        pass

    anywhere = pl.BlockSpec(memory_space=pl.ANY)
    return pl.pallas_call(
        kernel,
        out_shape=jax.ShapeDtypeStruct(value.shape, value.dtype),
        in_specs=[anywhere] * (1 + len(earlier)),
        out_specs=anywhere,
        input_output_aliases={0: 0},
        name="gate",
    )(value, *earlier)


def fetch_join(piece, bit):
    return order_halves(bit_of(bit), piece, dp_swap(piece, bit))


def bounce(name, jobs, shapes, arrays, earlier=()):
    count, late, given = len(arrays), len(earlier), len(shapes)

    def kernel(*refs):
        targets = refs[count + late : count + late + given]
        held, sems = refs[count + late + given : -1], refs[-1]
        work = jobs(refs[:count], held)
        copies = [
            pltpu.make_async_copy(source, target, sems.at[given + index])
            for index, (_, source, target) in enumerate(work)
        ]
        for copy in copies:
            copy.start()
        leaving = [
            pltpu.make_async_copy(source, target, sems.at[index])
            for index, (source, target) in enumerate(zip(held, targets))
        ]
        for slot in range(given):
            for (place, _, _), copy in zip(work, copies):
                if place == slot:
                    copy.wait()
            leaving[slot].start()
        for copy in leaving:
            copy.wait()

    space = pl.BlockSpec(memory_space=pltpu.HBM)
    return pl.pallas_call(
        kernel,
        out_shape=[jax.ShapeDtypeStruct(shape, low_type) for shape in shapes],
        in_specs=[space] * count + [pl.BlockSpec(memory_space=pl.ANY)] * late,
        out_specs=[space] * given,
        scratch_shapes=[pltpu.VMEM(shape, low_type) for shape in shapes]
        + [pltpu.SemaphoreType.DMA((4 * given,))],
        compiler_params=pltpu.CompilerParams(vmem_limit_bytes=vmem_bytes),
        name=name,
    )(*arrays, *earlier)


def span(index, count):
    return pl.ds(pl.multiple_of(index * count, count), count)


def cut_first(inputs, up_weight):
    length, width = inputs.shape[1:]
    size = up_weight.shape[1] // 2
    rows = width // lax.axis_size("dp")

    def jobs(sources, held):
        own = sources[1].at[span(lax.axis_index("dp"), rows)]
        return [
            (0, own.at[:, pl.ds(0, size)], held[0].at[pl.ds(0, rows)]),
            (0, own.at[:, pl.ds(size, size)], held[0].at[pl.ds(rows, rows)]),
            (1, sources[0].at[1 - mp_place()], held[1]),
        ]

    shapes = ((2 * rows, size), (length, width))
    return bounce("cut_first", jobs, shapes, (inputs, up_weight))


def cut_next(cotangent, down_one, up_two, down_two, earlier):
    length, width = cotangent.shape[1:]
    size = up_two.shape[1] // 2
    quarter = (width // 4, size // 4)

    def jobs(sources, held):
        cots, down_a, up_b, down_b = sources
        place, core = lax.axis_index("dp"), core_place()
        near, away = lax.rem(place // 2, 2), lax.rem(place // 4, 2)
        up = up_b.at[span(2 * near + away, quarter[0]), span(core, size)]
        down = down_b.at[span(core * 4 + 2 * away + near, quarter[1])]
        return [
            (0, down_a.at[span(core, size)], held[0]),
            (1, up, held[1]),
            (2, down, held[2]),
            (3, cots.at[1 - mp_place()], held[3]),
        ]

    shapes = ((size, width), (quarter[0], size), (quarter[1], width), (length, width))
    return bounce("cut_next", jobs, shapes, (cotangent, down_one, up_two, down_two), earlier)


def select_rows(rows, count):
    index = lax.broadcasted_iota(jnp.int32, (count, rows[0].shape[0]), 0)
    total = jnp.zeros(index.shape, wide_type)
    for place, row in enumerate(rows):
        total = jnp.where(index == place, row.astype(wide_type)[None], total)
    return total


def core_groups():
    return [
        [place for place in range(lax.axis_size("dp")) if place % 2 == which] for which in (0, 1)
    ]


def total_plain(part, hidden_axis):
    own = lax.psum_scatter(part, "mp", scatter_dimension=hidden_axis, tiled=True)
    return lax.psum(own, "dp").astype(wide_type)


def total_small(vector):
    for bit in dp_bits():
        vector = vector + dp_swap(vector, bit)
    if lax.axis_size("mp") == 2:
        return vector + mp_swap(vector)
    return lax.psum(vector, "mp")


def given_row(array):
    return lax.dynamic_index_in_dim(array, 1 - lax.axis_index("mp"), 0, keepdims=False)


def gathered_row(array):
    return lax.all_to_all(array, "mp", split_axis=0, concat_axis=1, tiled=True)[0]


def return_rows(array):
    return lax.all_to_all(array[None], "mp", split_axis=1, concat_axis=0, tiled=True)


def staged(name, body, loads, outs, earlier=(), scratch=(), flops=0, stress=0):
    count, late, given = len(loads), len(earlier), len(outs)

    def kernel(*refs):
        sources = refs[1 : 1 + count]
        targets = refs[1 + count + late : 1 + count + late + given]
        rest = refs[1 + count + late + given :]
        held, made = rest[:count], rest[count : count + given]
        in_sems, out_sems, *extra = rest[count + given :]
        copies, begun, sent = {}, set(), []
        for index, load in enumerate(loads):
            view = load[2](sources[index])
            copies[index] = pltpu.make_async_copy(view, held[index], in_sems.at[index])
        queue = sorted(range(count), key=lambda index: math.prod(loads[index][1]) > 2**16)

        def begin(index):
            if index not in begun:
                copies[index].start()
                begun.add(index)

        def get(index):
            begin(index)
            if index in copies:
                copies.pop(index).wait()
                while sum(place in copies for place in begun) < window and len(begun) < count:
                    begin(next(place for place in queue if place not in begun))
            return held[index]

        for index in queue:
            if math.prod(loads[index][1]) <= 2**16 or len(begun) < window:
                begin(index)

        def done(*indices):
            for index in indices:
                slot = len(sent)
                if isinstance(index, tuple):
                    index, place = index
                    source, target = made[index].at[place], targets[index].at[place]
                else:
                    source, target = made[index], targets[index]
                copy = pltpu.make_async_copy(source, target, out_sems.at[slot])
                copy.start()
                sent.append((index, copy))

        body(get, made, done, extra, refs[0])
        for index in list(copies):
            get(index)
        left = {index for index, _ in sent}
        done(*[index for index in range(given) if index not in left])
        for _, copy in sent:
            copy.wait()

    space = pl.BlockSpec(memory_space=pltpu.HBM)
    moved = sum(math.prod(load[1]) * load[0].dtype.itemsize for load in loads)
    moved += sum(math.prod(out[0]) * jnp.dtype(out[1]).itemsize for out in outs)
    call = pl.pallas_call(
        kernel,
        out_shape=[jax.ShapeDtypeStruct(*out) for out in outs],
        in_specs=[pl.BlockSpec(memory_space=pltpu.SMEM)]
        + [space] * count
        + [pl.BlockSpec(memory_space=pl.ANY)] * late,
        out_specs=[space] * given,
        cost_estimate=pl.CostEstimate(
            flops=1 + stress * flops, bytes_accessed=1 + stress * moved, transcendentals=0
        ),
        scratch_shapes=[pltpu.VMEM(load[1], load[0].dtype) for load in loads]
        + [pltpu.VMEM(*out) for out in outs]
        + [pltpu.SemaphoreType.DMA((count,)), pltpu.SemaphoreType.DMA((2 * given,))]
        + list(scratch),
        compiler_params=pltpu.CompilerParams(vmem_limit_bytes=vmem_bytes),
        name=name,
    )
    return lambda pads: call(pads, *[load[0] for load in loads], *earlier)


def whole(array):
    return (array, array.shape, lambda ref: ref)


def part(array, index):
    return (array, array.shape[1:], lambda ref: ref.at[index()])


def mp_place():
    return lax.axis_index("mp")


def core_place():
    return lax.rem(lax.axis_index("dp"), 2)


def share(flip):
    return (core_place() + flip) % 2


def own_block(up_weight, down_weight, flip):
    width, size = up_weight.shape[0], up_weight.shape[1] // 2

    def span():
        return pl.ds(pl.multiple_of(share(flip) * size, size), size)

    return (
        (up_weight, (width, size), lambda ref: ref.at[:, span()]),
        (down_weight, (size, width), lambda ref: ref.at[span()]),
    )


def far_columns(pieces, flip):
    places, rows, size = pieces.shape
    half = rows // 2
    return (
        pieces,
        (places, half, size),
        lambda ref: ref.at[:, pl.ds(pl.multiple_of(share(flip) * half, half), half)],
    )


def matrix(ref):
    return ref[...].reshape(-1, ref.shape[-1])


def tiles(total, size):
    return [slice(start, start + size) for start in range(0, total, size)]


def live_rows(pads_ref, rows, length):
    place = lax.broadcasted_iota(jnp.int32, (rows.stop - rows.start, 1), 0) + rows.start
    place = lax.rem(place + mp_place() * (length // 2), length)
    return (place < length - pads_ref[mp_place()]).astype(wide_type)


def row_of(ref, index):
    return ref[index : index + 1, :]


row_tile = 128


def mix_rows(summed, normed, low, spectra, wide_table, pair_table, vectors):
    length, width = summed.shape
    low[...] = summed[...].astype(low_type)
    wide = wide_table()
    for columns in tiles(2 * width, width):
        spectra[:, columns] = dot(low[...], wide[:, columns]).astype(low_type)
    pair = pair_table()
    summed[...] += dot(pair[:, :length], spectra[:, :width])
    summed[...] += dot(pair[:, length:], spectra[:, width:])
    for rows in tiles(length, row_tile):
        normal, _ = normalize(summed[rows, :])
        value = normal * row_of(vectors, 0) + row_of(vectors, 1)
        normed[rows, :] = value
        low[rows, :] = value.astype(low_type)


def feed_block(low, up_weight, bias, down_weight, hidden, slope):
    hidden[...], slope[...] = gate_pair(dot(low[...], matrix(up_weight())) + bias)
    return dot(hidden[...], matrix(down_weight()))


def out_norm(residual, normed, parts, vectors):
    for rows in tiles(residual.shape[0], row_tile):
        value = normed[rows, :]
        for item in parts:
            value = value + item[rows, :]
        value = value + row_of(vectors, 2)
        residual[rows, :] = value
        normal, _ = normalize(value)
        yield rows, normal * row_of(vectors, 3) + row_of(vectors, 4)


def enter_body(get, made, done, extra, pads_ref):
    summed, normed, low, partial, hidden, slope = made
    (spectra,) = extra
    length, width = summed.shape
    half = length // 2
    for rows in tiles(length, row_tile):
        start = rows.start % half
        piece = get(rows.start // half)[start : start + row_tile, :].astype(wide_type)
        summed[rows, :] = piece * live_rows(pads_ref, rows, length)
    vectors = get(4)
    mix_rows(summed, normed, low, spectra, lambda: get(2), lambda: get(3), vectors)
    done(0, 1, 2)
    for block in range(2):
        value = feed_block(
            low,
            lambda: get(5 + 2 * block),
            row_of(vectors, 5 + block),
            lambda: get(6 + 2 * block),
            hidden.at[block],
            slope.at[block],
        )
        partial[...] = value if block == 0 else partial[...] + value


def enter(inputs, received, tables, vectors, blocks, pads):
    pair_table, wide_table, _ = tables
    length, width = 2 * received.shape[0], received.shape[1]
    size = blocks[0][0][1][1]
    loads = [part(inputs, mp_place), whole(received), whole(wide_table)]
    loads += [part(pair_table, mp_place), whole(vectors), *blocks[0], *blocks[1]]
    rows = (length, width)
    return staged(
        "enter",
        enter_body,
        loads,
        [(rows, wide_type), (rows, wide_type), (rows, low_type), (rows, wide_type)]
        + [((2, length, size), low_type)] * 2,
        (),
        [pltpu.VMEM((length, 2 * width), low_type)],
        4 * length * width * (length + width + 2 * size),
    )(pads)


def rest_body(get, made, done, extra, pads_ref):
    hidden, slope, residual, result = made
    (total,) = extra
    length = result.shape[0]
    low, vectors = get(0), get(5)
    for block in range(2):
        value = feed_block(
            low,
            lambda: get(1 + 2 * block),
            row_of(vectors, 7 + block),
            lambda: get(2 + 2 * block),
            hidden.at[block],
            slope.at[block],
        )
        total[...] = value if block == 0 else total[...] + value
    done(0, 1)
    for rows, value in out_norm(residual, get(6), (total, get(7)), vectors):
        result[rows, :] = value * live_rows(pads_ref, rows, length)


def rest(low, normed, partial, vectors, blocks, pads, earlier=()):
    length, width = rows = low.shape
    size = blocks[0][1][1][0] if len(blocks[0][1][1]) == 2 else width
    loads = [whole(low), *blocks[0], *blocks[1], whole(vectors), whole(normed), whole(partial)]
    return staged(
        "rest",
        rest_body,
        loads,
        [((2, length, size), low_type)] * 2 + [(rows, wide_type)] * 2,
        earlier,
        [pltpu.VMEM(rows, wide_type)],
        8 * length * width * size,
    )(pads)


def again_body(get, made, done, extra, pads_ref):
    summed, normed, low = made
    (spectra,) = extra
    summed[...] = get(0)[...]
    mix_rows(summed, normed, low, spectra, lambda: get(1), lambda: get(2), get(3))


def again(result, tables, vectors, pads, earlier=()):
    pair_table, wide_table, _ = tables
    length, width = rows = result.shape
    loads = [whole(result), whole(wide_table), part(pair_table, mp_place), whole(vectors)]
    return staged(
        "again",
        again_body,
        loads,
        [(rows, wide_type), (rows, wide_type), (rows, low_type)],
        earlier,
        [pltpu.VMEM((length, 2 * width), low_type)],
        4 * length * width * (length + width),
    )(pads)


def some_body(first, count, get, made, done, extra, pads_ref):
    partial, hidden, slope = made
    low, vectors = get(0), get(1)
    for block in range(count):
        value = feed_block(
            low,
            lambda: get(2 + 2 * block),
            row_of(vectors, first + block),
            lambda: get(3 + 2 * block),
            hidden.at[block],
            slope.at[block],
        )
        if block or first > 5:
            before = get(2 + 2 * count) if block == 0 else partial
            value = value + before[...]
        partial[...] = value


def some(first, low, vectors, blocks, pads, before=(), earlier=()):
    length, width = rows = low.shape
    size = blocks[0][0][1][1]
    loads = [whole(low), whole(vectors)]
    for block in blocks:
        loads += list(block)
    loads += [whole(array) for array in before]
    count = len(blocks)
    return staged(
        "some",
        functools.partial(some_body, first, count),
        loads,
        [(rows, wide_type)] + [((count, length, size), low_type)] * 2,
        earlier,
        (),
        4 * count * length * width * size,
    )(pads)


def down_grads(hiddens, cot, keep, send):
    for step, target in ((1, send), (0, keep)):
        for half in range(2):
            value = dot_tn(hiddens[2 * half + step][...], cot[...]).astype(low_type)
            if len(target.shape) == 4:
                target[:, half] = value.reshape(target.shape[0], *target.shape[2:])
            else:
                target[half] = value


def leave_body(get, made, done, extra, pads_ref):
    out_own, out_given, resid, cot, small, slope, keep, send = made
    hidden, total, residual = extra
    length, width = resid.shape
    half = length // 2
    low, vectors = get(0), get(3)
    total[...] = feed_block(
        low, lambda: get(1), row_of(vectors, 8), lambda: get(2), hidden, slope
    )
    done(5)
    sums = [jnp.zeros((1, width), wide_type)] * 3
    for rows, value in out_norm(residual, get(4), (total, get(5)), vectors):
        live = live_rows(pads_ref, rows, length)
        start = rows.start % half
        target = (out_own, out_given)[rows.start // half]
        target[start : start + row_tile, :] = (value * live).astype(low_type)
        grad = get(6 + rows.start // half)[start : start + row_tile, :].astype(wide_type) * live
        resid[rows, :], cot[rows, :] = out_rows(grad, residual[rows, :], row_of(vectors, 3), sums)
    small[...] = jnp.zeros_like(small)
    for index, value in enumerate(sums):
        small[index : index + 1, :] = value
    done(0, 1, 2, 3, 4)
    own, mine = get(8), get(9)
    down_grads((own.at[0], own.at[1], mine, hidden), cot, keep, send)


def leave(low, normed, partial, vectors, block, cotangent, received, hiddens, pads, earlier=()):
    length, width = rows = low.shape
    size = hiddens[0].shape[2]
    shares = lax.axis_size("dp") // 2
    loads = [whole(low), *block, whole(vectors), whole(normed), whole(partial)]
    loads += [part(cotangent, mp_place), whole(received)]
    loads += [whole(hiddens[0]), part(hiddens[1], lambda: 0)]
    half, grads = (length // 2, width), ((shares, 2, size // shares, width), low_type)
    return staged(
        "leave",
        leave_body,
        loads,
        [(half, low_type), (half, low_type), (rows, wide_type), (rows, low_type)]
        + [((8, width), wide_type), ((length, size), low_type), grads, grads],
        earlier,
        [pltpu.VMEM((length, size), low_type)] + [pltpu.VMEM(rows, wide_type)] * 2,
        12 * length * width * size,
    )(pads)


def out_rows(grad, residual, gain, sums):
    normal, inverse = normalize(residual)
    resid_grad = norm_backward(grad, normal, inverse, gain)
    low = resid_grad.astype(low_type)
    parts = (grad * normal, grad, low.astype(wide_type))
    for index, value in enumerate(parts):
        sums[index] = sums[index] + jnp.sum(value, axis=0, keepdims=True)
    return resid_grad, low


def cot_body(get, made, done, extra, pads_ref):
    grads, total, small = made
    (cots,) = extra
    branch_cot = get(0)
    small[...] = jnp.zeros_like(small)
    places = ((1, 2, 5), (6, 7, 8))
    for half in range(2):
        down_weight, slope, up_weight = places[half]
        value = dot_nt(branch_cot[...], matrix(get(down_weight)))
        value = (value * get(slope)[...].astype(wide_type)).astype(low_type)
        cots[...] = value
        small[half : half + 1, :] = jnp.sum(value.astype(wide_type), axis=0, keepdims=True)
        grads[half] = dot_tn(get(3)[...], cots[...]).astype(low_type)
        done((0, half))
        before = get(4) if half == 0 else total
        total[...] = before[...] + dot_nt(cots[...], matrix(get(up_weight)))


def cot_rows(branch_cot, low, before, slopes, blocks, pads, earlier=()):
    length, width = rows = low.shape
    (up_a, down_a), (up_b, down_b) = blocks
    loads = [whole(branch_cot), down_a, slopes[0], whole(low), whole(before), up_a]
    loads += [down_b, slopes[1], up_b]
    size = slopes[0][1][1]
    return staged(
        "cot_rows",
        cot_body,
        loads,
        [((2, width, size), low_type), (rows, wide_type), ((8, size), wide_type)],
        earlier,
        [pltpu.VMEM((length, size), low_type)],
        12 * length * width * size,
        20,
    )(pads)


def small_body(get, made, done, extra, pads_ref):
    total = made[0]
    width = total.shape[1]
    index = lax.broadcasted_iota(jnp.int32, (4, 1), 0)
    for level in range(2):
        mix, out, *biases = (get(4 * level + step) for step in range(4))
        start = 9 * level
        total[start : start + 2, :] = mix[0:2, :]
        first = 0 if level else 2
        total[start + 2 : start + 3, :] = out[first + 2 : first + 3, :]
        total[start + 3 : start + 5, :] = out[first : first + 2, :]
        rows = jnp.zeros((4, width), wide_type)
        for block in range(4):
            half = (mp_place() + block // 2) % 2
            rows = rows + jnp.where(
                index == 2 * half + share(block % 2),
                biases[block % 2][block // 2 : block // 2 + 1, :],
                0.0,
            )
        total[start + 5 : start + 9, :] = rows
    total[18:, :] = jnp.zeros((total.shape[0] - 18, width), wide_type)


def small_matrix(parts, pads):
    loads = [whole(array) for level in parts for array in level]
    width = parts[0][0].shape[1]
    outs = [((24, width), wide_type)]
    return staged("small_matrix", small_body, loads, outs)(pads)[0]


def widen(mine, theirs, axis, earlier):
    size = mine.shape[axis]
    shape = tuple(2 * extent if place == axis else extent for place, extent in enumerate(mine.shape))

    def kernel(own, near, *refs):
        target, first, second, low_first, low_second, sems = refs[len(earlier) :]
        core = core_place()
        copies = [
            pltpu.make_async_copy(own, low_first, sems.at[0]),
            pltpu.make_async_copy(near, low_second, sems.at[1]),
        ]
        for copy in copies:
            copy.start()
        leaving = []
        for copy, source, held, place, sem in (
            (copies[0], low_first, first, core, 2),
            (copies[1], low_second, second, 1 - core, 3),
        ):
            copy.wait()
            held[...] = source[...].astype(wide_type)
            span = pl.ds(pl.multiple_of(place * size, size), size)
            where = target.at[:, span] if axis else target.at[span]
            leaving.append(pltpu.make_async_copy(held, where, sems.at[sem]))
            leaving[-1].start()
        for copy in leaving:
            copy.wait()

    far = pl.BlockSpec(memory_space=pltpu.HBM)
    return pl.pallas_call(
        kernel,
        out_shape=jax.ShapeDtypeStruct(shape, wide_type),
        in_specs=[far] * 2 + [pl.BlockSpec(memory_space=pl.ANY)] * len(earlier),
        out_specs=far,
        scratch_shapes=[pltpu.VMEM(mine.shape, wide_type)] * 2
        + [pltpu.VMEM(mine.shape, low_type)] * 2
        + [pltpu.SemaphoreType.DMA((4,))],
        compiler_params=pltpu.CompilerParams(vmem_limit_bytes=vmem_bytes),
        cost_estimate=pl.CostEstimate(flops=weight[0], bytes_accessed=1, transcendentals=0),
        name="widen",
    )(mine, theirs, *earlier)


def widen_gathered(both, width, earlier):
    shares = both.shape[0] // 2
    rows = both.shape[1] // 2
    pieces = both.reshape(shares, 2, 2, rows, width)

    def kernel(source, *refs):
        up, down, low, held, sems = refs[len(earlier) :]
        copies = [
            pltpu.make_async_copy(
                source.at[:, core, kind], low.at[2 * kind + core], sems.at[2 * kind + core]
            )
            for kind in range(2)
            for core in range(2)
        ]
        for copy in copies:
            copy.start()
        leaving = []
        for kind in range(2):
            for core in range(2):
                slot = 2 * kind + core
                copies[slot].wait()
                held[slot] = low[slot].reshape(shares * rows, width).astype(wide_type)
                span = pl.ds(core * width, width)
                where = down.at[pl.ds(core * shares * rows, shares * rows)] if kind else up.at[:, span]
                leaving.append(pltpu.make_async_copy(held.at[slot], where, sems.at[4 + slot]))
                leaving[-1].start()
        for copy in leaving:
            copy.wait()

    far = pl.BlockSpec(memory_space=pltpu.HBM)
    return pl.pallas_call(
        kernel,
        out_shape=[
            jax.ShapeDtypeStruct((shares * rows, 2 * width), wide_type),
            jax.ShapeDtypeStruct((2 * shares * rows, width), wide_type),
        ],
        in_specs=[far] + [pl.BlockSpec(memory_space=pl.ANY)] * len(earlier),
        out_specs=[far] * 2,
        scratch_shapes=[
            pltpu.VMEM((4, shares, rows, width), low_type),
            pltpu.VMEM((4, shares * rows, width), wide_type),
            pltpu.SemaphoreType.DMA((8,)),
        ],
        compiler_params=pltpu.CompilerParams(vmem_limit_bytes=vmem_bytes),
        cost_estimate=pl.CostEstimate(flops=weight[0], bytes_accessed=1, transcendentals=0),
        name="widen_gathered",
    )(pieces, *earlier)


def place_rows(own, received, kind, earlier=()):
    length, width = own.shape

    def kernel(mine, theirs, *refs):
        target, low_mine, low_theirs, first, second, sems = refs[len(earlier) :]
        copies = [
            pltpu.make_async_copy(source, room, sems.at[index])
            for index, (source, room) in enumerate(((mine, low_mine), (theirs, low_theirs)))
        ]
        for copy in copies:
            copy.start()
        leaving = []
        for index, (room, made, place) in enumerate(
            ((low_mine, first, mp_place()), (low_theirs, second, 1 - mp_place()))
        ):
            copies[index].wait()
            made[...] = room[...].astype(kind)
            leaving.append(pltpu.make_async_copy(made, target.at[place], sems.at[2 + index]))
            leaving[-1].start()
        for copy in leaving:
            copy.wait()

    space = pl.BlockSpec(memory_space=pltpu.HBM)
    return pl.pallas_call(
        kernel,
        out_shape=jax.ShapeDtypeStruct((2, length, width), kind),
        in_specs=[space] * 2 + [pl.BlockSpec(memory_space=pl.ANY)] * len(earlier),
        out_specs=space,
        scratch_shapes=[pltpu.VMEM(own.shape, own.dtype), pltpu.VMEM(own.shape, received.dtype)]
        + [pltpu.VMEM(own.shape, kind)] * 2
        + [pltpu.SemaphoreType.DMA((4,))],
        compiler_params=pltpu.CompilerParams(vmem_limit_bytes=vmem_bytes),
        cost_estimate=pl.CostEstimate(flops=weight[0], bytes_accessed=1, transcendentals=0),
        name="place_rows",
    )(own, received, *earlier)


def swap(array, bit):
    return mp_swap(array) if bit == "mp" else dp_swap(array, bit)


def add_small(left, right, earlier):
    def kernel(first, second, *refs):
        refs[-1][...] = first[...] + second[...]

    inside = pl.BlockSpec(memory_space=pltpu.VMEM)
    return pl.pallas_call(
        kernel,
        out_shape=jax.ShapeDtypeStruct(left.shape, left.dtype),
        in_specs=[inside] * 2 + [pl.BlockSpec(memory_space=pl.ANY)] * len(earlier),
        out_specs=inside,
        cost_estimate=pl.CostEstimate(flops=weight[0], bytes_accessed=1, transcendentals=0),
        name="add_small",
    )(left, right, *earlier)


class SmallTotal:
    def __init__(self, total):
        self.total = total
        self.steps = [*dp_bits(), "mp"]
        self.received = swap(total, self.steps.pop(0))

    def finish(self, *earlier):
        self.total = add_small(self.total, self.received, earlier)
        if self.steps:
            self.received = swap(self.total, self.steps.pop(0))
        return self.total


def unpack_small(total, earlier):
    width = total.shape[1]

    def kernel(source, *refs):
        results = refs[len(earlier) :]
        for level in range(2):
            start = 9 * level
            for step in range(5):
                results[6 * level + step][...] = source[start + step, :]
            first = start + 5 + 2 * mp_place()
            for step in range(2):
                results[6 * level + 5][pl.ds(step * width, width)] = source[first + step, :]

    inside = pl.BlockSpec(memory_space=pltpu.VMEM)
    shapes = ([(width,)] * 5 + [(2 * width,)]) * 2
    return pl.pallas_call(
        kernel,
        out_shape=[jax.ShapeDtypeStruct(shape, wide_type) for shape in shapes],
        in_specs=[inside] + [pl.BlockSpec(memory_space=pl.ANY)] * len(earlier),
        out_specs=[inside] * 12,
        cost_estimate=pl.CostEstimate(flops=weight[0], bytes_accessed=1, transcendentals=0),
        name="unpack_small",
    )(total, *earlier)


def mix_back_body(last, get, made, done, extra, pads_ref):
    low, flat, work = extra
    normed_grad, summed, vectors = (get(index) for index in range(3))
    length, width = summed.shape
    half = length // 2
    sums = [jnp.zeros((1, width), wide_type)] * 2
    for rows in tiles(length, row_tile):
        grad = normed_grad[rows, :]
        normal, inverse = normalize(summed[rows, :])
        value = norm_backward(grad, normal, inverse, row_of(vectors, 0))
        work[rows, :] = value
        low[rows, :] = value.astype(low_type)
        sums[0] = sums[0] + jnp.sum(grad * normal, axis=0, keepdims=True)
        sums[1] = sums[1] + jnp.sum(grad, axis=0, keepdims=True)
    pair_table = get(3)
    for step in range(2):
        flat[:, step * width : (step + 1) * width] = dot(
            pair_table[:, step * length : (step + 1) * length], low[...]
        ).astype(low_type)
    work[...] += dot(flat[...], get(4)[...])
    small = made[0]
    small[...] = jnp.zeros_like(small)
    if last:
        for rows in tiles(length, row_tile):
            value = work[rows, :] * live_rows(pads_ref, rows, length)
            start = rows.start % half
            target = made[1 + rows.start // half]
            target[start : start + row_tile, :] = value.astype(target.dtype)
    else:
        residual, below = get(5), get(6)
        out_sums = [jnp.zeros((1, width), wide_type)] * 3
        for rows in tiles(length, row_tile):
            grad = work[rows, :] * live_rows(pads_ref, rows, length)
            made[1][rows, :], made[2][rows, :] = out_rows(
                grad, residual[rows, :], row_of(below, 3), out_sums
            )
        sums = sums + out_sums
        done(1, 2)
        own, other = get(7), get(8)
        down_grads((own.at[0], own.at[1], other.at[0], other.at[1]), made[2], made[3], made[4])
    for index, value in enumerate(sums):
        small[index : index + 1, :] = value


def mix_back(normed_grad, summed, vectors, tables, pads, below=None, earlier=()):
    pair_table, _, stack_table = tables
    length, width = rows = summed.shape
    loads = [whole(array) for array in (normed_grad, summed, vectors)]
    loads += [part(pair_table, mp_place), whole(stack_table)]
    outs = [((8, width), wide_type)]
    flops = 4 * length * width * (length + width)
    if below is None:
        half = (length // 2, width)
        outs += [(half, wide_type), (half, low_type)]
    else:
        loads += [whole(array) for array in below]
        size = below[2].shape[2]
        outs += [(rows, wide_type), (rows, low_type)] + [((2, size, width), low_type)] * 2
        flops += 8 * length * width * size
    return staged(
        "mix_back",
        functools.partial(mix_back_body, below is None),
        loads,
        outs,
        earlier,
        [
            pltpu.VMEM(rows, low_type),
            pltpu.VMEM((length, 2 * width), low_type),
            pltpu.VMEM(rows, wide_type),
        ],
        flops,
        20,
    )(pads)


def layer_mix(layer_in, live_mask, params, tables):
    gain_mix, shift_mix = params[:2]
    pair_table, wide_table, stack_table = tables
    width = layer_in.shape[1]
    masked = layer_in * live_mask
    spectra = dot(masked.astype(low_type), wide_table).astype(low_type)
    stacked = jnp.concatenate([spectra[:, :width], spectra[:, width:]], axis=0)
    summed = masked + dot(pair_table, stacked)
    normal, inverse = normalize(summed)
    normed = normal * gain_mix + shift_mix
    return summed, normed, normed.astype(low_type)


def layer_hidden(normed_low, up_weight, up_bias):
    return gate_pair(dot(normed_low, up_weight) + up_bias.astype(wide_type))


def layer_out(normed, branch, live_mask, params):
    down_bias, gain_out, shift_out = params[2:]
    residual = normed + branch + down_bias
    out_normal, out_inverse = normalize(residual)
    result = (out_normal * gain_out + shift_out) * live_mask
    return result, residual


def out_backward(result_cot, live_mask, gain_out, residual):
    out_grad = result_cot * live_mask
    out_normal, out_inverse = normalize(residual)
    resid_grad = norm_backward(out_grad, out_normal, out_inverse, gain_out)
    gainout_grad = jnp.sum(out_grad * out_normal, axis=0)
    shiftout_grad = jnp.sum(out_grad, axis=0)
    branch_cot = resid_grad.astype(low_type)
    downbias_grad = jnp.sum(branch_cot, axis=0, dtype=wide_type)
    return resid_grad, branch_cot, (downbias_grad, gainout_grad, shiftout_grad)


def cot_of(branch_cot, down_weight, slope):
    return (dot_nt(branch_cot, down_weight) * slope.astype(wide_type)).astype(low_type)


def mix_backward(normed_grad, live_mask, gain_mix, summed, tables):
    pair_table, wide_table, stack_table = tables
    length = summed.shape[0]
    normal, inverse = normalize(summed)
    summed_grad = norm_backward(normed_grad, normal, inverse, gain_mix)
    gainmix_grad = jnp.sum(normed_grad * normal, axis=0)
    shiftmix_grad = jnp.sum(normed_grad, axis=0)
    summed_low = summed_grad.astype(low_type)
    flat_grad = jnp.concatenate(
        [
            dot(pair_table[:, :length], summed_low).astype(low_type),
            dot(pair_table[:, length:], summed_low).astype(low_type),
        ],
        axis=1,
    )
    masked_grad = (summed_grad + dot(flat_grad, stack_table)) * live_mask
    return masked_grad, (gainmix_grad, shiftmix_grad)


def paired(first, second):
    return dot_tn(*first) + dot_tn(*second)


def core_swap(array):
    return dp_swap(array, dp_bits()[0])


def cut(ref, axis, index):
    return ref.at[(slice(None),) * axis + (index,)]


def moved(name, body, arrays, shapes, scratch, copies, earlier):
    space = pl.BlockSpec(memory_space=pltpu.HBM)
    count, late, given = len(arrays), len(earlier), len(shapes)

    def kernel(*refs):
        rest = refs[count + late + given :]
        body(refs[:count], refs[count + late : count + late + given], rest[:-1], rest[-1])

    return pl.pallas_call(
        kernel,
        out_shape=[jax.ShapeDtypeStruct(shape, low_type) for shape in shapes],
        in_specs=[space] * count + [pl.BlockSpec(memory_space=pl.ANY)] * late,
        out_specs=[space] * given,
        cost_estimate=pl.CostEstimate(flops=weight[0], bytes_accessed=1, transcendentals=0),
        scratch_shapes=[pltpu.VMEM(shape, low_type) for shape in scratch]
        + [pltpu.SemaphoreType.DMA((copies,))],
        compiler_params=pltpu.CompilerParams(vmem_limit_bytes=vmem_bytes),
        name=name,
    )(*arrays, *earlier)


def sum_parts(arrays, views, targets, shapes, part_shape, earlier):
    count, terms = len(views), len(arrays)

    def body(sources, results, held, sems):
        loads = [
            [
                pltpu.make_async_copy(
                    view(source), held[terms * index + side], sems.at[terms * index + side]
                )
                for side, source in enumerate(sources)
            ]
            for index, view in enumerate(views)
        ]
        for group in loads:
            for copy in group:
                copy.start()
        leaving = []
        for index, group in enumerate(loads):
            for copy in group:
                copy.wait()
            rooms = held[terms * index : terms * (index + 1)]
            value = sum(room[...].astype(wide_type) for room in rooms)
            rooms[0][...] = value.astype(low_type)
            leaving.append(
                pltpu.make_async_copy(
                    rooms[0], targets[index](results), sems.at[terms * count + index]
                )
            )
            leaving[-1].start()
        for copy in leaving:
            copy.wait()

    return moved(
        "sum_parts",
        body,
        arrays,
        shapes,
        [part_shape] * (terms * count),
        (terms + 1) * count,
        earlier,
    )


def sum_split(arrays, axis, place, earlier=()):
    shape, count = arrays[0].shape, arrays[0].shape[axis]
    shape = shape[:axis] + shape[axis + 1 :]
    order = [*range(1, count), 0]
    return sum_parts(
        arrays,
        [lambda ref, step=step: cut(ref, axis, place() ^ step) for step in order],
        [lambda refs, step=step: refs[step] for step in order],
        [shape] * count,
        shape,
        earlier,
    )


def sum_whole(arrays, earlier=()):
    shape = arrays[0].shape
    parts = 2 if shape[0] % 2 == 0 and len(shape) > 2 else 1
    size = shape[0] // parts
    spans = [pl.ds(step * size, size) for step in range(parts)]
    return sum_parts(
        arrays,
        [lambda ref, at=at: ref.at[at] for at in spans],
        [lambda refs, at=at: refs[0].at[at] for at in spans],
        [shape],
        (size, *shape[1:]),
        earlier,
    )[0]


def sum_below(above, arrays, earlier=()):
    rows, width = above.shape

    def body(sources, results, held, sems):
        copies = [
            pltpu.make_async_copy(source, room, sems.at[step])
            for step, (source, room) in enumerate(zip(sources, held))
        ]
        for copy in copies:
            copy.start()
        for copy in copies:
            copy.wait()
        value = sum(room[...].astype(wide_type) for room in held[1:])
        held[1][...] = value.astype(low_type)
        leaving = [
            pltpu.make_async_copy(
                held[step], results[0].at[pl.ds(step * rows, rows)], sems.at[3 + step]
            )
            for step in range(2)
        ]
        for copy in leaving:
            copy.start()
        for copy in leaving:
            copy.wait()

    return moved(
        "sum_below",
        body,
        (above, *arrays),
        [(2 * rows, width)],
        [(rows, width)] * 3,
        5,
        earlier,
    )[0]


def join_parts(arrays, axis, place, earlier=()):
    shape, count = arrays[0].shape, len(arrays)
    whole_shape = shape[:axis] + (count,) + shape[axis:]

    def body(sources, results, held, sems):
        copies = [
            pltpu.make_async_copy(source, room, sems.at[step])
            for step, (source, room) in enumerate(zip(sources, held))
        ]
        for copy in copies:
            copy.start()
        leaving = [
            pltpu.make_async_copy(
                room, cut(results[0], axis, place() ^ step), sems.at[count + step]
            )
            for step, room in enumerate(held)
        ]
        for copy, after in zip(copies, leaving):
            copy.wait()
            after.start()
        for copy in leaving:
            copy.wait()

    return moved(
        "join_parts", body, arrays, [whole_shape], [shape] * count, 2 * count, earlier
    )[0]


def axis_place(axis):
    if axis == "mp":
        return lambda: 0
    if axis == "near":
        return lambda: lax.rem(lax.axis_index("dp") // 2, 2)
    return lambda: lax.axis_index("dp") // 4


def axis_count(axis):
    return lax.axis_size("dp") // 4 if axis == "far" else 2


def axis_swap(array, axis, step):
    if axis == "mp":
        return mp_swap(array)
    return dp_swap(array, (2 if axis == "near" else 4) * step)


class FarTotal:
    def __init__(self, own, received, steps, earlier=()):
        self.axes = ["mp", "far", "near"]
        shape = tuple(axis_count(axis) for axis in self.axes) + (-1, own.shape[-1])
        self.arrays = [own.reshape(shape), received.reshape(shape)]
        self.steps, self.gone = list(steps), []
        self.finish(*earlier)

    def finish(self, *earlier):
        if not self.steps:
            self.total = self.last = sum_whole(self.arrays, earlier)
            return self.last
        name = self.steps.pop(0)
        axis = self.axes.index(name)
        self.axes.pop(axis)
        if name != "mp":
            self.gone.append((name, axis - ("mp" in self.axes)))
        own, *given = sum_split(self.arrays, axis, axis_place(name), earlier)
        self.arrays = [own] + [
            axis_swap(array, name, step + 1) for step, array in enumerate(given)
        ]
        self.last = own
        return own

    def turn(self):
        name, _ = self.gone[-1]
        self.arrays = [self.total] + [
            axis_swap(self.total, name, step) for step in range(1, axis_count(name))
        ]

    def gather(self, *earlier):
        name, axis = self.gone.pop()
        self.total = self.last = join_parts(self.arrays, axis, axis_place(name), earlier)
        if self.gone:
            self.turn()
        else:
            self.total = self.total.reshape(-1, self.total.shape[-1])
        return self.last


def backward_overlapped(leaving, forward_parts, vectors, tables, blocks, pads, final_out):
    resid, cot, small_out, down_keep, down_send = leaving
    (summed_one, low_one, residual_one, hiddens_one, slopes_one), (summed, low, slopes) = (
        forward_parts
    )
    width = low.shape[1]
    shares = lax.axis_size("dp") // 2
    down_near = core_swap(down_send)
    up_send, total, bias_send = cot_rows(
        cot, low, resid, slopes[1::2], blocks[1][1::2], pads
    )
    down_two = sum_whole([down_keep, down_near], (total,))
    scattered = lax.psum_scatter(
        down_two, "dp", scatter_dimension=0, axis_index_groups=core_groups(), tiled=False
    )
    up_near = core_swap(up_send)
    up_keep, normed_grad, bias_keep = cot_rows(
        cot, low, total, slopes[0::2], blocks[1][0::2], pads, (down_two,)
    )
    bias_two = (bias_keep, bias_send)
    up_two = FarTotal(
        up_keep, up_near, ("mp", "near", "far"), (normed_grad,)
    )
    small_mix, resid, cot, down_keep, down_send = mix_back(
        normed_grad,
        summed,
        vectors[1],
        tables,
        pads,
        (residual_one, vectors[0], *hiddens_one),
        (up_two.last,),
    )
    down_near = core_swap(down_send)
    up_send, total, bias_send = cot_rows(
        cot, low_one, resid, slopes_one[1::2], blocks[0][1::2], pads
    )
    up_near = core_swap(up_send)
    last = up_two.finish(total)
    down_one = FarTotal(
        down_keep, down_near, ("mp", "far", "near"), (last,)
    )
    up_keep, normed_grad, bias_keep = cot_rows(
        cot, low_one, total, slopes_one[0::2], blocks[0][0::2], pads, (down_one.last,)
    )
    bias_one = (bias_keep, bias_send)
    up_one = FarTotal(
        up_keep, up_near, ("near", "mp", "far"), (normed_grad,)
    )
    last = up_two.finish(up_one.last)
    last = down_one.finish(last)
    small_last, grad_own, grad_given = mix_back(
        normed_grad, summed_one, vectors[0], tables, pads, None, (last, final_out)
    )
    small = SmallTotal(
        small_matrix(
            ((small_last, small_mix, *bias_one), (small_mix, small_out, *bias_two)), pads
        )
    )
    scattered = scattered.reshape(2, -1, width)
    weight[0] = heavy
    last = up_two.finish(small.total)
    pieces = sum_below(up_two.total, [scattered[0], mp_swap(scattered[1])], (last,))
    both = lax.all_gather(pieces, "dp", axis=0, tiled=False)
    last = up_one.finish(pieces)
    last = small.finish(last)
    last = down_one.finish(last)
    last = small.finish(last)
    last = up_one.finish(last)
    last = small.finish(last)
    last = down_one.finish(last)
    down_one.turn()
    grad_received = mp_swap(gate(grad_given, last))
    last = down_one.gather(last)
    last = small.finish(last)
    last = up_one.finish(last)
    up_one.turn()
    last = small.finish(last)
    last = down_one.gather(last)
    down_near = core_swap(down_one.total)
    input_grad = place_rows(grad_own, grad_received, wide_type, (last,))
    last = up_one.gather(input_grad)
    small = unpack_small(small.total, (last,))
    down_one = widen(down_one.total, down_near, 0, (small[0],))
    up_two, down_two = widen_gathered(both, width, (down_one,))
    last = up_one.gather(up_two)
    up_one = widen(up_one.total, core_swap(up_one.total), 1, ())
    weight[0] = 1
    return input_grad, ((up_one, down_one), (up_two, down_two)), small


def backward_plain(grad, live_mask, params, weights, tables, saved):
    large, small, bias = [None] * 2, [None] * 2, [None] * 2
    for level in (1, 0):
        gain_mix, _, _, gain_out, _ = params[level]
        summed, normed_low, residual, kept = saved[level]
        ((up_weight, down_weight),) = weights[level]
        ((hidden, slope),) = kept
        resid_grad, branch_cot, small_out = out_backward(grad, live_mask, gain_out, residual)
        down_grad = dot_tn(hidden, branch_cot).astype(low_type)
        cot = cot_of(branch_cot, down_weight, slope)
        up_grad = dot_tn(normed_low, cot).astype(low_type)
        bias[level] = [jnp.sum(cot, axis=0, dtype=wide_type)]
        grad, small_mix = mix_backward(
            resid_grad + dot_nt(cot, up_weight), live_mask, gain_mix, summed, tables
        )
        small[level] = small_mix + small_out
        large[level] = (total_plain(up_grad, 1), total_plain(down_grad, 0))
    return grad, large, small, bias


def on_device(*arguments):
    inputs, pad_counts = arguments[:2]
    layer_args = (arguments[2:10], arguments[10:18])
    cotangent = arguments[18]
    mp_count = lax.axis_size("mp")
    mine = lax.axis_index("mp")
    feature_width = inputs.shape[2]
    row_length = inputs.shape[1] * mp_count
    cos_seq, sin_seq = fourier_table(row_length)
    pair_full = np.concatenate([cos_seq, -sin_seq], axis=1)
    turned = 1 - 2 * ((np.arange(row_length)[:, None] + np.arange(2 * row_length)[None, :]) % 2)
    if mp_count == 2:
        pair_table = jnp.asarray(np.stack([pair_full, pair_full * turned]), low_type)
    else:
        pair_table = jnp.asarray(pair_full, low_type)
    wide_table = jnp.asarray(np.concatenate(fourier_table(feature_width), axis=1), low_type)
    stack_table = jnp.asarray(np.concatenate(fourier_table(feature_width), axis=0), low_type)
    tables = (pair_table, wide_table, stack_table)
    (up_one, down_one), (up_two, down_two) = [(args[2], args[4]) for args in layer_args]
    biases = jnp.stack([args[3] for args in layer_args])
    if mp_count == 2:
        core, near, far = dp_bits()[:3]
        core_bit = bit_of(core)
        own_rows, given = cut_first(inputs, up_one)
        own_rows = mp_swap(own_rows)
        received = mp_swap(given)
        far_rows = lax.all_gather(own_rows, "dp", axis=0, tiled=False)
        block, up_part, down_part, given_cot = cut_next(
            cotangent, down_one, up_two, down_two, (given,)
        )
        down_first = mp_swap(block)
        other_biases = mp_swap(biases)
        vectors = []
        for level in range(2):
            args = layer_args[level]
            members = [args[0], args[1], args[5], args[6], args[7]]
            members += [
                take_block(array[level], (core_bit + flip) % 2)
                for array in (biases, other_biases)
                for flip in range(2)
            ]
            vectors.append(select_rows(members, 16))
        own_blocks = [
            [own_block(up, down, flip) for flip in range(2)]
            for up, down in ((up_one, down_one), (up_two, down_two))
        ]
        summed_one, normed, low_one, partial, hidden_a, slope_a = enter(
            inputs, received, tables, vectors[0], own_blocks[0], pad_counts
        )
        down_first = gate(down_first, low_one)
        up_part = mp_swap(gate(up_part, down_first))
        down_part = mp_swap(gate(down_part, down_first))
        down_second = core_swap(down_first)
        far_blocks = [
            (far_columns(far_rows, flip), whole(array))
            for flip, array in enumerate((down_first, down_second))
        ]
        hidden_b, slope_b, residual_one, result = rest(
            low_one, normed, partial, vectors[0], far_blocks, pad_counts
        )
        up_part = fetch_join(gate(up_part, result), far)
        down_part = fetch_join(gate(down_part, result), near)
        summed, normed, low = again(result, tables, vectors[1], pad_counts)
        received_cot = mp_swap(gate(given_cot, down_part))
        up_part = fetch_join(gate(up_part, low), near)
        down_part = fetch_join(gate(down_part, low), far)
        partial, hidden_c, slope_c = some(5, low, vectors[1], own_blocks[1], pad_counts)
        up_part, down_part = gate(up_part, partial), gate(down_part, partial)
        up_near = core_swap(up_part)
        down_near = core_swap(down_part)
        partial, hidden_d, slope_d = some(
            7,
            low,
            vectors[1],
            [(whole(up_part), whole(down_part))],
            pad_counts,
            (partial,),
        )
        out_own, out_given, resid, cot, small_out, slope_e, down_keep, down_send = leave(
            low,
            normed,
            partial,
            vectors[1],
            (whole(up_near), whole(down_near)),
            cotangent,
            received_cot,
            (hidden_c, hidden_d),
            pad_counts,
        )
        blocks = [
            own_blocks[0] + far_blocks,
            own_blocks[1]
            + [(whole(up_part), whole(down_part)), (whole(up_near), whole(down_near))],
        ]
        slopes_one = [part(array, lambda at=at: at) for array in (slope_a, slope_b) for at in (0, 1)]
        slopes_two = [part(slope_c, lambda at=at: at) for at in (0, 1)]
        slopes_two += [part(slope_d, lambda: 0), whole(slope_e)]
        out_received = mp_swap(out_given)
        final_out = place_rows(out_own, out_received, low_type)
        input_grad, large, small = backward_overlapped(
            (resid, cot, small_out, down_keep, down_send),
            (
                (summed_one, low_one, residual_one, (hidden_a, hidden_b), slopes_one),
                (summed, low, slopes_two),
            ),
            vectors,
            tables,
            blocks,
            pad_counts,
            final_out,
        )
    else:
        params = [
            tuple(args[step].astype(wide_type) for step in (0, 1, 5, 6, 7)) for args in layer_args
        ]
        position = jnp.arange(row_length, dtype=jnp.int32)
        pads = lax.dynamic_index_in_dim(pad_counts, mine, 0, False)
        live_mask = (position < row_length - pads).astype(wide_type)[:, None]
        weights, saved = [], []
        biases = lax.all_gather(biases, "mp", axis=1, tiled=True)
        current = gathered_row(inputs).astype(wide_type)
        for level, (up_weight, down_weight) in enumerate(((up_one, down_one), (up_two, down_two))):
            up_weight = lax.all_gather(up_weight, "mp", axis=1, tiled=True)
            down_weight = lax.all_gather(down_weight, "mp", axis=0, tiled=True)
            weights.append(((up_weight, down_weight),))
            summed, normed, normed_low = layer_mix(current, live_mask, params[level], tables)
            kept = layer_hidden(normed_low, up_weight, biases[level])
            current, residual = layer_out(
                normed, dot(kept[0], down_weight), live_mask, params[level]
            )
            saved.append((summed, normed_low, residual, (kept,)))
        grad = gathered_row(cotangent).astype(wide_type)
        final_out = return_rows(current.astype(low_type))
        grad, large, small, bias = backward_plain(grad, live_mask, params, weights, tables, saved)
        input_grad = return_rows(grad.astype(low_type)).astype(wide_type)
    hidden_own = layer_args[0][3].shape[0]
    if mp_count != 2:
        rows = []
        for level in range(2):
            rows.extend(small[level])
            rows.extend(bias[level][0].reshape(-1, feature_width))
        total = total_small(select_rows(rows, 8 * -(-len(rows) // 8)))
        count, small = len(rows) // 2, []
        for level in range(2):
            block = total[level * count : (level + 1) * count]
            small += [block[step] for step in range(5)]
            small.append(
                lax.dynamic_slice_in_dim(block[5:].reshape(-1), mine * hidden_own, hidden_own, 0)
            )
    results = [final_out, input_grad]
    for level in range(2):
        gainmix, shiftmix, downbias, gainout, shiftout, bias_total = small[6 * level : 6 * level + 6]
        up_total, down_total = large[level]
        results += [gainmix, shiftmix, up_total, bias_total, down_total, downbias, gainout, shiftout]
    return tuple(results)


def solution(mesh):
    layer_specs = (P(), P(), P(None, "mp"), P("mp"), P("mp", None), P(), P(), P())
    rows = P("dp", "mp", None)
    return jax.shard_map(
        on_device,
        mesh=mesh,
        in_specs=(rows, P("dp"), *layer_specs, *layer_specs, rows),
        out_specs=(rows, rows, *layer_specs, *layer_specs),
        check_vma=False,
    )
```

```python
import functools
import math

import jax
import jax.numpy as jnp
import numpy as np
from jax import lax
from jax.experimental import pallas as pl
from jax.experimental.pallas import tpu as pltpu
from jax.sharding import PartitionSpec as P

norm_eps = 1e-05
low_type = jnp.bfloat16
wide_type = jnp.float32
vmem_bytes = 62 * 2**20
window = 4
heavy = 6 * 10**9
weight = [1]


def fourier_table(points):
    indices = np.arange(points, dtype=np.int64)
    phases = (indices[:, None] * indices[None, :]) % points
    angles = phases.astype(np.float32) * np.float32(2.0 * math.pi / points)
    factor = np.float32(points ** (-0.5))
    return (np.cos(angles) * factor, np.sin(angles) * factor)


def dot(left, right):
    return jnp.dot(left, right, preferred_element_type=wide_type)


def dot_tn(left, right):
    return lax.dot_general(left, right, (((0,), (0,)), ((), ())), preferred_element_type=wide_type)


def dot_nt(left, right):
    return lax.dot_general(left, right, (((1,), (1,)), ((), ())), preferred_element_type=wide_type)


def normalize(activity):
    center = jnp.mean(activity, axis=-1, keepdims=True)
    centered = activity - center
    spread = jnp.mean(centered * centered, axis=-1, keepdims=True)
    inverse = lax.rsqrt(spread + norm_eps)
    return centered * inverse, inverse


def norm_backward(grad, normal, inverse, gain):
    pulled = grad * gain
    first = jnp.mean(pulled, axis=-1, keepdims=True)
    second = jnp.mean(pulled * normal, axis=-1, keepdims=True)
    return inverse * (pulled - first - normal * second)


def gate_pair(preact):
    scale = math.sqrt(2.0 / math.pi)
    square = preact * preact
    turn = jnp.tanh(preact * (scale + (0.044715 * scale) * square))
    half = 0.5 + 0.5 * turn
    hidden = preact * half
    slope = half + hidden * (1.0 - turn) * (scale + (3 * 0.044715 * scale) * square)
    return hidden.astype(low_type), slope.astype(low_type)


def flip_pairs(size, bit):
    return [(index, index ^ bit) for index in range(size)]


def order_halves(bit_value, mine, theirs, axis=0):
    return jnp.where(
        bit_value == 0,
        jnp.concatenate([mine, theirs], axis=axis),
        jnp.concatenate([theirs, mine], axis=axis),
    )


def take_block(array, which, count=2, axis=0):
    size = array.shape[axis] // count
    return lax.dynamic_slice_in_dim(array, which * size, size, axis)


def dp_bits():
    return [1 << level for level in range(lax.axis_size("dp").bit_length() - 1)]


def bit_of(bit):
    return (lax.axis_index("dp") // bit) % 2


def dp_swap(array, bit):
    return lax.ppermute(array, "dp", flip_pairs(lax.axis_size("dp"), bit))


def mp_swap(array):
    return lax.ppermute(array, "mp", [(0, 1), (1, 0)])


def add_low(left, right):
    return (left.astype(wide_type) + right.astype(wide_type)).astype(low_type)


def gate(value, *earlier):
    def kernel(*refs):
        pass

    anywhere = pl.BlockSpec(memory_space=pl.ANY)
    return pl.pallas_call(
        kernel,
        out_shape=jax.ShapeDtypeStruct(value.shape, value.dtype),
        in_specs=[anywhere] * (1 + len(earlier)),
        out_specs=anywhere,
        input_output_aliases={0: 0},
        name="gate",
    )(value, *earlier)


def fetch_join(piece, bit):
    return order_halves(bit_of(bit), piece, dp_swap(piece, bit))


def bounce(name, jobs, shapes, arrays, earlier=()):
    count, late, given = len(arrays), len(earlier), len(shapes)

    def kernel(*refs):
        targets = refs[count + late : count + late + given]
        held, sems = refs[count + late + given : -1], refs[-1]
        work = jobs(refs[:count], held)
        copies = [
            pltpu.make_async_copy(source, target, sems.at[given + index])
            for index, (_, source, target) in enumerate(work)
        ]
        for copy in copies:
            copy.start()
        leaving = [
            pltpu.make_async_copy(source, target, sems.at[index])
            for index, (source, target) in enumerate(zip(held, targets))
        ]
        for slot in range(given):
            for (place, _, _), copy in zip(work, copies):
                if place == slot:
                    copy.wait()
            leaving[slot].start()
        for copy in leaving:
            copy.wait()

    space = pl.BlockSpec(memory_space=pltpu.HBM)
    return pl.pallas_call(
        kernel,
        out_shape=[jax.ShapeDtypeStruct(shape, low_type) for shape in shapes],
        in_specs=[space] * count + [pl.BlockSpec(memory_space=pl.ANY)] * late,
        out_specs=[space] * given,
        scratch_shapes=[pltpu.VMEM(shape, low_type) for shape in shapes]
        + [pltpu.SemaphoreType.DMA((4 * given,))],
        compiler_params=pltpu.CompilerParams(vmem_limit_bytes=vmem_bytes),
        name=name,
    )(*arrays, *earlier)


def span(index, count):
    return pl.ds(pl.multiple_of(index * count, count), count)


def cut_first(up_one, up_two, down_two):
    width, size = up_one.shape[0], up_one.shape[1] // 2
    rows = width // lax.axis_size("dp")
    quarter = (width // 4, size // 4)

    def jobs(sources, held):
        place, core = lax.axis_index("dp"), core_place()
        near, away = lax.rem(place // 2, 2), lax.rem(place // 4, 2)
        own = sources[0].at[span(place, rows)]
        return [
            (0, own.at[:, pl.ds(0, size)], held[0].at[pl.ds(0, rows)]),
            (0, own.at[:, pl.ds(size, size)], held[0].at[pl.ds(rows, rows)]),
            (1, sources[1].at[span(2 * near + away, quarter[0]), span(core, size)], held[1]),
            (2, sources[2].at[span(core * 4 + 2 * away + near, quarter[1])], held[2]),
        ]

    shapes = ((2 * rows, size), (quarter[0], size), (quarter[1], width))
    return bounce("cut_first", jobs, shapes, (up_one, up_two, down_two))


def cut_next(inputs, cotangent, down_one, earlier):
    length, width = cotangent.shape[1:]
    size = down_one.shape[0] // 2

    def jobs(sources, held):
        rows, cots, down = sources
        return [
            (0, rows.at[1 - mp_place()], held[0]),
            (1, down.at[span(core_place(), size)], held[1]),
            (2, cots.at[1 - mp_place()], held[2]),
        ]

    shapes = ((length, width), (size, width), (length, width))
    return bounce("cut_next", jobs, shapes, (inputs, cotangent, down_one), earlier)


def select_rows(rows, count):
    index = lax.broadcasted_iota(jnp.int32, (count, rows[0].shape[0]), 0)
    total = jnp.zeros(index.shape, wide_type)
    for place, row in enumerate(rows):
        total = jnp.where(index == place, row.astype(wide_type)[None], total)
    return total


def core_groups():
    return [
        [place for place in range(lax.axis_size("dp")) if place % 2 == which] for which in (0, 1)
    ]


def total_plain(part, hidden_axis):
    own = lax.psum_scatter(part, "mp", scatter_dimension=hidden_axis, tiled=True)
    return lax.psum(own, "dp").astype(wide_type)


def total_small(vector):
    for bit in dp_bits():
        vector = vector + dp_swap(vector, bit)
    if lax.axis_size("mp") == 2:
        return vector + mp_swap(vector)
    return lax.psum(vector, "mp")


def given_row(array):
    return lax.dynamic_index_in_dim(array, 1 - lax.axis_index("mp"), 0, keepdims=False)


def gathered_row(array):
    return lax.all_to_all(array, "mp", split_axis=0, concat_axis=1, tiled=True)[0]


def return_rows(array):
    return lax.all_to_all(array[None], "mp", split_axis=1, concat_axis=0, tiled=True)


def staged(name, body, loads, outs, earlier=(), scratch=(), flops=0, stress=0):
    count, late, given = len(loads), len(earlier), len(outs)

    def kernel(*refs):
        sources = refs[1 : 1 + count]
        targets = refs[1 + count + late : 1 + count + late + given]
        rest = refs[1 + count + late + given :]
        held, made = rest[:count], rest[count : count + given]
        in_sems, out_sems, *extra = rest[count + given :]
        copies, begun, sent = {}, set(), []
        for index, load in enumerate(loads):
            view = load[2](sources[index])
            copies[index] = pltpu.make_async_copy(view, held[index], in_sems.at[index])
        queue = sorted(range(count), key=lambda index: math.prod(loads[index][1]) > 2**16)

        def begin(index):
            if index not in begun:
                copies[index].start()
                begun.add(index)

        def get(index):
            begin(index)
            if index in copies:
                copies.pop(index).wait()
                while sum(place in copies for place in begun) < window and len(begun) < count:
                    begin(next(place for place in queue if place not in begun))
            return held[index]

        for index in queue:
            if math.prod(loads[index][1]) <= 2**16 or len(begun) < window:
                begin(index)

        def done(*indices):
            for index in indices:
                slot = len(sent)
                if isinstance(index, tuple):
                    index, place = index
                    source, target = made[index].at[place], targets[index].at[place]
                else:
                    source, target = made[index], targets[index]
                copy = pltpu.make_async_copy(source, target, out_sems.at[slot])
                copy.start()
                sent.append((index, copy))

        body(get, made, done, extra, refs[0])
        for index in list(copies):
            get(index)
        left = {index for index, _ in sent}
        done(*[index for index in range(given) if index not in left])
        for _, copy in sent:
            copy.wait()

    space = pl.BlockSpec(memory_space=pltpu.HBM)
    moved = sum(math.prod(load[1]) * load[0].dtype.itemsize for load in loads)
    moved += sum(math.prod(out[0]) * jnp.dtype(out[1]).itemsize for out in outs)
    call = pl.pallas_call(
        kernel,
        out_shape=[jax.ShapeDtypeStruct(*out) for out in outs],
        in_specs=[pl.BlockSpec(memory_space=pltpu.SMEM)]
        + [space] * count
        + [pl.BlockSpec(memory_space=pl.ANY)] * late,
        out_specs=[space] * given,
        cost_estimate=pl.CostEstimate(
            flops=1 + stress * flops, bytes_accessed=1 + stress * moved, transcendentals=0
        ),
        scratch_shapes=[pltpu.VMEM(load[1], load[0].dtype) for load in loads]
        + [pltpu.VMEM(*out) for out in outs]
        + [pltpu.SemaphoreType.DMA((count,)), pltpu.SemaphoreType.DMA((2 * given,))]
        + list(scratch),
        compiler_params=pltpu.CompilerParams(vmem_limit_bytes=vmem_bytes),
        name=name,
    )
    return lambda pads: call(pads, *[load[0] for load in loads], *earlier)


def whole(array):
    return (array, array.shape, lambda ref: ref)


def part(array, index):
    return (array, array.shape[1:], lambda ref: ref.at[index()])


def mp_place():
    return lax.axis_index("mp")


def core_place():
    return lax.rem(lax.axis_index("dp"), 2)


def share(flip):
    return (core_place() + flip) % 2


def own_block(up_weight, down_weight, flip):
    width, size = up_weight.shape[0], up_weight.shape[1] // 2

    def span():
        return pl.ds(pl.multiple_of(share(flip) * size, size), size)

    return (
        (up_weight, (width, size), lambda ref: ref.at[:, span()]),
        (down_weight, (size, width), lambda ref: ref.at[span()]),
    )


def far_columns(pieces, flip):
    places, rows, size = pieces.shape
    half = rows // 2
    return (
        pieces,
        (places, half, size),
        lambda ref: ref.at[:, pl.ds(pl.multiple_of(share(flip) * half, half), half)],
    )


def matrix(ref):
    return ref[...].reshape(-1, ref.shape[-1])


def tiles(total, size):
    return [slice(start, start + size) for start in range(0, total, size)]


def live_rows(pads_ref, rows, length):
    place = lax.broadcasted_iota(jnp.int32, (rows.stop - rows.start, 1), 0) + rows.start
    place = lax.rem(place + mp_place() * (length // 2), length)
    return (place < length - pads_ref[mp_place()]).astype(wide_type)


def row_of(ref, index):
    return ref[index : index + 1, :]


row_tile = 128


def mix_rows(summed, normed, low, spectra, wide_table, pair_table, vectors):
    length, width = summed.shape
    low[...] = summed[...].astype(low_type)
    wide = wide_table()
    for columns in tiles(2 * width, width):
        spectra[:, columns] = dot(low[...], wide[:, columns]).astype(low_type)
    pair = pair_table()
    summed[...] += dot(pair[:, :length], spectra[:, :width])
    summed[...] += dot(pair[:, length:], spectra[:, width:])
    for rows in tiles(length, row_tile):
        normal, _ = normalize(summed[rows, :])
        value = normal * row_of(vectors, 0) + row_of(vectors, 1)
        normed[rows, :] = value
        low[rows, :] = value.astype(low_type)


def feed_block(low, up_weight, bias, down_weight, hidden, slope):
    hidden[...], slope[...] = gate_pair(dot(low[...], matrix(up_weight())) + bias)
    return dot(hidden[...], matrix(down_weight()))


def out_norm(residual, normed, parts, vectors):
    for rows in tiles(residual.shape[0], row_tile):
        value = normed[rows, :]
        for item in parts:
            value = value + item[rows, :]
        value = value + row_of(vectors, 2)
        residual[rows, :] = value
        normal, _ = normalize(value)
        yield rows, normal * row_of(vectors, 3) + row_of(vectors, 4)


def enter_body(get, made, done, extra, pads_ref):
    summed, normed, low, partial, hidden, slope = made
    (spectra,) = extra
    length, width = summed.shape
    half = length // 2
    for rows in tiles(length, row_tile):
        start = rows.start % half
        piece = get(rows.start // half)[start : start + row_tile, :].astype(wide_type)
        summed[rows, :] = piece * live_rows(pads_ref, rows, length)
    vectors = get(4)
    mix_rows(summed, normed, low, spectra, lambda: get(2), lambda: get(3), vectors)
    done(0, 1, 2)
    for block in range(2):
        value = feed_block(
            low,
            lambda: get(5 + 2 * block),
            row_of(vectors, 5 + block),
            lambda: get(6 + 2 * block),
            hidden.at[block],
            slope.at[block],
        )
        done((4, block), (5, block))
        partial[...] = value if block == 0 else partial[...] + value


def enter(inputs, received, tables, vectors, blocks, pads):
    pair_table, wide_table, _ = tables
    length, width = 2 * received.shape[0], received.shape[1]
    size = blocks[0][0][1][1]
    loads = [part(inputs, mp_place), whole(received), whole(wide_table)]
    loads += [part(pair_table, mp_place), whole(vectors), *blocks[0], *blocks[1]]
    rows = (length, width)
    return staged(
        "enter",
        enter_body,
        loads,
        [(rows, wide_type), (rows, wide_type), (rows, low_type), (rows, wide_type)]
        + [((2, length, size), low_type)] * 2,
        (),
        [pltpu.VMEM((length, 2 * width), low_type)],
        4 * length * width * (length + width + 2 * size),
    )(pads)


def middle_body(get, made, done, extra, pads_ref):
    hidden, slope, residual, summed, normed, low, partial, hidden_two, slope_two = made
    spectra, total = extra
    length = summed.shape[0]
    low_one, vectors = get(0), get(5)
    for block in range(2):
        value = feed_block(
            low_one,
            lambda: get(1 + 2 * block),
            row_of(vectors, 7 + block),
            lambda: get(2 + 2 * block),
            hidden.at[block],
            slope.at[block],
        )
        done((0, block), (1, block))
        total[...] = value if block == 0 else total[...] + value
    for rows, value in out_norm(residual, get(6), (total, get(7)), vectors):
        summed[rows, :] = value * live_rows(pads_ref, rows, length)
    done(2)
    vectors = get(10)
    mix_rows(summed, normed, low, spectra, lambda: get(8), lambda: get(9), vectors)
    done(3, 4, 5)
    for block in range(2):
        value = feed_block(
            low,
            lambda: get(11 + 2 * block),
            row_of(vectors, 5 + block),
            lambda: get(12 + 2 * block),
            hidden_two.at[block],
            slope_two.at[block],
        )
        done((7, block), (8, block))
        partial[...] = value if block == 0 else partial[...] + value


def middle(low, normed, partial, tables, vectors, far_blocks, own_blocks, pads, earlier=()):
    pair_table, wide_table, _ = tables
    length, width = rows = low.shape
    size = own_blocks[0][0][1][1]
    loads = [whole(low), *far_blocks[0], *far_blocks[1], whole(vectors[0])]
    loads += [whole(normed), whole(partial), whole(wide_table), part(pair_table, mp_place)]
    loads += [whole(vectors[1]), *own_blocks[0], *own_blocks[1]]
    hidden = ((2, length, size), low_type)
    return staged(
        "middle",
        middle_body,
        loads,
        [hidden, hidden, (rows, wide_type), (rows, wide_type), (rows, wide_type)]
        + [(rows, low_type), (rows, wide_type), hidden, hidden],
        earlier,
        [pltpu.VMEM((length, 2 * width), low_type), pltpu.VMEM(rows, wide_type)],
        4 * length * width * (length + width + 4 * size),
    )(pads)


def down_grads(hiddens, cot, made, done, keep, send):
    for step, index in ((1, send), (0, keep)):
        target = made[index]
        for half in range(2):
            value = dot_tn(hiddens[2 * half + step][...], cot[...]).astype(low_type)
            if len(target.shape) == 4:
                target[:, half] = value.reshape(target.shape[0], *target.shape[2:])
                place = (slice(None), half)
            else:
                target[half] = value
                place = half
            done((index, place))


def leave_body(get, made, done, extra, pads_ref):
    out_own, out_given, resid, cot, small, slope, keep, send = made
    hidden, total, residual = extra
    length, width = resid.shape
    half = length // 2
    low, vectors = get(0), get(5)
    for block in range(2):
        value = feed_block(
            low,
            lambda: get(1 + 2 * block),
            row_of(vectors, 7 + block),
            lambda: get(2 + 2 * block),
            hidden.at[block],
            slope.at[block],
        )
        done((5, block))
        total[...] = value if block == 0 else total[...] + value
    sums = [jnp.zeros((1, width), wide_type)] * 3
    for rows, value in out_norm(residual, get(6), (total, get(7)), vectors):
        live = live_rows(pads_ref, rows, length)
        start = rows.start % half
        target = (out_own, out_given)[rows.start // half]
        target[start : start + row_tile, :] = (value * live).astype(low_type)
        grad = get(8 + rows.start // half)[start : start + row_tile, :].astype(wide_type) * live
        resid[rows, :], cot[rows, :] = out_rows(grad, residual[rows, :], row_of(vectors, 3), sums)
    small[...] = jnp.zeros_like(small)
    for index, value in enumerate(sums):
        small[index : index + 1, :] = value
    done(0, 1, 2, 3, 4)
    own = get(10)
    down_grads((own.at[0], own.at[1], hidden.at[0], hidden.at[1]), cot, made, done, 6, 7)


def leave(low, normed, partial, vectors, blocks, cotangent, received, hidden, pads, earlier=()):
    length, width = rows = low.shape
    size = hidden.shape[2]
    shares = lax.axis_size("dp") // 2
    loads = [whole(low), *blocks[0], *blocks[1], whole(vectors), whole(normed), whole(partial)]
    loads += [part(cotangent, mp_place), whole(received), whole(hidden)]
    half, grads = (length // 2, width), ((shares, 2, size // shares, width), low_type)
    return staged(
        "leave",
        leave_body,
        loads,
        [(half, low_type), (half, low_type), (rows, wide_type), (rows, low_type)]
        + [((8, width), wide_type), ((2, length, size), low_type), grads, grads],
        earlier,
        [pltpu.VMEM((2, length, size), low_type)] + [pltpu.VMEM(rows, wide_type)] * 2,
        16 * length * width * size,
    )(pads)


def out_rows(grad, residual, gain, sums):
    normal, inverse = normalize(residual)
    resid_grad = norm_backward(grad, normal, inverse, gain)
    low = resid_grad.astype(low_type)
    parts = (grad * normal, grad, low.astype(wide_type))
    for index, value in enumerate(parts):
        sums[index] = sums[index] + jnp.sum(value, axis=0, keepdims=True)
    return resid_grad, low


def cot_body(get, made, done, extra, pads_ref):
    grads, total, small = made
    (cots,) = extra
    branch_cot = get(0)
    small[...] = jnp.zeros_like(small)
    places = ((1, 2, 5), (6, 7, 8))
    for half in range(2):
        down_weight, slope, up_weight = places[half]
        value = dot_nt(branch_cot[...], matrix(get(down_weight)))
        value = (value * get(slope)[...].astype(wide_type)).astype(low_type)
        cots[...] = value
        small[half : half + 1, :] = jnp.sum(value.astype(wide_type), axis=0, keepdims=True)
        value = dot_tn(get(3)[...], cots[...]).astype(low_type)
        if len(grads.shape) == 4:
            grads[:, half] = value.reshape(grads.shape[0], *grads.shape[2:])
            done((0, (slice(None), half)))
        else:
            grads[half] = value
            done((0, half))
        before, up_weight = (get(4) if half == 0 else total), get(up_weight)
        count = 1 + half
        for rows in tiles(total.shape[0], total.shape[0] // count):
            total[rows, :] = before[rows, :] + dot_nt(cots[rows, :], matrix(up_weight))
            if half:
                done((1, pl.ds(rows.start, rows.stop - rows.start)))


def cot_rows(branch_cot, low, before, slopes, blocks, pads, earlier=(), shares=0):
    length, width = rows = low.shape
    (up_a, down_a), (up_b, down_b) = blocks
    loads = [whole(branch_cot), down_a, slopes[0], whole(low), whole(before), up_a]
    loads += [down_b, slopes[1], up_b]
    size = slopes[0][1][1]
    return staged(
        "cot_rows",
        cot_body,
        loads,
        [
            ((shares, 2, width // shares, size) if shares else (2, width, size), low_type),
            (rows, wide_type),
            ((8, size), wide_type),
        ],
        earlier,
        [pltpu.VMEM((length, size), low_type)],
        12 * length * width * size,
        20,
    )(pads)


def small_body(get, made, done, extra, pads_ref):
    total = made[0]
    width = total.shape[1]
    index = lax.broadcasted_iota(jnp.int32, (4, 1), 0)
    for level in range(2):
        mix, out, *biases = (get(4 * level + step) for step in range(4))
        start = 9 * level
        total[start : start + 2, :] = mix[0:2, :]
        first = 0 if level else 2
        total[start + 2 : start + 3, :] = out[first + 2 : first + 3, :]
        total[start + 3 : start + 5, :] = out[first : first + 2, :]
        rows = jnp.zeros((4, width), wide_type)
        for block in range(4):
            half = (mp_place() + block // 2) % 2
            rows = rows + jnp.where(
                index == 2 * half + share(block % 2),
                biases[block % 2][block // 2 : block // 2 + 1, :],
                0.0,
            )
        total[start + 5 : start + 9, :] = rows
    total[18:, :] = jnp.zeros((total.shape[0] - 18, width), wide_type)


def small_matrix(parts, pads, earlier=()):
    loads = [whole(array) for level in parts for array in level]
    width = parts[0][0].shape[1]
    outs = [((32, width), wide_type)]
    return staged("small_matrix", small_body, loads, outs, earlier)(pads)[0]


def pack_pieces(groups, smalls, earlier):
    arrays = [array for group in groups for array in group]
    rows, width = arrays[0].shape
    small_rows = smalls[0].shape[0] if smalls else 0
    count, late = len(arrays), len(earlier)
    size = rows * len(groups) + 2 * small_rows

    def kernel(*refs):
        sources, small_refs = refs[:count], refs[count : count + len(smalls)]
        target, packed, *held = refs[count + len(smalls) + late : -1]
        sems = refs[-1]
        copies = [
            pltpu.make_async_copy(source, room, sems.at[index])
            for index, (source, room) in enumerate(zip((*sources, *small_refs), held))
        ]
        for copy in copies:
            copy.start()
        leaving, first = [], 0
        for place, group in enumerate(groups):
            span = slice(place * rows, (place + 1) * rows)
            value = 0.0
            for index in range(first, first + len(group)):
                copies[index].wait()
                value = value + held[index][...].astype(wide_type)
            packed[span, :] = value.astype(low_type)
            first += len(group)
        if smalls:
            for copy in copies[count:]:
                copy.wait()
            total = held[count][...] + held[count + 1][...]
            high = total.astype(low_type)
            start = rows * len(groups)
            packed[start : start + small_rows, :] = high
            packed[start + small_rows :, :] = (total - high.astype(wide_type)).astype(low_type)
        copy = pltpu.make_async_copy(packed, target, sems.at[count + 2])
        copy.start()
        copy.wait()

    space = pl.BlockSpec(memory_space=pltpu.HBM)
    return pl.pallas_call(
        kernel,
        out_shape=jax.ShapeDtypeStruct((size, width), low_type),
        in_specs=[space] * (count + len(smalls)) + [pl.BlockSpec(memory_space=pl.ANY)] * late,
        out_specs=space,
        scratch_shapes=[pltpu.VMEM((size, width), low_type)]
        + [pltpu.VMEM((rows, width), low_type)] * count
        + [pltpu.VMEM((small_rows, width), wide_type) for _ in smalls]
        + [pltpu.SemaphoreType.DMA((count + 3,))],
        compiler_params=pltpu.CompilerParams(vmem_limit_bytes=vmem_bytes),
        cost_estimate=pl.CostEstimate(flops=weight[0], bytes_accessed=1, transcendentals=0),
        name="pack_pieces",
    )(*arrays, *smalls, *earlier)


def unpack_pair(mine, theirs):
    shares, both_rows, width = mine.shape
    rows = both_rows // 2
    size = shares * rows

    def kernel(own, near, down, up, low, held, sems):
        jobs = [(kind, side) for side in range(2) for kind in range(2)]
        copies = [
            pltpu.make_async_copy(
                (own, near)[side].at[:, pl.ds(kind * rows, rows)], low.at[slot], sems.at[slot]
            )
            for slot, (kind, side) in enumerate(jobs)
        ]
        for copy in copies:
            copy.start()
        leaving = []
        for slot, (kind, side) in enumerate(jobs):
            copies[slot].wait()
            held[slot] = low[slot].reshape(size, width).astype(wide_type)
            place = share(side)
            if kind:
                where = up.at[:, pl.ds(pl.multiple_of(place * width, width), width)]
            else:
                where = down.at[pl.ds(pl.multiple_of(place * size, size), size)]
            leaving.append(pltpu.make_async_copy(held.at[slot], where, sems.at[4 + slot]))
            leaving[-1].start()
        for copy in leaving:
            copy.wait()

    space = pl.BlockSpec(memory_space=pltpu.HBM)
    return pl.pallas_call(
        kernel,
        out_shape=[
            jax.ShapeDtypeStruct((2 * size, width), wide_type),
            jax.ShapeDtypeStruct((size, 2 * width), wide_type),
        ],
        in_specs=[space] * 2,
        out_specs=[space] * 2,
        scratch_shapes=[
            pltpu.VMEM((4, shares, rows, width), low_type),
            pltpu.VMEM((4, size, width), wide_type),
            pltpu.SemaphoreType.DMA((8,)),
        ],
        compiler_params=pltpu.CompilerParams(vmem_limit_bytes=vmem_bytes),
        cost_estimate=pl.CostEstimate(flops=weight[0], bytes_accessed=1, transcendentals=0),
        name="unpack_pair",
    )(mine, theirs)


def unpack_pieces(gathered, small_rows, earlier):
    shares, width = gathered.shape[0] // 2, gathered.shape[2]
    rows = (gathered.shape[1] - 2 * small_rows) // 2
    size = shares * rows
    pieces = gathered.reshape(shares, 2, -1, width)
    rising = (False, True)

    def kernel(source, *refs):
        refs = refs[len(earlier) :]
        targets, results = refs[:2], refs[2:14]
        low, held, small, sems = refs[14:]
        jobs = [(kind, core) for kind in range(2) for core in range(2)]
        copies = [
            pltpu.make_async_copy(
                source.at[:, core, pl.ds(kind * rows, rows)], low.at[slot], sems.at[slot]
            )
            for slot, (kind, core) in enumerate(jobs)
        ]
        copies.append(
            pltpu.make_async_copy(
                source.at[:, :, pl.ds(2 * rows, 2 * small_rows)], small, sems.at[8]
            )
        )
        for copy in copies:
            copy.start()
        leaving = []
        for slot, (kind, core) in enumerate(jobs):
            copies[slot].wait()
            held[slot] = low[slot].reshape(size, width).astype(wide_type)
            if rising[kind]:
                where = targets[kind].at[:, pl.ds(core * width, width)]
            else:
                where = targets[kind].at[pl.ds(core * size, size)]
            leaving.append(pltpu.make_async_copy(held.at[slot], where, sems.at[4 + slot]))
            leaving[-1].start()
        copies[-1].wait()
        total = jnp.zeros((2 * small_rows, width), wide_type)
        for place in range(shares):
            for core in range(2):
                total = total + small[place, core].astype(wide_type)
        total = total[:small_rows] + total[small_rows:]
        for level in range(2):
            start = 9 * level
            for step in range(5):
                results[6 * level + step][...] = total[start + step]
            for step in range(2):
                own = jnp.where(
                    mp_place() == 0, total[start + 5 + step], total[start + 7 + step]
                )
                results[6 * level + 5][step * width : (step + 1) * width] = own
        for copy in leaving:
            copy.wait()

    space, inside = pl.BlockSpec(memory_space=pltpu.HBM), pl.BlockSpec(memory_space=pltpu.VMEM)
    shapes = [(size, 2 * width) if up else (2 * size, width) for up in rising]
    shapes += ([(width,)] * 5 + [(2 * width,)]) * 2
    return pl.pallas_call(
        kernel,
        out_shape=[jax.ShapeDtypeStruct(shape, wide_type) for shape in shapes],
        in_specs=[space] + [pl.BlockSpec(memory_space=pl.ANY)] * len(earlier),
        out_specs=[space] * 2 + [inside] * 12,
        scratch_shapes=[
            pltpu.VMEM((4, shares, rows, width), low_type),
            pltpu.VMEM((4, size, width), wide_type),
            pltpu.VMEM((shares, 2, 2 * small_rows, width), low_type),
            pltpu.SemaphoreType.DMA((9,)),
        ],
        compiler_params=pltpu.CompilerParams(vmem_limit_bytes=vmem_bytes),
        cost_estimate=pl.CostEstimate(flops=weight[0], bytes_accessed=1, transcendentals=0),
        name="unpack_pieces",
    )(pieces, *earlier)


def place_rows(own, received, kind, earlier=()):
    length, width = own.shape

    def kernel(mine, theirs, *refs):
        target, low_mine, low_theirs, first, second, sems = refs[len(earlier) :]
        copies = [
            pltpu.make_async_copy(source, room, sems.at[index])
            for index, (source, room) in enumerate(((mine, low_mine), (theirs, low_theirs)))
        ]
        for copy in copies:
            copy.start()
        leaving = []
        for index, (room, made, place) in enumerate(
            ((low_mine, first, mp_place()), (low_theirs, second, 1 - mp_place()))
        ):
            copies[index].wait()
            made[...] = room[...].astype(kind)
            leaving.append(pltpu.make_async_copy(made, target.at[place], sems.at[2 + index]))
            leaving[-1].start()
        for copy in leaving:
            copy.wait()

    space = pl.BlockSpec(memory_space=pltpu.HBM)
    return pl.pallas_call(
        kernel,
        out_shape=jax.ShapeDtypeStruct((2, length, width), kind),
        in_specs=[space] * 2 + [pl.BlockSpec(memory_space=pl.ANY)] * len(earlier),
        out_specs=space,
        scratch_shapes=[pltpu.VMEM(own.shape, own.dtype), pltpu.VMEM(own.shape, received.dtype)]
        + [pltpu.VMEM(own.shape, kind)] * 2
        + [pltpu.SemaphoreType.DMA((4,))],
        compiler_params=pltpu.CompilerParams(vmem_limit_bytes=vmem_bytes),
        cost_estimate=pl.CostEstimate(flops=weight[0], bytes_accessed=1, transcendentals=0),
        name="place_rows",
    )(own, received, *earlier)


def mix_back_body(last, get, made, done, extra, pads_ref):
    low, flat, work = extra
    normed_grad, summed, vectors = (get(index) for index in range(3))
    length, width = summed.shape
    half = length // 2
    sums = [jnp.zeros((1, width), wide_type)] * 2
    for rows in tiles(length, row_tile):
        grad = normed_grad[rows, :]
        normal, inverse = normalize(summed[rows, :])
        value = norm_backward(grad, normal, inverse, row_of(vectors, 0))
        work[rows, :] = value
        low[rows, :] = value.astype(low_type)
        sums[0] = sums[0] + jnp.sum(grad * normal, axis=0, keepdims=True)
        sums[1] = sums[1] + jnp.sum(grad, axis=0, keepdims=True)
    pair_table = get(3)
    for step in range(2):
        flat[:, step * width : (step + 1) * width] = dot(
            pair_table[:, step * length : (step + 1) * length], low[...]
        ).astype(low_type)
    work[...] += dot(flat[...], get(4)[...])
    small = made[0]
    small[...] = jnp.zeros_like(small)
    if last:
        for rows in tiles(length, row_tile):
            value = work[rows, :] * live_rows(pads_ref, rows, length)
            start = rows.start % half
            target = made[1 + rows.start // half]
            target[start : start + row_tile, :] = value.astype(target.dtype)
    else:
        residual, below = get(5), get(6)
        out_sums = [jnp.zeros((1, width), wide_type)] * 3
        for rows in tiles(length, row_tile):
            grad = work[rows, :] * live_rows(pads_ref, rows, length)
            made[1][rows, :], made[2][rows, :] = out_rows(
                grad, residual[rows, :], row_of(below, 3), out_sums
            )
        sums = sums + out_sums
        done(1, 2)
        own, other = get(7), get(8)
        hiddens = (own.at[0], own.at[1], other.at[0], other.at[1])
        down_grads(hiddens, made[2], made, done, 3, 4)
    for index, value in enumerate(sums):
        small[index : index + 1, :] = value


def mix_back(normed_grad, summed, vectors, tables, pads, below=None, earlier=()):
    pair_table, _, stack_table = tables
    length, width = rows = summed.shape
    loads = [whole(array) for array in (normed_grad, summed, vectors)]
    loads += [part(pair_table, mp_place), whole(stack_table)]
    outs = [((8, width), wide_type)]
    flops = 4 * length * width * (length + width)
    if below is None:
        half = (length // 2, width)
        outs += [(half, wide_type), (half, low_type)]
    else:
        loads += [whole(array) for array in below]
        size = below[2].shape[2]
        outs += [(rows, wide_type), (rows, low_type)] + [((2, size, width), low_type)] * 2
        flops += 8 * length * width * size
    return staged(
        "mix_back",
        functools.partial(mix_back_body, below is None),
        loads,
        outs,
        earlier,
        [
            pltpu.VMEM(rows, low_type),
            pltpu.VMEM((length, 2 * width), low_type),
            pltpu.VMEM(rows, wide_type),
        ],
        flops,
        20,
    )(pads)


def layer_mix(layer_in, live_mask, params, tables):
    gain_mix, shift_mix = params[:2]
    pair_table, wide_table, stack_table = tables
    width = layer_in.shape[1]
    masked = layer_in * live_mask
    spectra = dot(masked.astype(low_type), wide_table).astype(low_type)
    stacked = jnp.concatenate([spectra[:, :width], spectra[:, width:]], axis=0)
    summed = masked + dot(pair_table, stacked)
    normal, inverse = normalize(summed)
    normed = normal * gain_mix + shift_mix
    return summed, normed, normed.astype(low_type)


def layer_hidden(normed_low, up_weight, up_bias):
    return gate_pair(dot(normed_low, up_weight) + up_bias.astype(wide_type))


def layer_out(normed, branch, live_mask, params):
    down_bias, gain_out, shift_out = params[2:]
    residual = normed + branch + down_bias
    out_normal, out_inverse = normalize(residual)
    result = (out_normal * gain_out + shift_out) * live_mask
    return result, residual


def out_backward(result_cot, live_mask, gain_out, residual):
    out_grad = result_cot * live_mask
    out_normal, out_inverse = normalize(residual)
    resid_grad = norm_backward(out_grad, out_normal, out_inverse, gain_out)
    gainout_grad = jnp.sum(out_grad * out_normal, axis=0)
    shiftout_grad = jnp.sum(out_grad, axis=0)
    branch_cot = resid_grad.astype(low_type)
    downbias_grad = jnp.sum(branch_cot, axis=0, dtype=wide_type)
    return resid_grad, branch_cot, (downbias_grad, gainout_grad, shiftout_grad)


def cot_of(branch_cot, down_weight, slope):
    return (dot_nt(branch_cot, down_weight) * slope.astype(wide_type)).astype(low_type)


def mix_backward(normed_grad, live_mask, gain_mix, summed, tables):
    pair_table, wide_table, stack_table = tables
    length = summed.shape[0]
    normal, inverse = normalize(summed)
    summed_grad = norm_backward(normed_grad, normal, inverse, gain_mix)
    gainmix_grad = jnp.sum(normed_grad * normal, axis=0)
    shiftmix_grad = jnp.sum(normed_grad, axis=0)
    summed_low = summed_grad.astype(low_type)
    flat_grad = jnp.concatenate(
        [
            dot(pair_table[:, :length], summed_low).astype(low_type),
            dot(pair_table[:, length:], summed_low).astype(low_type),
        ],
        axis=1,
    )
    masked_grad = (summed_grad + dot(flat_grad, stack_table)) * live_mask
    return masked_grad, (gainmix_grad, shiftmix_grad)


def paired(first, second):
    return dot_tn(*first) + dot_tn(*second)


def core_swap(array):
    return dp_swap(array, dp_bits()[0])


def cut(ref, axis, index):
    return ref.at[(slice(None),) * axis + (index,)]


def moved(name, body, arrays, shapes, scratch, copies, earlier):
    space = pl.BlockSpec(memory_space=pltpu.HBM)
    count, late, given = len(arrays), len(earlier), len(shapes)

    def kernel(*refs):
        rest = refs[count + late + given :]
        body(refs[:count], refs[count + late : count + late + given], rest[:-1], rest[-1])

    return pl.pallas_call(
        kernel,
        out_shape=[jax.ShapeDtypeStruct(shape, low_type) for shape in shapes],
        in_specs=[space] * count + [pl.BlockSpec(memory_space=pl.ANY)] * late,
        out_specs=[space] * given,
        cost_estimate=pl.CostEstimate(flops=weight[0], bytes_accessed=1, transcendentals=0),
        scratch_shapes=[pltpu.VMEM(shape, low_type) for shape in scratch]
        + [pltpu.SemaphoreType.DMA((copies,))],
        compiler_params=pltpu.CompilerParams(vmem_limit_bytes=vmem_bytes),
        name=name,
    )(*arrays, *earlier)


def sum_parts(arrays, views, targets, shapes, part_shape, earlier):
    count, terms = len(views), len(arrays)

    def body(sources, results, held, sems):
        loads = [
            [
                pltpu.make_async_copy(
                    view(source), held[terms * index + side], sems.at[terms * index + side]
                )
                for side, source in enumerate(sources)
            ]
            for index, view in enumerate(views)
        ]
        for group in loads:
            for copy in group:
                copy.start()
        leaving = []
        for index, group in enumerate(loads):
            for copy in group:
                copy.wait()
            rooms = held[terms * index : terms * (index + 1)]
            value = sum(room[...].astype(wide_type) for room in rooms)
            rooms[0][...] = value.astype(low_type)
            leaving.append(
                pltpu.make_async_copy(
                    rooms[0], targets[index](results), sems.at[terms * count + index]
                )
            )
            leaving[-1].start()
        for copy in leaving:
            copy.wait()

    return moved(
        "sum_parts",
        body,
        arrays,
        shapes,
        [part_shape] * (terms * count),
        (terms + 1) * count,
        earlier,
    )


def sum_split(arrays, axis, place, earlier=()):
    shape, count = arrays[0].shape, arrays[0].shape[axis]
    shape = shape[:axis] + shape[axis + 1 :]
    order = [*range(1, count), 0]
    return sum_parts(
        arrays,
        [lambda ref, step=step: cut(ref, axis, place() ^ step) for step in order],
        [lambda refs, step=step: refs[step] for step in order],
        [shape] * count,
        shape,
        earlier,
    )


def sum_whole(arrays, earlier=()):
    shape = arrays[0].shape
    parts = 2 if shape[0] % 2 == 0 and len(shape) > 2 else 1
    size = shape[0] // parts
    spans = [pl.ds(step * size, size) for step in range(parts)]
    return sum_parts(
        arrays,
        [lambda ref, at=at: ref.at[at] for at in spans],
        [lambda refs, at=at: refs[0].at[at] for at in spans],
        [shape],
        (size, *shape[1:]),
        earlier,
    )[0]


def sum_both(first, second, earlier):
    shares, halves, rows, width = first[0].shape
    arrays = (*first, *second)
    jobs = [(kind, half) for half in range(halves) for kind in range(2)]
    part_shape = (shares, rows, width)

    def body(sources, results, held, sems):
        loads = []
        for slot, (kind, half) in enumerate(jobs):
            loads.append(
                [
                    pltpu.make_async_copy(
                        sources[2 * kind + side].at[:, half],
                        held[2 * slot + side],
                        sems.at[2 * slot + side],
                    )
                    for side in range(2)
                ]
            )
            for copy in loads[-1]:
                copy.start()
        leaving = []
        for slot, group in enumerate(loads):
            for copy in group:
                copy.wait()
            left, right = held[2 * slot], held[2 * slot + 1]
            value = left[...].astype(wide_type) + right[...].astype(wide_type)
            left[...] = value.astype(low_type)
            target = results[0].at[:, pl.ds(slot * rows, rows)]
            leaving.append(pltpu.make_async_copy(left, target, sems.at[8 + slot]))
            leaving[-1].start()
        for copy in leaving:
            copy.wait()

    return moved(
        "sum_both",
        body,
        arrays,
        [(shares, 2 * halves * rows, width)],
        [part_shape] * 8,
        12,
        earlier,
    )[0]


def join_parts(arrays, axis, place, earlier=()):
    shape, count = arrays[0].shape, len(arrays)
    whole_shape = shape[:axis] + (count,) + shape[axis:]

    def body(sources, results, held, sems):
        copies = [
            pltpu.make_async_copy(source, room, sems.at[step])
            for step, (source, room) in enumerate(zip(sources, held))
        ]
        for copy in copies:
            copy.start()
        leaving = [
            pltpu.make_async_copy(
                room, cut(results[0], axis, place() ^ step), sems.at[count + step]
            )
            for step, room in enumerate(held)
        ]
        for copy, after in zip(copies, leaving):
            copy.wait()
            after.start()
        for copy in leaving:
            copy.wait()

    return moved(
        "join_parts", body, arrays, [whole_shape], [shape] * count, 2 * count, earlier
    )[0]


def axis_place(axis):
    if axis == "mp":
        return lambda: 0
    if axis == "near":
        return lambda: lax.rem(lax.axis_index("dp") // 2, 2)
    return lambda: lax.axis_index("dp") // 4


def axis_count(axis):
    return lax.axis_size("dp") // 4 if axis == "far" else 2


def axis_swap(array, axis, step):
    if axis == "mp":
        return mp_swap(array)
    return dp_swap(array, (2 if axis == "near" else 4) * step)


class FarTotal:
    def __init__(self, own, received, steps, earlier=()):
        self.axes = ["mp", "far", "near"]
        shape = tuple(axis_count(axis) for axis in self.axes) + (-1, own.shape[-1])
        self.arrays = [own.reshape(shape), received.reshape(shape)]
        self.steps, self.gone = list(steps), []
        self.finish(*earlier)

    def finish(self, *earlier):
        if not self.steps:
            self.total = self.last = sum_whole(self.arrays, earlier)
            return self.last
        name = self.steps.pop(0)
        axis = self.axes.index(name)
        self.axes.pop(axis)
        if name != "mp":
            self.gone.append((name, axis - ("mp" in self.axes)))
        own, *given = sum_split(self.arrays, axis, axis_place(name), earlier)
        self.arrays = [own] + [
            axis_swap(array, name, step + 1) for step, array in enumerate(given)
        ]
        self.last = own
        return own

    def turn(self):
        name, _ = self.gone[-1]
        self.arrays = [self.total] + [
            axis_swap(self.total, name, step) for step in range(1, axis_count(name))
        ]

    def gather(self, *earlier):
        name, axis = self.gone.pop()
        self.total = self.last = join_parts(self.arrays, axis, axis_place(name), earlier)
        if self.gone:
            self.turn()
        else:
            self.total = self.total.reshape(-1, self.total.shape[-1])
        return self.last


def backward_overlapped(leaving, forward_parts, vectors, tables, blocks, pads, final_out):
    resid, cot, small_out, down_keep, down_send = leaving
    (summed_one, low_one, residual_one, hiddens_one, slopes_one), (summed, low, slopes) = (
        forward_parts
    )
    width = low.shape[1]
    shares = lax.axis_size("dp") // 2
    down_near = core_swap(down_send)
    up_send, total, bias_send = cot_rows(
        cot, low, resid, slopes[1::2], blocks[1][1::2], pads, (), shares
    )
    up_near = core_swap(up_send)
    up_keep, normed_grad, bias_keep = cot_rows(
        cot, low, total, slopes[0::2], blocks[1][0::2], pads, (), shares
    )
    bias_two = (bias_keep, bias_send)
    layer_two = sum_both((down_keep, down_near), (up_keep, up_near), (normed_grad,))
    scattered = lax.psum_scatter(
        layer_two, "dp", scatter_dimension=0, axis_index_groups=core_groups(), tiled=False
    )
    small_mix, resid, cot, down_keep, down_send = mix_back(
        normed_grad,
        summed,
        vectors[1],
        tables,
        pads,
        (residual_one, vectors[0], *hiddens_one),
        (layer_two,),
    )
    down_near = core_swap(down_send)
    up_send, total, bias_send = cot_rows(
        cot, low_one, resid, slopes_one[1::2], blocks[0][1::2], pads
    )
    up_near = core_swap(up_send)
    down_one = FarTotal(down_keep, down_near, ("mp", "far", "near"), (total,))
    up_keep, normed_grad, bias_keep = cot_rows(
        cot, low_one, total, slopes_one[0::2], blocks[0][0::2], pads, (down_one.last,)
    )
    bias_one = (bias_keep, bias_send)
    up_one = FarTotal(up_keep, up_near, ("near", "mp", "far"), (normed_grad,))
    last = down_one.finish(up_one.last)
    small_last, grad_own, grad_given = mix_back(
        normed_grad, summed_one, vectors[0], tables, pads, None, (last, final_out)
    )
    last = up_one.finish(grad_given)
    small = small_matrix(
        ((small_last, small_mix, *bias_one), (small_mix, small_out, *bias_two)), pads, (last,)
    )
    small_other = mp_swap(small)
    weight[0] = heavy
    last = down_one.finish(small)
    grad_received = mp_swap(gate(grad_given, last))
    last = up_one.finish(last)
    input_grad = place_rows(grad_own, grad_received, wide_type, (last,))
    piece = pack_pieces([down_one.arrays, up_one.arrays], [], (input_grad,))
    pieces = [piece] + [axis_swap(piece, "far", step) for step in range(1, axis_count("far"))]
    half = scattered.shape[0] // 2
    packed = pack_pieces(
        [[scattered[:half], mp_swap(scattered[half:])]], [small, small_other], (piece,)
    )
    both = lax.all_gather(packed, "dp", axis=0, tiled=False)
    joined = join_parts(pieces, 0, axis_place("far"), (packed,))
    joined = join_parts([joined, axis_swap(joined, "near", 1)], 1, axis_place("near"))
    joined = joined.reshape(-1, *piece.shape)
    near_joined = core_swap(joined)
    down_two, up_two, *small = unpack_pieces(both, small.shape[0], (joined,))
    down_one, up_one = unpack_pair(joined, near_joined)
    weight[0] = 1
    return input_grad, ((up_one, down_one), (up_two, down_two)), small


def backward_plain(grad, live_mask, params, weights, tables, saved):
    large, small, bias = [None] * 2, [None] * 2, [None] * 2
    for level in (1, 0):
        gain_mix, _, _, gain_out, _ = params[level]
        summed, normed_low, residual, kept = saved[level]
        ((up_weight, down_weight),) = weights[level]
        ((hidden, slope),) = kept
        resid_grad, branch_cot, small_out = out_backward(grad, live_mask, gain_out, residual)
        down_grad = dot_tn(hidden, branch_cot).astype(low_type)
        cot = cot_of(branch_cot, down_weight, slope)
        up_grad = dot_tn(normed_low, cot).astype(low_type)
        bias[level] = [jnp.sum(cot, axis=0, dtype=wide_type)]
        grad, small_mix = mix_backward(
            resid_grad + dot_nt(cot, up_weight), live_mask, gain_mix, summed, tables
        )
        small[level] = small_mix + small_out
        large[level] = (total_plain(up_grad, 1), total_plain(down_grad, 0))
    return grad, large, small, bias


def on_device(*arguments):
    inputs, pad_counts = arguments[:2]
    layer_args = (arguments[2:10], arguments[10:18])
    cotangent = arguments[18]
    mp_count = lax.axis_size("mp")
    mine = lax.axis_index("mp")
    feature_width = inputs.shape[2]
    row_length = inputs.shape[1] * mp_count
    cos_seq, sin_seq = fourier_table(row_length)
    pair_full = np.concatenate([cos_seq, -sin_seq], axis=1)
    turned = 1 - 2 * ((np.arange(row_length)[:, None] + np.arange(2 * row_length)[None, :]) % 2)
    if mp_count == 2:
        pair_table = jnp.asarray(np.stack([pair_full, pair_full * turned]), low_type)
    else:
        pair_table = jnp.asarray(pair_full, low_type)
    wide_table = jnp.asarray(np.concatenate(fourier_table(feature_width), axis=1), low_type)
    stack_table = jnp.asarray(np.concatenate(fourier_table(feature_width), axis=0), low_type)
    tables = (pair_table, wide_table, stack_table)
    (up_one, down_one), (up_two, down_two) = [(args[2], args[4]) for args in layer_args]
    biases = jnp.stack([args[3] for args in layer_args])
    if mp_count == 2:
        core, near, far = dp_bits()[:3]
        core_bit = bit_of(core)
        own_rows, up_part, down_part = cut_first(up_one, up_two, down_two)
        own_rows = mp_swap(own_rows)
        given, block, given_cot = cut_next(inputs, cotangent, down_one, (own_rows,))
        up_part, down_part = mp_swap(up_part), mp_swap(down_part)
        received = mp_swap(given)
        far_rows = lax.all_gather(own_rows, "dp", axis=0, tiled=False)
        up_part = fetch_join(up_part, far)
        down_part = fetch_join(down_part, near)
        down_first = mp_swap(gate(block, received))
        other_biases = mp_swap(biases)
        vectors = []
        for level in range(2):
            args = layer_args[level]
            members = [args[0], args[1], args[5], args[6], args[7]]
            members += [
                take_block(array[level], (core_bit + flip) % 2)
                for array in (biases, other_biases)
                for flip in range(2)
            ]
            vectors.append(select_rows(members, 16))
        own_blocks = [
            [own_block(up, down, flip) for flip in range(2)]
            for up, down in ((up_one, down_one), (up_two, down_two))
        ]
        summed_one, normed, low_one, partial, hidden_a, slope_a = enter(
            inputs, received, tables, vectors[0], own_blocks[0], pad_counts
        )
        up_part = fetch_join(gate(up_part, low_one), near)
        down_part = fetch_join(gate(down_part, low_one), far)
        up_near, down_near = core_swap(up_part), core_swap(down_part)
        received_cot = mp_swap(gate(given_cot, down_part))
        down_second = core_swap(down_first)
        far_blocks = [
            (far_columns(far_rows, flip), whole(array))
            for flip, array in enumerate((down_first, down_second))
        ]
        hidden_b, slope_b, residual_one, summed, normed, low, partial, hidden_c, slope_c = middle(
            low_one,
            normed,
            partial,
            tables,
            vectors,
            far_blocks,
            own_blocks[1],
            pad_counts,
        )
        late_blocks = [(whole(up_part), whole(down_part)), (whole(up_near), whole(down_near))]
        out_own, out_given, resid, cot, small_out, slope_d, down_keep, down_send = leave(
            low,
            normed,
            partial,
            vectors[1],
            late_blocks,
            cotangent,
            received_cot,
            hidden_c,
            pad_counts,
        )
        blocks = [own_blocks[0] + far_blocks, own_blocks[1] + late_blocks]
        slopes_one, slopes_two = (
            [part(array, lambda at=at: at) for array in arrays for at in (0, 1)]
            for arrays in ((slope_a, slope_b), (slope_c, slope_d))
        )
        out_received = mp_swap(out_given)
        final_out = place_rows(out_own, out_received, low_type)
        input_grad, large, small = backward_overlapped(
            (resid, cot, small_out, down_keep, down_send),
            (
                (summed_one, low_one, residual_one, (hidden_a, hidden_b), slopes_one),
                (summed, low, slopes_two),
            ),
            vectors,
            tables,
            blocks,
            pad_counts,
            final_out,
        )
    else:
        params = [
            tuple(args[step].astype(wide_type) for step in (0, 1, 5, 6, 7)) for args in layer_args
        ]
        position = jnp.arange(row_length, dtype=jnp.int32)
        pads = lax.dynamic_index_in_dim(pad_counts, mine, 0, False)
        live_mask = (position < row_length - pads).astype(wide_type)[:, None]
        weights, saved = [], []
        biases = lax.all_gather(biases, "mp", axis=1, tiled=True)
        current = gathered_row(inputs).astype(wide_type)
        for level, (up_weight, down_weight) in enumerate(((up_one, down_one), (up_two, down_two))):
            up_weight = lax.all_gather(up_weight, "mp", axis=1, tiled=True)
            down_weight = lax.all_gather(down_weight, "mp", axis=0, tiled=True)
            weights.append(((up_weight, down_weight),))
            summed, normed, normed_low = layer_mix(current, live_mask, params[level], tables)
            kept = layer_hidden(normed_low, up_weight, biases[level])
            current, residual = layer_out(
                normed, dot(kept[0], down_weight), live_mask, params[level]
            )
            saved.append((summed, normed_low, residual, (kept,)))
        grad = gathered_row(cotangent).astype(wide_type)
        final_out = return_rows(current.astype(low_type))
        grad, large, small, bias = backward_plain(grad, live_mask, params, weights, tables, saved)
        input_grad = return_rows(grad.astype(low_type)).astype(wide_type)
    hidden_own = layer_args[0][3].shape[0]
    if mp_count != 2:
        rows = []
        for level in range(2):
            rows.extend(small[level])
            rows.extend(bias[level][0].reshape(-1, feature_width))
        total = total_small(select_rows(rows, 8 * -(-len(rows) // 8)))
        count, small = len(rows) // 2, []
        for level in range(2):
            block = total[level * count : (level + 1) * count]
            small += [block[step] for step in range(5)]
            small.append(
                lax.dynamic_slice_in_dim(block[5:].reshape(-1), mine * hidden_own, hidden_own, 0)
            )
    results = [final_out, input_grad]
    for level in range(2):
        gainmix, shiftmix, downbias, gainout, shiftout, bias_total = small[6 * level : 6 * level + 6]
        up_total, down_total = large[level]
        results += [gainmix, shiftmix, up_total, bias_total, down_total, downbias, gainout, shiftout]
    return tuple(results)


def solution(mesh):
    layer_specs = (P(), P(), P(None, "mp"), P("mp"), P("mp", None), P(), P(), P())
    rows = P("dp", "mp", None)
    return jax.shard_map(
        on_device,
        mesh=mesh,
        in_specs=(rows, P("dp"), *layer_specs, *layer_specs, rows),
        out_specs=(rows, rows, *layer_specs, *layer_specs),
        check_vma=False,
    )
```

```python
import functools
import math

import jax
import jax.numpy as jnp
import numpy as np
from jax import lax
from jax.experimental import pallas as pl
from jax.experimental.pallas import tpu as pltpu
from jax.sharding import PartitionSpec as P

norm_eps = 1e-05
low_type = jnp.bfloat16
wide_type = jnp.float32
vmem_bytes = 62 * 2**20
window = 4
heavy = 6 * 10**9
weight = [1]


def fourier_table(points):
    indices = np.arange(points, dtype=np.int64)
    phases = (indices[:, None] * indices[None, :]) % points
    angles = phases.astype(np.float32) * np.float32(2.0 * math.pi / points)
    factor = np.float32(points ** (-0.5))
    return (np.cos(angles) * factor, np.sin(angles) * factor)


def dot(left, right):
    return jnp.dot(left, right, preferred_element_type=wide_type)


def dot_tn(left, right):
    return lax.dot_general(left, right, (((0,), (0,)), ((), ())), preferred_element_type=wide_type)


def dot_nt(left, right):
    return lax.dot_general(left, right, (((1,), (1,)), ((), ())), preferred_element_type=wide_type)


def normalize(activity):
    center = jnp.mean(activity, axis=-1, keepdims=True)
    centered = activity - center
    spread = jnp.mean(centered * centered, axis=-1, keepdims=True)
    inverse = lax.rsqrt(spread + norm_eps)
    return centered * inverse, inverse


def norm_backward(grad, normal, inverse, gain):
    pulled = grad * gain
    first = jnp.mean(pulled, axis=-1, keepdims=True)
    second = jnp.mean(pulled * normal, axis=-1, keepdims=True)
    return inverse * (pulled - first - normal * second)


def gate_pair(preact):
    scale = math.sqrt(2.0 / math.pi)
    square = preact * preact
    turn = jnp.tanh(preact * (scale + (0.044715 * scale) * square))
    half = 0.5 + 0.5 * turn
    hidden = preact * half
    slope = half + hidden * (1.0 - turn) * (scale + (3 * 0.044715 * scale) * square)
    return hidden.astype(low_type), slope.astype(low_type)


def flip_pairs(size, bit):
    return [(index, index ^ bit) for index in range(size)]


def order_halves(bit_value, mine, theirs, axis=0):
    return jnp.where(
        bit_value == 0,
        jnp.concatenate([mine, theirs], axis=axis),
        jnp.concatenate([theirs, mine], axis=axis),
    )


def take_block(array, which, count=2, axis=0):
    size = array.shape[axis] // count
    return lax.dynamic_slice_in_dim(array, which * size, size, axis)


def dp_bits():
    return [1 << level for level in range(lax.axis_size("dp").bit_length() - 1)]


def bit_of(bit):
    return (lax.axis_index("dp") // bit) % 2


def dp_swap(array, bit):
    return lax.ppermute(array, "dp", flip_pairs(lax.axis_size("dp"), bit))


def mp_swap(array):
    return lax.ppermute(array, "mp", [(0, 1), (1, 0)])


def add_low(left, right):
    return (left.astype(wide_type) + right.astype(wide_type)).astype(low_type)


def gate(value, *earlier):
    def kernel(*refs):
        pass

    anywhere = pl.BlockSpec(memory_space=pl.ANY)
    return pl.pallas_call(
        kernel,
        out_shape=jax.ShapeDtypeStruct(value.shape, value.dtype),
        in_specs=[anywhere] * (1 + len(earlier)),
        out_specs=anywhere,
        input_output_aliases={0: 0},
        name="gate",
    )(value, *earlier)


def fetch_join(piece, bit):
    return order_halves(bit_of(bit), piece, dp_swap(piece, bit))


def bounce(name, jobs, shapes, arrays, earlier=()):
    count, late, given = len(arrays), len(earlier), len(shapes)

    def kernel(*refs):
        targets = refs[count + late : count + late + given]
        held, sems = refs[count + late + given : -1], refs[-1]
        work = jobs(refs[:count], held)
        copies = [
            pltpu.make_async_copy(source, target, sems.at[given + index])
            for index, (_, source, target) in enumerate(work)
        ]
        for copy in copies:
            copy.start()
        leaving = [
            pltpu.make_async_copy(source, target, sems.at[index])
            for index, (source, target) in enumerate(zip(held, targets))
        ]
        for slot in range(given):
            for (place, _, _), copy in zip(work, copies):
                if place == slot:
                    copy.wait()
            leaving[slot].start()
        for copy in leaving:
            copy.wait()

    space = pl.BlockSpec(memory_space=pltpu.HBM)
    return pl.pallas_call(
        kernel,
        out_shape=[jax.ShapeDtypeStruct(shape, low_type) for shape in shapes],
        in_specs=[space] * count + [pl.BlockSpec(memory_space=pl.ANY)] * late,
        out_specs=[space] * given,
        scratch_shapes=[pltpu.VMEM(shape, low_type) for shape in shapes]
        + [pltpu.SemaphoreType.DMA((4 * given,))],
        compiler_params=pltpu.CompilerParams(vmem_limit_bytes=vmem_bytes),
        name=name,
    )(*arrays, *earlier)


def span(index, count):
    return pl.ds(pl.multiple_of(index * count, count), count)


def cut_first(up_one, up_two, down_two):
    width, size = up_one.shape[0], up_one.shape[1] // 2
    rows = width // lax.axis_size("dp")
    quarter = (width // 4, size // 4)

    def jobs(sources, held):
        place, core = lax.axis_index("dp"), core_place()
        near, away = lax.rem(place // 2, 2), lax.rem(place // 4, 2)
        own = sources[0].at[span(place, rows)]
        return [
            (0, own.at[:, pl.ds(0, size)], held[0].at[pl.ds(0, rows)]),
            (0, own.at[:, pl.ds(size, size)], held[0].at[pl.ds(rows, rows)]),
            (1, sources[1].at[span(2 * near + away, quarter[0]), span(core, size)], held[1]),
            (2, sources[2].at[span(core * 4 + 2 * away + near, quarter[1])], held[2]),
        ]

    shapes = ((2 * rows, size), (quarter[0], size), (quarter[1], width))
    return bounce("cut_first", jobs, shapes, (up_one, up_two, down_two))


def cut_next(inputs, cotangent, down_one, earlier):
    length, width = cotangent.shape[1:]
    size = down_one.shape[0] // 2

    def jobs(sources, held):
        rows, cots, down = sources
        return [
            (0, rows.at[1 - mp_place()], held[0]),
            (1, down.at[span(core_place(), size)], held[1]),
            (2, cots.at[1 - mp_place()], held[2]),
        ]

    shapes = ((length, width), (size, width), (length, width))
    return bounce("cut_next", jobs, shapes, (inputs, cotangent, down_one), earlier)


def select_rows(rows, count):
    index = lax.broadcasted_iota(jnp.int32, (count, rows[0].shape[0]), 0)
    total = jnp.zeros(index.shape, wide_type)
    for place, row in enumerate(rows):
        total = jnp.where(index == place, row.astype(wide_type)[None], total)
    return total


def core_groups():
    return [
        [place for place in range(lax.axis_size("dp")) if place % 2 == which] for which in (0, 1)
    ]


def total_plain(part, hidden_axis):
    own = lax.psum_scatter(part, "mp", scatter_dimension=hidden_axis, tiled=True)
    return lax.psum(own, "dp").astype(wide_type)


def total_small(vector):
    for bit in dp_bits():
        vector = vector + dp_swap(vector, bit)
    if lax.axis_size("mp") == 2:
        return vector + mp_swap(vector)
    return lax.psum(vector, "mp")


def given_row(array):
    return lax.dynamic_index_in_dim(array, 1 - lax.axis_index("mp"), 0, keepdims=False)


def gathered_row(array):
    return lax.all_to_all(array, "mp", split_axis=0, concat_axis=1, tiled=True)[0]


def return_rows(array):
    return lax.all_to_all(array[None], "mp", split_axis=1, concat_axis=0, tiled=True)


def staged(name, body, loads, outs, earlier=(), scratch=(), flops=0, stress=0):
    count, late, given = len(loads), len(earlier), len(outs)

    def kernel(*refs):
        sources = refs[1 : 1 + count]
        targets = refs[1 + count + late : 1 + count + late + given]
        rest = refs[1 + count + late + given :]
        held, made = rest[:count], rest[count : count + given]
        in_sems, out_sems, *extra = rest[count + given :]
        copies, begun, sent = {}, set(), []
        for index, load in enumerate(loads):
            view = load[2](sources[index])
            copies[index] = pltpu.make_async_copy(view, held[index], in_sems.at[index])
        queue = sorted(range(count), key=lambda index: math.prod(loads[index][1]) > 2**16)

        def begin(index):
            if index not in begun:
                copies[index].start()
                begun.add(index)

        def get(index):
            begin(index)
            if index in copies:
                copies.pop(index).wait()
                while sum(place in copies for place in begun) < window and len(begun) < count:
                    begin(next(place for place in queue if place not in begun))
            return held[index]

        for index in queue:
            if math.prod(loads[index][1]) <= 2**16 or len(begun) < window:
                begin(index)

        def done(*indices):
            for index in indices:
                slot = len(sent)
                if isinstance(index, tuple):
                    index, place = index
                    source, target = made[index].at[place], targets[index].at[place]
                else:
                    source, target = made[index], targets[index]
                copy = pltpu.make_async_copy(source, target, out_sems.at[slot])
                copy.start()
                sent.append((index, copy))

        body(get, made, done, extra, refs[0])
        for index in list(copies):
            get(index)
        left = {index for index, _ in sent}
        done(*[index for index in range(given) if index not in left])
        for _, copy in sent:
            copy.wait()

    space = pl.BlockSpec(memory_space=pltpu.HBM)
    moved = sum(math.prod(load[1]) * load[0].dtype.itemsize for load in loads)
    moved += sum(math.prod(out[0]) * jnp.dtype(out[1]).itemsize for out in outs)
    call = pl.pallas_call(
        kernel,
        out_shape=[jax.ShapeDtypeStruct(*out) for out in outs],
        in_specs=[pl.BlockSpec(memory_space=pltpu.SMEM)]
        + [space] * count
        + [pl.BlockSpec(memory_space=pl.ANY)] * late,
        out_specs=[space] * given,
        cost_estimate=pl.CostEstimate(
            flops=1 + stress * flops, bytes_accessed=1 + stress * moved, transcendentals=0
        ),
        scratch_shapes=[pltpu.VMEM(load[1], load[0].dtype) for load in loads]
        + [pltpu.VMEM(*out) for out in outs]
        + [pltpu.SemaphoreType.DMA((count,)), pltpu.SemaphoreType.DMA((2 * given,))]
        + list(scratch),
        compiler_params=pltpu.CompilerParams(vmem_limit_bytes=vmem_bytes),
        name=name,
    )
    return lambda pads: call(pads, *[load[0] for load in loads], *earlier)


def whole(array):
    return (array, array.shape, lambda ref: ref)


def part(array, index):
    return (array, array.shape[1:], lambda ref: ref.at[index()])


def mp_place():
    return lax.axis_index("mp")


def core_place():
    return lax.rem(lax.axis_index("dp"), 2)


def share(flip):
    return (core_place() + flip) % 2


def own_block(up_weight, down_weight, flip):
    width, size = up_weight.shape[0], up_weight.shape[1] // 2

    def span():
        return pl.ds(pl.multiple_of(share(flip) * size, size), size)

    return (
        (up_weight, (width, size), lambda ref: ref.at[:, span()]),
        (down_weight, (size, width), lambda ref: ref.at[span()]),
    )


def far_columns(pieces, flip):
    places, rows, size = pieces.shape
    half = rows // 2
    return (
        pieces,
        (places, half, size),
        lambda ref: ref.at[:, pl.ds(pl.multiple_of(share(flip) * half, half), half)],
    )


def matrix(ref):
    return ref[...].reshape(-1, ref.shape[-1])


def tiles(total, size):
    return [slice(start, start + size) for start in range(0, total, size)]


def live_rows(pads_ref, rows, length):
    place = lax.broadcasted_iota(jnp.int32, (rows.stop - rows.start, 1), 0) + rows.start
    place = lax.rem(place + mp_place() * (length // 2), length)
    return (place < length - pads_ref[mp_place()]).astype(wide_type)


def row_of(ref, index):
    return ref[index : index + 1, :]


row_tile = 128


def mix_rows(summed, normed, low, spectra, wide_table, pair_table, vectors):
    length, width = summed.shape
    low[...] = summed[...].astype(low_type)
    wide = wide_table()
    for columns in tiles(2 * width, width):
        spectra[:, columns] = dot(low[...], wide[:, columns]).astype(low_type)
    pair = pair_table()
    summed[...] += dot(pair[:, :length], spectra[:, :width])
    summed[...] += dot(pair[:, length:], spectra[:, width:])
    for rows in tiles(length, row_tile):
        normal, _ = normalize(summed[rows, :])
        value = normal * row_of(vectors, 0) + row_of(vectors, 1)
        normed[rows, :] = value
        low[rows, :] = value.astype(low_type)


def feed_block(low, up_weight, bias, down_weight, hidden, slope):
    hidden[...], slope[...] = gate_pair(dot(low[...], matrix(up_weight())) + bias)
    return dot(hidden[...], matrix(down_weight()))


def out_norm(residual, normed, parts, vectors):
    for rows in tiles(residual.shape[0], row_tile):
        value = normed[rows, :]
        for item in parts:
            value = value + item[rows, :]
        value = value + row_of(vectors, 2)
        residual[rows, :] = value
        normal, _ = normalize(value)
        yield rows, normal * row_of(vectors, 3) + row_of(vectors, 4)


def enter_body(get, made, done, extra, pads_ref):
    summed, normed, low, partial, hidden, slope = made
    (spectra,) = extra
    length, width = summed.shape
    half = length // 2
    for rows in tiles(length, row_tile):
        start = rows.start % half
        piece = get(rows.start // half)[start : start + row_tile, :].astype(wide_type)
        summed[rows, :] = piece * live_rows(pads_ref, rows, length)
    vectors = get(4)
    mix_rows(summed, normed, low, spectra, lambda: get(2), lambda: get(3), vectors)
    done(0, 1, 2)
    for block in range(2):
        value = feed_block(
            low,
            lambda: get(5 + 2 * block),
            row_of(vectors, 5 + block),
            lambda: get(6 + 2 * block),
            hidden.at[block],
            slope.at[block],
        )
        done((4, block), (5, block))
        partial[...] = value if block == 0 else partial[...] + value


def enter(inputs, received, tables, vectors, blocks, pads):
    pair_table, wide_table, _ = tables
    length, width = 2 * received.shape[0], received.shape[1]
    size = blocks[0][0][1][1]
    loads = [part(inputs, mp_place), whole(received), whole(wide_table)]
    loads += [part(pair_table, mp_place), whole(vectors), *blocks[0], *blocks[1]]
    rows = (length, width)
    return staged(
        "enter",
        enter_body,
        loads,
        [(rows, wide_type), (rows, wide_type), (rows, low_type), (rows, wide_type)]
        + [((2, length, size), low_type)] * 2,
        (),
        [pltpu.VMEM((length, 2 * width), low_type)],
        4 * length * width * (length + width + 2 * size),
    )(pads)


def middle_body(get, made, done, extra, pads_ref):
    hidden, slope, residual, summed, normed, low, partial, hidden_two, slope_two = made
    spectra, total = extra
    length = summed.shape[0]
    low_one, vectors = get(0), get(5)
    for block in range(2):
        value = feed_block(
            low_one,
            lambda: get(1 + 2 * block),
            row_of(vectors, 7 + block),
            lambda: get(2 + 2 * block),
            hidden.at[block],
            slope.at[block],
        )
        done((0, block), (1, block))
        total[...] = value if block == 0 else total[...] + value
    for rows, value in out_norm(residual, get(6), (total, get(7)), vectors):
        summed[rows, :] = value * live_rows(pads_ref, rows, length)
    done(2)
    vectors = get(10)
    mix_rows(summed, normed, low, spectra, lambda: get(8), lambda: get(9), vectors)
    done(3, 4, 5)
    for block in range(2):
        value = feed_block(
            low,
            lambda: get(11 + 2 * block),
            row_of(vectors, 5 + block),
            lambda: get(12 + 2 * block),
            hidden_two.at[block],
            slope_two.at[block],
        )
        done((7, block), (8, block))
        partial[...] = value if block == 0 else partial[...] + value


def middle(low, normed, partial, tables, vectors, far_blocks, own_blocks, pads, earlier=()):
    pair_table, wide_table, _ = tables
    length, width = rows = low.shape
    size = own_blocks[0][0][1][1]
    loads = [whole(low), *far_blocks[0], *far_blocks[1], whole(vectors[0])]
    loads += [whole(normed), whole(partial), whole(wide_table), part(pair_table, mp_place)]
    loads += [whole(vectors[1]), *own_blocks[0], *own_blocks[1]]
    hidden = ((2, length, size), low_type)
    return staged(
        "middle",
        middle_body,
        loads,
        [hidden, hidden, (rows, wide_type), (rows, wide_type), (rows, wide_type)]
        + [(rows, low_type), (rows, wide_type), hidden, hidden],
        earlier,
        [pltpu.VMEM((length, 2 * width), low_type), pltpu.VMEM(rows, wide_type)],
        4 * length * width * (length + width + 4 * size),
    )(pads)


def down_grads(hiddens, cot, made, done, keep, send):
    for step, index in ((1, send), (0, keep)):
        target = made[index]
        for half in range(2):
            value = dot_tn(hiddens[2 * half + step][...], cot[...]).astype(low_type)
            if len(target.shape) == 4:
                target[:, half] = value.reshape(target.shape[0], *target.shape[2:])
                place = (slice(None), half)
            else:
                target[half] = value
                place = half
            done((index, place))


def leave_body(get, made, done, extra, pads_ref):
    out_own, out_given, resid, cot, small, slope, keep, send = made
    hidden, total, residual = extra
    length, width = resid.shape
    half = length // 2
    low, vectors = get(0), get(5)
    for block in range(2):
        value = feed_block(
            low,
            lambda: get(1 + 2 * block),
            row_of(vectors, 7 + block),
            lambda: get(2 + 2 * block),
            hidden.at[block],
            slope.at[block],
        )
        done((5, block))
        total[...] = value if block == 0 else total[...] + value
    sums = [jnp.zeros((1, width), wide_type)] * 3
    for rows, value in out_norm(residual, get(6), (total, get(7)), vectors):
        live = live_rows(pads_ref, rows, length)
        start = rows.start % half
        target = (out_own, out_given)[rows.start // half]
        target[start : start + row_tile, :] = (value * live).astype(low_type)
        grad = get(8 + rows.start // half)[start : start + row_tile, :].astype(wide_type) * live
        resid[rows, :], cot[rows, :] = out_rows(grad, residual[rows, :], row_of(vectors, 3), sums)
    small[...] = jnp.zeros_like(small)
    for index, value in enumerate(sums):
        small[index : index + 1, :] = value
    done(0, 1, 2, 3, 4)
    own = get(10)
    down_grads((own.at[0], own.at[1], hidden.at[0], hidden.at[1]), cot, made, done, 6, 7)


def leave(low, normed, partial, vectors, blocks, cotangent, received, hidden, pads, earlier=()):
    length, width = rows = low.shape
    size = hidden.shape[2]
    shares = lax.axis_size("dp") // 2
    loads = [whole(low), *blocks[0], *blocks[1], whole(vectors), whole(normed), whole(partial)]
    loads += [part(cotangent, mp_place), whole(received), whole(hidden)]
    half, grads = (length // 2, width), ((shares, 2, size // shares, width), low_type)
    return staged(
        "leave",
        leave_body,
        loads,
        [(half, low_type), (half, low_type), (rows, wide_type), (rows, low_type)]
        + [((8, width), wide_type), ((2, length, size), low_type), grads, grads],
        earlier,
        [pltpu.VMEM((2, length, size), low_type)] + [pltpu.VMEM(rows, wide_type)] * 2,
        16 * length * width * size,
    )(pads)


def out_rows(grad, residual, gain, sums):
    normal, inverse = normalize(residual)
    resid_grad = norm_backward(grad, normal, inverse, gain)
    low = resid_grad.astype(low_type)
    parts = (grad * normal, grad, low.astype(wide_type))
    for index, value in enumerate(parts):
        sums[index] = sums[index] + jnp.sum(value, axis=0, keepdims=True)
    return resid_grad, low


def cot_body(get, made, done, extra, pads_ref):
    grads, total, small = made
    (cots,) = extra
    branch_cot = get(0)
    small[...] = jnp.zeros_like(small)
    places = ((1, 2, 5), (6, 7, 8))
    for half in range(2):
        down_weight, slope, up_weight = places[half]
        value = dot_nt(branch_cot[...], matrix(get(down_weight)))
        value = (value * get(slope)[...].astype(wide_type)).astype(low_type)
        cots[...] = value
        small[half : half + 1, :] = jnp.sum(value.astype(wide_type), axis=0, keepdims=True)
        value = dot_tn(get(3)[...], cots[...]).astype(low_type)
        if len(grads.shape) == 4:
            grads[:, half] = value.reshape(grads.shape[0], *grads.shape[2:])
            done((0, (slice(None), half)))
        else:
            grads[half] = value
            done((0, half))
        before, up_weight = (get(4) if half == 0 else total), get(up_weight)
        count = 1 + half
        for rows in tiles(total.shape[0], total.shape[0] // count):
            total[rows, :] = before[rows, :] + dot_nt(cots[rows, :], matrix(up_weight))
            if half:
                done((1, pl.ds(rows.start, rows.stop - rows.start)))


def cot_rows(branch_cot, low, before, slopes, blocks, pads, earlier=(), shares=0):
    length, width = rows = low.shape
    (up_a, down_a), (up_b, down_b) = blocks
    loads = [whole(branch_cot), down_a, slopes[0], whole(low), whole(before), up_a]
    loads += [down_b, slopes[1], up_b]
    size = slopes[0][1][1]
    return staged(
        "cot_rows",
        cot_body,
        loads,
        [
            ((shares, 2, width // shares, size) if shares else (2, width, size), low_type),
            (rows, wide_type),
            ((8, size), wide_type),
        ],
        earlier,
        [pltpu.VMEM((length, size), low_type)],
        12 * length * width * size,
        20,
    )(pads)


def small_body(get, made, done, extra, pads_ref):
    total = made[0]
    width = total.shape[1]
    index = lax.broadcasted_iota(jnp.int32, (4, 1), 0)
    for level in range(2):
        mix, out, *biases = (get(4 * level + step) for step in range(4))
        start = 9 * level
        total[start : start + 2, :] = mix[0:2, :]
        first = 0 if level else 2
        total[start + 2 : start + 3, :] = out[first + 2 : first + 3, :]
        total[start + 3 : start + 5, :] = out[first : first + 2, :]
        rows = jnp.zeros((4, width), wide_type)
        for block in range(4):
            half = (mp_place() + block // 2) % 2
            rows = rows + jnp.where(
                index == 2 * half + share(block % 2),
                biases[block % 2][block // 2 : block // 2 + 1, :],
                0.0,
            )
        total[start + 5 : start + 9, :] = rows
    total[18:, :] = jnp.zeros((total.shape[0] - 18, width), wide_type)


def small_matrix(parts, pads, earlier=()):
    loads = [whole(array) for level in parts for array in level]
    width = parts[0][0].shape[1]
    outs = [((32, width), wide_type)]
    return staged("small_matrix", small_body, loads, outs, earlier)(pads)[0]


def pack_pieces(groups, smalls, earlier):
    arrays = [array for group in groups for array in group]
    width = arrays[0].shape[1]
    heights = [group[0].shape[0] for group in groups]
    small_rows = smalls[0].shape[0] if smalls else 0
    count, late = len(arrays), len(earlier)
    size = sum(heights) + 2 * small_rows

    def kernel(*refs):
        sources, small_refs = refs[:count], refs[count : count + len(smalls)]
        target, packed, *held = refs[count + len(smalls) + late : -1]
        sems = refs[-1]
        copies = [
            pltpu.make_async_copy(source, room, sems.at[index])
            for index, (source, room) in enumerate(zip((*sources, *small_refs), held))
        ]
        for copy in copies:
            copy.start()
        leaving, first = [], 0
        for place, group in enumerate(groups):
            span = slice(sum(heights[:place]), sum(heights[: place + 1]))
            value = 0.0
            for index in range(first, first + len(group)):
                copies[index].wait()
                value = value + held[index][...].astype(wide_type)
            packed[span, :] = value.astype(low_type)
            first += len(group)
        if smalls:
            for copy in copies[count:]:
                copy.wait()
            total = held[count][...] + held[count + 1][...]
            high = total.astype(low_type)
            start = sum(heights)
            packed[start : start + small_rows, :] = high
            packed[start + small_rows :, :] = (total - high.astype(wide_type)).astype(low_type)
        copy = pltpu.make_async_copy(packed, target, sems.at[count + 2])
        copy.start()
        copy.wait()

    space = pl.BlockSpec(memory_space=pl.ANY)
    return pl.pallas_call(
        kernel,
        out_shape=jax.ShapeDtypeStruct((size, width), low_type),
        in_specs=[space] * (count + len(smalls)) + [pl.BlockSpec(memory_space=pl.ANY)] * late,
        out_specs=space,
        scratch_shapes=[pltpu.VMEM((size, width), low_type)]
        + [pltpu.VMEM(array.shape, low_type) for array in arrays]
        + [pltpu.VMEM((small_rows, width), wide_type) for _ in smalls]
        + [pltpu.SemaphoreType.DMA((count + 3,))],
        compiler_params=pltpu.CompilerParams(vmem_limit_bytes=24 * 2**20),
        cost_estimate=pl.CostEstimate(flops=weight[0], bytes_accessed=1, transcendentals=0),
        name="pack_pieces",
    )(*arrays, *smalls, *earlier)


def unpack_pair(mine, theirs):
    shares, rows, width = mine.shape
    size = shares * rows

    def kernel(own, near, down, low, held, sems):
        copies = [
            pltpu.make_async_copy(source, low.at[side], sems.at[side])
            for side, source in enumerate((own, near))
        ]
        for copy in copies:
            copy.start()
        leaving = []
        for side in range(2):
            copies[side].wait()
            held[side] = low[side].reshape(size, width).astype(wide_type)
            where = down.at[pl.ds(pl.multiple_of(share(side) * size, size), size)]
            leaving.append(pltpu.make_async_copy(held.at[side], where, sems.at[2 + side]))
            leaving[-1].start()
        for copy in leaving:
            copy.wait()

    return pl.pallas_call(
        kernel,
        out_shape=jax.ShapeDtypeStruct((2 * size, width), wide_type),
        in_specs=[pl.BlockSpec(memory_space=pl.ANY)] * 2,
        out_specs=pl.BlockSpec(memory_space=pltpu.HBM),
        scratch_shapes=[
            pltpu.VMEM((2, shares, rows, width), low_type),
            pltpu.VMEM((2, size, width), wide_type),
            pltpu.SemaphoreType.DMA((4,)),
        ],
        compiler_params=pltpu.CompilerParams(vmem_limit_bytes=24 * 2**20),
        cost_estimate=pl.CostEstimate(flops=weight[0], bytes_accessed=1, transcendentals=0),
        name="unpack_pair",
    )(mine, theirs)


def unpack_pieces(gathered, small_rows, earlier):
    shares, width = gathered.shape[0] // 2, gathered.shape[2]
    rising = (False, True, True)
    kinds = len(rising)
    rows = (gathered.shape[1] - 2 * small_rows) // kinds
    size = shares * rows
    pieces = gathered.reshape(shares, 2, -1, width)

    def kernel(source, *refs):
        refs = refs[len(earlier) :]
        targets, results = refs[:kinds], refs[kinds : kinds + 12]
        low, held, small, sems = refs[kinds + 12 :]
        jobs = [(kind, core) for kind in range(kinds) for core in range(2)]
        copies = [
            pltpu.make_async_copy(
                source.at[:, core, pl.ds(kind * rows, rows)], low.at[slot], sems.at[slot]
            )
            for slot, (kind, core) in enumerate(jobs)
        ]
        copies.append(
            pltpu.make_async_copy(
                source.at[:, :, pl.ds(kinds * rows, 2 * small_rows)], small, sems.at[4 * kinds]
            )
        )
        for copy in copies:
            copy.start()
        leaving = []
        for slot, (kind, core) in enumerate(jobs):
            copies[slot].wait()
            held[slot] = low[slot].reshape(size, width).astype(wide_type)
            if rising[kind]:
                where = targets[kind].at[:, pl.ds(core * width, width)]
            else:
                where = targets[kind].at[pl.ds(core * size, size)]
            leaving.append(pltpu.make_async_copy(held.at[slot], where, sems.at[2 * kinds + slot]))
            leaving[-1].start()
        copies[-1].wait()
        total = jnp.zeros((2 * small_rows, width), wide_type)
        for place in range(shares):
            for core in range(2):
                total = total + small[place, core].astype(wide_type)
        total = total[:small_rows] + total[small_rows:]
        for level in range(2):
            start = 9 * level
            for step in range(5):
                results[6 * level + step][...] = total[start + step]
            for step in range(2):
                own = jnp.where(
                    mp_place() == 0, total[start + 5 + step], total[start + 7 + step]
                )
                results[6 * level + 5][step * width : (step + 1) * width] = own
        for copy in leaving:
            copy.wait()

    space, inside = pl.BlockSpec(memory_space=pltpu.HBM), pl.BlockSpec(memory_space=pltpu.VMEM)
    shapes = [(size, 2 * width) if up else (2 * size, width) for up in rising]
    shapes += ([(width,)] * 5 + [(2 * width,)]) * 2
    return pl.pallas_call(
        kernel,
        out_shape=[jax.ShapeDtypeStruct(shape, wide_type) for shape in shapes],
        in_specs=[space] + [pl.BlockSpec(memory_space=pl.ANY)] * len(earlier),
        out_specs=[space] * kinds + [inside] * 12,
        scratch_shapes=[
            pltpu.VMEM((2 * kinds, shares, rows, width), low_type),
            pltpu.VMEM((2 * kinds, size, width), wide_type),
            pltpu.VMEM((shares, 2, 2 * small_rows, width), low_type),
            pltpu.SemaphoreType.DMA((4 * kinds + 1,)),
        ],
        compiler_params=pltpu.CompilerParams(vmem_limit_bytes=vmem_bytes),
        cost_estimate=pl.CostEstimate(flops=weight[0], bytes_accessed=1, transcendentals=0),
        name="unpack_pieces",
    )(pieces, *earlier)


def place_rows(own, received, kind, earlier=()):
    length, width = own.shape

    def kernel(mine, theirs, *refs):
        target, low_mine, low_theirs, first, second, sems = refs[len(earlier) :]
        copies = [
            pltpu.make_async_copy(source, room, sems.at[index])
            for index, (source, room) in enumerate(((mine, low_mine), (theirs, low_theirs)))
        ]
        for copy in copies:
            copy.start()
        leaving = []
        for index, (room, made, place) in enumerate(
            ((low_mine, first, mp_place()), (low_theirs, second, 1 - mp_place()))
        ):
            copies[index].wait()
            made[...] = room[...].astype(kind)
            leaving.append(pltpu.make_async_copy(made, target.at[place], sems.at[2 + index]))
            leaving[-1].start()
        for copy in leaving:
            copy.wait()

    space = pl.BlockSpec(memory_space=pltpu.HBM)
    return pl.pallas_call(
        kernel,
        out_shape=jax.ShapeDtypeStruct((2, length, width), kind),
        in_specs=[pl.BlockSpec(memory_space=pl.ANY)] * 2 + [pl.BlockSpec(memory_space=pl.ANY)] * len(earlier),
        out_specs=space,
        scratch_shapes=[pltpu.VMEM(own.shape, own.dtype), pltpu.VMEM(own.shape, received.dtype)]
        + [pltpu.VMEM(own.shape, kind)] * 2
        + [pltpu.SemaphoreType.DMA((4,))],
        compiler_params=pltpu.CompilerParams(vmem_limit_bytes=24 * 2**20),
        cost_estimate=pl.CostEstimate(flops=weight[0], bytes_accessed=1, transcendentals=0),
        name="place_rows",
    )(own, received, *earlier)


def mix_back_body(last, get, made, done, extra, pads_ref):
    low, flat, work = extra
    normed_grad, summed, vectors = (get(index) for index in range(3))
    length, width = summed.shape
    half = length // 2
    sums = [jnp.zeros((1, width), wide_type)] * 2
    for rows in tiles(length, row_tile):
        grad = normed_grad[rows, :]
        normal, inverse = normalize(summed[rows, :])
        value = norm_backward(grad, normal, inverse, row_of(vectors, 0))
        work[rows, :] = value
        low[rows, :] = value.astype(low_type)
        sums[0] = sums[0] + jnp.sum(grad * normal, axis=0, keepdims=True)
        sums[1] = sums[1] + jnp.sum(grad, axis=0, keepdims=True)
    pair_table = get(3)
    for step in range(2):
        flat[:, step * width : (step + 1) * width] = dot(
            pair_table[:, step * length : (step + 1) * length], low[...]
        ).astype(low_type)
    work[...] += dot(flat[...], get(4)[...])
    small = made[0]
    small[...] = jnp.zeros_like(small)
    if last:
        for rows in tiles(length, row_tile):
            value = work[rows, :] * live_rows(pads_ref, rows, length)
            start = rows.start % half
            target = made[1 + rows.start // half]
            target[start : start + row_tile, :] = value.astype(target.dtype)
    else:
        residual, below = get(5), get(6)
        out_sums = [jnp.zeros((1, width), wide_type)] * 3
        for rows in tiles(length, row_tile):
            grad = work[rows, :] * live_rows(pads_ref, rows, length)
            made[1][rows, :], made[2][rows, :] = out_rows(
                grad, residual[rows, :], row_of(below, 3), out_sums
            )
        sums = sums + out_sums
        done(1, 2)
        own, other = get(7), get(8)
        hiddens = (own.at[0], own.at[1], other.at[0], other.at[1])
        down_grads(hiddens, made[2], made, done, 3, 4)
    for index, value in enumerate(sums):
        small[index : index + 1, :] = value


def mix_back(normed_grad, summed, vectors, tables, pads, below=None, earlier=()):
    pair_table, _, stack_table = tables
    length, width = rows = summed.shape
    loads = [whole(array) for array in (normed_grad, summed, vectors)]
    loads += [part(pair_table, mp_place), whole(stack_table)]
    outs = [((8, width), wide_type)]
    flops = 4 * length * width * (length + width)
    if below is None:
        half = (length // 2, width)
        outs += [(half, wide_type), (half, low_type)]
    else:
        loads += [whole(array) for array in below]
        size = below[2].shape[2]
        outs += [(rows, wide_type), (rows, low_type)] + [((2, size, width), low_type)] * 2
        flops += 8 * length * width * size
    return staged(
        "mix_back",
        functools.partial(mix_back_body, below is None),
        loads,
        outs,
        earlier,
        [
            pltpu.VMEM(rows, low_type),
            pltpu.VMEM((length, 2 * width), low_type),
            pltpu.VMEM(rows, wide_type),
        ],
        flops,
        20,
    )(pads)


def layer_mix(layer_in, live_mask, params, tables):
    gain_mix, shift_mix = params[:2]
    pair_table, wide_table, stack_table = tables
    width = layer_in.shape[1]
    masked = layer_in * live_mask
    spectra = dot(masked.astype(low_type), wide_table).astype(low_type)
    stacked = jnp.concatenate([spectra[:, :width], spectra[:, width:]], axis=0)
    summed = masked + dot(pair_table, stacked)
    normal, inverse = normalize(summed)
    normed = normal * gain_mix + shift_mix
    return summed, normed, normed.astype(low_type)


def layer_hidden(normed_low, up_weight, up_bias):
    return gate_pair(dot(normed_low, up_weight) + up_bias.astype(wide_type))


def layer_out(normed, branch, live_mask, params):
    down_bias, gain_out, shift_out = params[2:]
    residual = normed + branch + down_bias
    out_normal, out_inverse = normalize(residual)
    result = (out_normal * gain_out + shift_out) * live_mask
    return result, residual


def out_backward(result_cot, live_mask, gain_out, residual):
    out_grad = result_cot * live_mask
    out_normal, out_inverse = normalize(residual)
    resid_grad = norm_backward(out_grad, out_normal, out_inverse, gain_out)
    gainout_grad = jnp.sum(out_grad * out_normal, axis=0)
    shiftout_grad = jnp.sum(out_grad, axis=0)
    branch_cot = resid_grad.astype(low_type)
    downbias_grad = jnp.sum(branch_cot, axis=0, dtype=wide_type)
    return resid_grad, branch_cot, (downbias_grad, gainout_grad, shiftout_grad)


def cot_of(branch_cot, down_weight, slope):
    return (dot_nt(branch_cot, down_weight) * slope.astype(wide_type)).astype(low_type)


def mix_backward(normed_grad, live_mask, gain_mix, summed, tables):
    pair_table, wide_table, stack_table = tables
    length = summed.shape[0]
    normal, inverse = normalize(summed)
    summed_grad = norm_backward(normed_grad, normal, inverse, gain_mix)
    gainmix_grad = jnp.sum(normed_grad * normal, axis=0)
    shiftmix_grad = jnp.sum(normed_grad, axis=0)
    summed_low = summed_grad.astype(low_type)
    flat_grad = jnp.concatenate(
        [
            dot(pair_table[:, :length], summed_low).astype(low_type),
            dot(pair_table[:, length:], summed_low).astype(low_type),
        ],
        axis=1,
    )
    masked_grad = (summed_grad + dot(flat_grad, stack_table)) * live_mask
    return masked_grad, (gainmix_grad, shiftmix_grad)


def paired(first, second):
    return dot_tn(*first) + dot_tn(*second)


def core_swap(array):
    return dp_swap(array, dp_bits()[0])


def cut(ref, axis, index):
    return ref.at[(slice(None),) * axis + (index,)]


def moved(name, body, arrays, shapes, scratch, copies, earlier):
    space = pl.BlockSpec(memory_space=pl.ANY if weight[0] > 1 else pltpu.HBM)
    count, late, given = len(arrays), len(earlier), len(shapes)

    def kernel(*refs):
        rest = refs[count + late + given :]
        body(refs[:count], refs[count + late : count + late + given], rest[:-1], rest[-1])

    return pl.pallas_call(
        kernel,
        out_shape=[jax.ShapeDtypeStruct(shape, low_type) for shape in shapes],
        in_specs=[space] * count + [pl.BlockSpec(memory_space=pl.ANY)] * late,
        out_specs=[space] * given,
        cost_estimate=pl.CostEstimate(flops=weight[0], bytes_accessed=1, transcendentals=0),
        scratch_shapes=[pltpu.VMEM(shape, low_type) for shape in scratch]
        + [pltpu.SemaphoreType.DMA((copies,))],
        compiler_params=pltpu.CompilerParams(vmem_limit_bytes=24 * 2**20 if weight[0] > 1 else vmem_bytes),
        name=name,
    )(*arrays, *earlier)


def sum_parts(arrays, views, targets, shapes, part_shape, earlier):
    count, terms = len(views), len(arrays)

    def body(sources, results, held, sems):
        loads = [
            [
                pltpu.make_async_copy(
                    view(source), held[terms * index + side], sems.at[terms * index + side]
                )
                for side, source in enumerate(sources)
            ]
            for index, view in enumerate(views)
        ]
        for group in loads:
            for copy in group:
                copy.start()
        leaving = []
        for index, group in enumerate(loads):
            for copy in group:
                copy.wait()
            rooms = held[terms * index : terms * (index + 1)]
            value = sum(room[...].astype(wide_type) for room in rooms)
            rooms[0][...] = value.astype(low_type)
            leaving.append(
                pltpu.make_async_copy(
                    rooms[0], targets[index](results), sems.at[terms * count + index]
                )
            )
            leaving[-1].start()
        for copy in leaving:
            copy.wait()

    return moved(
        "sum_parts",
        body,
        arrays,
        shapes,
        [part_shape] * (terms * count),
        (terms + 1) * count,
        earlier,
    )


def sum_split(arrays, axis, place, earlier=()):
    shape, count = arrays[0].shape, arrays[0].shape[axis]
    shape = shape[:axis] + shape[axis + 1 :]
    order = [*range(1, count), 0]
    return sum_parts(
        arrays,
        [lambda ref, step=step: cut(ref, axis, place() ^ step) for step in order],
        [lambda refs, step=step: refs[step] for step in order],
        [shape] * count,
        shape,
        earlier,
    )


def sum_whole(arrays, earlier=()):
    shape = arrays[0].shape
    parts = 2 if shape[0] % 2 == 0 and len(shape) > 2 else 1
    size = shape[0] // parts
    spans = [pl.ds(step * size, size) for step in range(parts)]
    return sum_parts(
        arrays,
        [lambda ref, at=at: ref.at[at] for at in spans],
        [lambda refs, at=at: refs[0].at[at] for at in spans],
        [shape],
        (size, *shape[1:]),
        earlier,
    )[0]


def sum_both(first, second, earlier):
    shares, halves, rows, width = first[0].shape
    arrays = (*first, *second)
    jobs = [(kind, half) for half in range(halves) for kind in range(2)]
    part_shape = (shares, rows, width)

    def body(sources, results, held, sems):
        loads = []
        for slot, (kind, half) in enumerate(jobs):
            loads.append(
                [
                    pltpu.make_async_copy(
                        sources[2 * kind + side].at[:, half],
                        held[2 * slot + side],
                        sems.at[2 * slot + side],
                    )
                    for side in range(2)
                ]
            )
            for copy in loads[-1]:
                copy.start()
        leaving = []
        for slot, group in enumerate(loads):
            for copy in group:
                copy.wait()
            left, right = held[2 * slot], held[2 * slot + 1]
            value = left[...].astype(wide_type) + right[...].astype(wide_type)
            left[...] = value.astype(low_type)
            target = results[0].at[:, pl.ds(slot * rows, rows)]
            leaving.append(pltpu.make_async_copy(left, target, sems.at[8 + slot]))
            leaving[-1].start()
        for copy in leaving:
            copy.wait()

    return moved(
        "sum_both",
        body,
        arrays,
        [(shares, 2 * halves * rows, width)],
        [part_shape] * 8,
        12,
        earlier,
    )[0]


def join_parts(arrays, axis, place, earlier=()):
    shape, count = arrays[0].shape, len(arrays)
    whole_shape = shape[:axis] + (count,) + shape[axis:]

    def body(sources, results, held, sems):
        copies = [
            pltpu.make_async_copy(source, room, sems.at[step])
            for step, (source, room) in enumerate(zip(sources, held))
        ]
        for copy in copies:
            copy.start()
        leaving = [
            pltpu.make_async_copy(
                room, cut(results[0], axis, place() ^ step), sems.at[count + step]
            )
            for step, room in enumerate(held)
        ]
        for copy, after in zip(copies, leaving):
            copy.wait()
            after.start()
        for copy in leaving:
            copy.wait()

    return moved(
        "join_parts", body, arrays, [whole_shape], [shape] * count, 2 * count, earlier
    )[0]


def axis_place(axis):
    if axis == "mp":
        return lambda: 0
    if axis == "near":
        return lambda: lax.rem(lax.axis_index("dp") // 2, 2)
    return lambda: lax.axis_index("dp") // 4


def axis_count(axis):
    return lax.axis_size("dp") // 4 if axis == "far" else 2


def axis_swap(array, axis, step):
    if axis == "mp":
        return mp_swap(array)
    return dp_swap(array, (2 if axis == "near" else 4) * step)


class FarTotal:
    def __init__(self, own, received, steps, earlier=()):
        self.axes = ["mp", "far", "near"]
        shape = tuple(axis_count(axis) for axis in self.axes) + (-1, own.shape[-1])
        self.arrays = [own.reshape(shape), received.reshape(shape)]
        self.steps, self.gone = list(steps), []
        self.finish(*earlier)

    def finish(self, *earlier):
        if not self.steps:
            self.total = self.last = sum_whole(self.arrays, earlier)
            return self.last
        name = self.steps.pop(0)
        axis = self.axes.index(name)
        self.axes.pop(axis)
        if name != "mp":
            self.gone.append((name, axis - ("mp" in self.axes)))
        own, *given = sum_split(self.arrays, axis, axis_place(name), earlier)
        self.arrays = [own] + [
            axis_swap(array, name, step + 1) for step, array in enumerate(given)
        ]
        self.last = own
        return own

    def turn(self):
        name, _ = self.gone[-1]
        self.arrays = [self.total] + [
            axis_swap(self.total, name, step) for step in range(1, axis_count(name))
        ]

    def gather(self, *earlier):
        name, axis = self.gone.pop()
        self.total = self.last = join_parts(self.arrays, axis, axis_place(name), earlier)
        if self.gone:
            self.turn()
        else:
            self.total = self.total.reshape(-1, self.total.shape[-1])
        return self.last


def sum_jobs(arrays, jobs, shapes, earlier):
    count = sum(len(sources) for sources, _, _, _ in jobs)

    def body(sources, results, held, sems):
        loads, slot = [], 0
        for views, _, _, _ in jobs:
            loads.append([])
            for index, view in views:
                copy = pltpu.make_async_copy(view(sources[index]), held[slot], sems.at[slot])
                copy.start()
                loads[-1].append((copy, held[slot]))
                slot += 1
        leaving = []
        for place, (group, (_, out, where, _)) in enumerate(zip(loads, jobs)):
            for copy, _ in group:
                copy.wait()
            room = group[0][1]
            value = sum(term[...].astype(wide_type) for _, term in group)
            room[...] = value.astype(low_type)
            leaving.append(
                pltpu.make_async_copy(room, where(results[out]), sems.at[count + place])
            )
            leaving[-1].start()
        for copy in leaving:
            copy.wait()

    scratch = [shape for views, _, _, shape in jobs for _ in views]
    return moved("sum_jobs", body, arrays, shapes, scratch, count + len(jobs), earlier)


def every(ref):
    return ref


class PairTotal:
    def __init__(self, own, received, earlier=()):
        far, width = axis_count("far"), own.shape[-1]
        shape = (2, far, 2, -1, width)
        own, received = own.reshape(shape), received.reshape(shape)
        self.far, self.width, self.half = far, width, own.shape[3] // 2
        top, below = pl.ds(0, self.half), pl.ds(self.half, self.half)
        near = axis_place("near")
        views = (
            lambda ref: ref.at[:, :, near(), top],
            lambda ref: ref.at[:, :, 1 - near(), top],
            lambda ref: ref.at[0, :, :, below],
            lambda ref: ref.at[1, :, :, below],
        )
        shapes = [(2, far, self.half, width)] * 2 + [(far, 2, self.half, width)] * 2
        jobs = [
            ([(0, views[out]), (1, views[out])], out, every, shapes[out]) for out in (1, 3, 0, 2)
        ]
        parts = sum_jobs((own, received), jobs, shapes, earlier)
        self.arrays = (
            parts[0],
            axis_swap(parts[1], "near", 1),
            parts[2],
            mp_swap(parts[3]),
        )
        self.last = parts[0]

    def second(self, *earlier):
        near = axis_place("near")
        views = (
            lambda ref: ref.at[0],
            lambda ref: ref.at[1],
            lambda ref: ref.at[:, near()],
            lambda ref: ref.at[:, 1 - near()],
        )
        shape = (self.far, self.half, self.width)
        jobs = []
        for out in (1, 3, 0, 2):
            first = 2 * (out // 2)
            jobs.append(([(first, views[out]), (first + 1, views[out])], out, every, shape))
        parts = sum_jobs(self.arrays, jobs, [shape] * 4, earlier)
        self.arrays = (
            parts[0],
            mp_swap(parts[1]),
            parts[2],
            axis_swap(parts[3], "near", 1),
        )
        return parts[0]

    def third(self, *earlier):
        place = axis_place("far")
        jobs = []
        for step in (*range(1, self.far), 0):
            for side in range(2):
                jobs.append(
                    (
                        [
                            (2 * side + term, lambda ref, step=step: ref.at[place() ^ step])
                            for term in range(2)
                        ],
                        step,
                        lambda ref, side=side: ref.at[pl.ds(side * self.half, self.half)],
                        (self.half, self.width),
                    )
                )
        shapes = [(2 * self.half, self.width)] * self.far
        own, *given = sum_jobs(self.arrays, jobs, shapes, earlier)
        self.arrays = [own] + [
            axis_swap(array, "far", step + 1) for step, array in enumerate(given)
        ]
        return own


def backward_overlapped(leaving, forward_parts, vectors, tables, blocks, pads, final_out):
    resid, cot, small_out, down_keep, down_send = leaving
    (summed_one, low_one, residual_one, hiddens_one, slopes_one), (summed, low, slopes) = (
        forward_parts
    )
    width = low.shape[1]
    shares = lax.axis_size("dp") // 2
    down_near = core_swap(down_send)
    up_send, total, bias_send = cot_rows(
        cot, low, resid, slopes[1::2], blocks[1][1::2], pads, (), shares
    )
    up_near = core_swap(up_send)
    up_keep, normed_grad, bias_keep = cot_rows(
        cot, low, total, slopes[0::2], blocks[1][0::2], pads, (), shares
    )
    bias_two = (bias_keep, bias_send)
    layer_two = sum_both((down_keep, down_near), (up_keep, up_near), (normed_grad,))
    scattered = lax.psum_scatter(
        layer_two, "dp", scatter_dimension=0, axis_index_groups=core_groups(), tiled=False
    )
    small_mix, resid, cot, down_keep, down_send = mix_back(
        normed_grad,
        summed,
        vectors[1],
        tables,
        pads,
        (residual_one, vectors[0], *hiddens_one),
        (layer_two,),
    )
    down_near = core_swap(down_send)
    up_send, total, bias_send = cot_rows(
        cot, low_one, resid, slopes_one[1::2], blocks[0][1::2], pads
    )
    up_near = core_swap(up_send)
    down_one = FarTotal(down_keep, down_near, ("mp", "far", "near"), (total,))
    up_keep, normed_grad, bias_keep = cot_rows(
        cot, low_one, total, slopes_one[0::2], blocks[0][0::2], pads, (down_one.last,)
    )
    bias_one = (bias_keep, bias_send)
    up_one = PairTotal(up_keep, up_near, (normed_grad,))
    last = down_one.finish(up_one.last)
    small_last, grad_own, grad_given = mix_back(
        normed_grad, summed_one, vectors[0], tables, pads, None, (last,)
    )
    weight[0] = heavy
    last = up_one.second(grad_given)
    small = small_matrix(
        ((small_last, small_mix, *bias_one), (small_mix, small_out, *bias_two)), pads, (last,)
    )
    small_other = mp_swap(small)
    last = down_one.finish(small)
    last = up_one.third(last)
    grad_received = mp_swap(gate(grad_given, last))
    scattered = gate(scattered, last)
    half = scattered.shape[0] // 2
    packed = pack_pieces(
        [[scattered[:half], mp_swap(scattered[half:])], up_one.arrays],
        [small, small_other],
        (last,),
    )
    both = lax.all_gather(packed, "dp", axis=0, tiled=False)
    piece = pack_pieces([down_one.arrays], [], (packed,))
    pieces = [piece] + [axis_swap(piece, "far", step) for step in range(1, axis_count("far"))]
    final_out = place_rows(*final_out, low_type, (piece,))
    input_grad = place_rows(grad_own, grad_received, wide_type, (final_out,))
    joined = join_parts(pieces, 0, axis_place("far"), (input_grad,))
    joined = join_parts([joined, axis_swap(joined, "near", 1)], 1, axis_place("near"))
    joined = joined.reshape(-1, *piece.shape)
    down_one = unpack_pair(joined, core_swap(joined))
    down_two, up_two, up_one, *small = unpack_pieces(both, small.shape[0], (down_one,))
    weight[0] = 1
    return final_out, input_grad, ((up_one, down_one), (up_two, down_two)), small


def backward_plain(grad, live_mask, params, weights, tables, saved):
    large, small, bias = [None] * 2, [None] * 2, [None] * 2
    for level in (1, 0):
        gain_mix, _, _, gain_out, _ = params[level]
        summed, normed_low, residual, kept = saved[level]
        ((up_weight, down_weight),) = weights[level]
        ((hidden, slope),) = kept
        resid_grad, branch_cot, small_out = out_backward(grad, live_mask, gain_out, residual)
        down_grad = dot_tn(hidden, branch_cot).astype(low_type)
        cot = cot_of(branch_cot, down_weight, slope)
        up_grad = dot_tn(normed_low, cot).astype(low_type)
        bias[level] = [jnp.sum(cot, axis=0, dtype=wide_type)]
        grad, small_mix = mix_backward(
            resid_grad + dot_nt(cot, up_weight), live_mask, gain_mix, summed, tables
        )
        small[level] = small_mix + small_out
        large[level] = (total_plain(up_grad, 1), total_plain(down_grad, 0))
    return grad, large, small, bias


def on_device(*arguments):
    inputs, pad_counts = arguments[:2]
    layer_args = (arguments[2:10], arguments[10:18])
    cotangent = arguments[18]
    mp_count = lax.axis_size("mp")
    mine = lax.axis_index("mp")
    feature_width = inputs.shape[2]
    row_length = inputs.shape[1] * mp_count
    cos_seq, sin_seq = fourier_table(row_length)
    pair_full = np.concatenate([cos_seq, -sin_seq], axis=1)
    turned = 1 - 2 * ((np.arange(row_length)[:, None] + np.arange(2 * row_length)[None, :]) % 2)
    if mp_count == 2:
        pair_table = jnp.asarray(np.stack([pair_full, pair_full * turned]), low_type)
    else:
        pair_table = jnp.asarray(pair_full, low_type)
    wide_table = jnp.asarray(np.concatenate(fourier_table(feature_width), axis=1), low_type)
    stack_table = jnp.asarray(np.concatenate(fourier_table(feature_width), axis=0), low_type)
    tables = (pair_table, wide_table, stack_table)
    (up_one, down_one), (up_two, down_two) = [(args[2], args[4]) for args in layer_args]
    biases = jnp.stack([args[3] for args in layer_args])
    if mp_count == 2:
        core, near, far = dp_bits()[:3]
        core_bit = bit_of(core)
        own_rows, up_part, down_part = cut_first(up_one, up_two, down_two)
        own_rows = mp_swap(own_rows)
        given, block, given_cot = cut_next(inputs, cotangent, down_one, (own_rows,))
        up_part, down_part = mp_swap(up_part), mp_swap(down_part)
        received = mp_swap(given)
        far_rows = lax.all_gather(own_rows, "dp", axis=0, tiled=False)
        up_part = fetch_join(up_part, far)
        down_part = fetch_join(down_part, near)
        down_first = mp_swap(gate(block, received))
        other_biases = mp_swap(biases)
        vectors = []
        for level in range(2):
            args = layer_args[level]
            members = [args[0], args[1], args[5], args[6], args[7]]
            members += [
                take_block(array[level], (core_bit + flip) % 2)
                for array in (biases, other_biases)
                for flip in range(2)
            ]
            vectors.append(select_rows(members, 16))
        own_blocks = [
            [own_block(up, down, flip) for flip in range(2)]
            for up, down in ((up_one, down_one), (up_two, down_two))
        ]
        summed_one, normed, low_one, partial, hidden_a, slope_a = enter(
            inputs, received, tables, vectors[0], own_blocks[0], pad_counts
        )
        up_part = fetch_join(gate(up_part, low_one), near)
        down_part = fetch_join(gate(down_part, low_one), far)
        up_near, down_near = core_swap(up_part), core_swap(down_part)
        received_cot = mp_swap(gate(given_cot, down_part))
        down_second = core_swap(down_first)
        far_blocks = [
            (far_columns(far_rows, flip), whole(array))
            for flip, array in enumerate((down_first, down_second))
        ]
        hidden_b, slope_b, residual_one, summed, normed, low, partial, hidden_c, slope_c = middle(
            low_one,
            normed,
            partial,
            tables,
            vectors,
            far_blocks,
            own_blocks[1],
            pad_counts,
        )
        late_blocks = [(whole(up_part), whole(down_part)), (whole(up_near), whole(down_near))]
        out_own, out_given, resid, cot, small_out, slope_d, down_keep, down_send = leave(
            low,
            normed,
            partial,
            vectors[1],
            late_blocks,
            cotangent,
            received_cot,
            hidden_c,
            pad_counts,
        )
        blocks = [own_blocks[0] + far_blocks, own_blocks[1] + late_blocks]
        slopes_one, slopes_two = (
            [part(array, lambda at=at: at) for array in arrays for at in (0, 1)]
            for arrays in ((slope_a, slope_b), (slope_c, slope_d))
        )
        out_received = mp_swap(out_given)
        final_out = (out_own, out_received)
        final_out, input_grad, large, small = backward_overlapped(
            (resid, cot, small_out, down_keep, down_send),
            (
                (summed_one, low_one, residual_one, (hidden_a, hidden_b), slopes_one),
                (summed, low, slopes_two),
            ),
            vectors,
            tables,
            blocks,
            pad_counts,
            final_out,
        )
    else:
        params = [
            tuple(args[step].astype(wide_type) for step in (0, 1, 5, 6, 7)) for args in layer_args
        ]
        position = jnp.arange(row_length, dtype=jnp.int32)
        pads = lax.dynamic_index_in_dim(pad_counts, mine, 0, False)
        live_mask = (position < row_length - pads).astype(wide_type)[:, None]
        weights, saved = [], []
        biases = lax.all_gather(biases, "mp", axis=1, tiled=True)
        current = gathered_row(inputs).astype(wide_type)
        for level, (up_weight, down_weight) in enumerate(((up_one, down_one), (up_two, down_two))):
            up_weight = lax.all_gather(up_weight, "mp", axis=1, tiled=True)
            down_weight = lax.all_gather(down_weight, "mp", axis=0, tiled=True)
            weights.append(((up_weight, down_weight),))
            summed, normed, normed_low = layer_mix(current, live_mask, params[level], tables)
            kept = layer_hidden(normed_low, up_weight, biases[level])
            current, residual = layer_out(
                normed, dot(kept[0], down_weight), live_mask, params[level]
            )
            saved.append((summed, normed_low, residual, (kept,)))
        grad = gathered_row(cotangent).astype(wide_type)
        final_out = return_rows(current.astype(low_type))
        grad, large, small, bias = backward_plain(grad, live_mask, params, weights, tables, saved)
        input_grad = return_rows(grad.astype(low_type)).astype(wide_type)
    hidden_own = layer_args[0][3].shape[0]
    if mp_count != 2:
        rows = []
        for level in range(2):
            rows.extend(small[level])
            rows.extend(bias[level][0].reshape(-1, feature_width))
        total = total_small(select_rows(rows, 8 * -(-len(rows) // 8)))
        count, small = len(rows) // 2, []
        for level in range(2):
            block = total[level * count : (level + 1) * count]
            small += [block[step] for step in range(5)]
            small.append(
                lax.dynamic_slice_in_dim(block[5:].reshape(-1), mine * hidden_own, hidden_own, 0)
            )
    results = [final_out, input_grad]
    for level in range(2):
        gainmix, shiftmix, downbias, gainout, shiftout, bias_total = small[6 * level : 6 * level + 6]
        up_total, down_total = large[level]
        results += [gainmix, shiftmix, up_total, bias_total, down_total, downbias, gainout, shiftout]
    return tuple(results)


def solution(mesh):
    layer_specs = (P(), P(), P(None, "mp"), P("mp"), P("mp", None), P(), P(), P())
    rows = P("dp", "mp", None)
    return jax.shard_map(
        on_device,
        mesh=mesh,
        in_specs=(rows, P("dp"), *layer_specs, *layer_specs, rows),
        out_specs=(rows, rows, *layer_specs, *layer_specs),
        check_vma=False,
    )
```

```python
import functools
import math

import jax
import jax.numpy as jnp
import numpy as np
from jax import lax
from jax.experimental import pallas as pl
from jax.experimental.pallas import tpu as pltpu
from jax.sharding import PartitionSpec as P

norm_eps = 1e-05
low_type = jnp.bfloat16
wide_type = jnp.float32
vmem_bytes = 62 * 2**20
window = 4
heavy = 6 * 10**10
weight = [1]


def fourier_table(points):
    indices = np.arange(points, dtype=np.int64)
    phases = (indices[:, None] * indices[None, :]) % points
    angles = phases.astype(np.float32) * np.float32(2.0 * math.pi / points)
    factor = np.float32(points ** (-0.5))
    return (np.cos(angles) * factor, np.sin(angles) * factor)


def dot(left, right):
    return jnp.dot(left, right, preferred_element_type=wide_type)


def dot_tn(left, right):
    return lax.dot_general(left, right, (((0,), (0,)), ((), ())), preferred_element_type=wide_type)


def dot_nt(left, right):
    return lax.dot_general(left, right, (((1,), (1,)), ((), ())), preferred_element_type=wide_type)


def normalize(activity):
    center = jnp.mean(activity, axis=-1, keepdims=True)
    centered = activity - center
    spread = jnp.mean(centered * centered, axis=-1, keepdims=True)
    inverse = lax.rsqrt(spread + norm_eps)
    return centered * inverse, inverse


def norm_backward(grad, normal, inverse, gain):
    pulled = grad * gain
    first = jnp.mean(pulled, axis=-1, keepdims=True)
    second = jnp.mean(pulled * normal, axis=-1, keepdims=True)
    return inverse * (pulled - first - normal * second)


def gate_pair(preact):
    scale = math.sqrt(2.0 / math.pi)
    square = preact * preact
    turn = jnp.tanh(preact * (scale + (0.044715 * scale) * square))
    half = 0.5 + 0.5 * turn
    hidden = preact * half
    slope = half + hidden * (1.0 - turn) * (scale + (3 * 0.044715 * scale) * square)
    return hidden.astype(low_type), slope.astype(low_type)


def flip_pairs(size, bit):
    return [(index, index ^ bit) for index in range(size)]


def order_halves(bit_value, mine, theirs, axis=0):
    return jnp.where(
        bit_value == 0,
        jnp.concatenate([mine, theirs], axis=axis),
        jnp.concatenate([theirs, mine], axis=axis),
    )


def take_block(array, which, count=2, axis=0):
    size = array.shape[axis] // count
    return lax.dynamic_slice_in_dim(array, which * size, size, axis)


def dp_bits():
    return [1 << level for level in range(lax.axis_size("dp").bit_length() - 1)]


def bit_of(bit):
    return (lax.axis_index("dp") // bit) % 2


def dp_swap(array, bit):
    return lax.ppermute(array, "dp", flip_pairs(lax.axis_size("dp"), bit))


def mp_swap(array):
    return lax.ppermute(array, "mp", [(0, 1), (1, 0)])


def add_low(left, right):
    return (left.astype(wide_type) + right.astype(wide_type)).astype(low_type)


def gate(value, *earlier):
    def kernel(*refs):
        pass

    anywhere = pl.BlockSpec(memory_space=pl.ANY)
    return pl.pallas_call(
        kernel,
        out_shape=jax.ShapeDtypeStruct(value.shape, value.dtype),
        in_specs=[anywhere] * (1 + len(earlier)),
        out_specs=anywhere,
        input_output_aliases={0: 0},
        name="gate",
    )(value, *earlier)


def fetch_join(piece, bit):
    return order_halves(bit_of(bit), piece, dp_swap(piece, bit))


def bounce(name, jobs, shapes, arrays, earlier=()):
    count, late, given = len(arrays), len(earlier), len(shapes)

    def kernel(*refs):
        targets = refs[count + late : count + late + given]
        held, sems = refs[count + late + given : -1], refs[-1]
        work = jobs(refs[:count], held)
        copies = [
            pltpu.make_async_copy(source, target, sems.at[given + index])
            for index, (_, source, target) in enumerate(work)
        ]
        for copy in copies:
            copy.start()
        leaving = [
            pltpu.make_async_copy(source, target, sems.at[index])
            for index, (source, target) in enumerate(zip(held, targets))
        ]
        for slot in range(given):
            for (place, _, _), copy in zip(work, copies):
                if place == slot:
                    copy.wait()
            leaving[slot].start()
        for copy in leaving:
            copy.wait()

    space = pl.BlockSpec(memory_space=pltpu.HBM)
    return pl.pallas_call(
        kernel,
        out_shape=[jax.ShapeDtypeStruct(shape, low_type) for shape in shapes],
        in_specs=[space] * count + [pl.BlockSpec(memory_space=pl.ANY)] * late,
        out_specs=[space] * given,
        scratch_shapes=[pltpu.VMEM(shape, low_type) for shape in shapes]
        + [pltpu.SemaphoreType.DMA((4 * given,))],
        compiler_params=pltpu.CompilerParams(vmem_limit_bytes=vmem_bytes),
        name=name,
    )(*arrays, *earlier)


def span(index, count):
    return pl.ds(pl.multiple_of(index * count, count), count)


def cut_first(up_one, up_two, down_two):
    width, size = up_one.shape[0], up_one.shape[1] // 2
    rows = width // lax.axis_size("dp")
    quarter = (width // 4, size // 4)

    def jobs(sources, held):
        place, core = lax.axis_index("dp"), core_place()
        near, away = lax.rem(place // 2, 2), lax.rem(place // 4, 2)
        own = sources[0].at[span(place, rows)]
        return [
            (0, own.at[:, pl.ds(0, size)], held[0].at[pl.ds(0, rows)]),
            (0, own.at[:, pl.ds(size, size)], held[0].at[pl.ds(rows, rows)]),
            (1, sources[1].at[span(2 * near + away, quarter[0]), span(core, size)], held[1]),
            (2, sources[2].at[span(core * 4 + 2 * away + near, quarter[1])], held[2]),
        ]

    shapes = ((2 * rows, size), (quarter[0], size), (quarter[1], width))
    return bounce("cut_first", jobs, shapes, (up_one, up_two, down_two))


def cut_next(inputs, cotangent, down_one, earlier):
    length, width = cotangent.shape[1:]
    size = down_one.shape[0] // 2

    def jobs(sources, held):
        rows, cots, down = sources
        return [
            (0, rows.at[1 - mp_place()], held[0]),
            (1, down.at[span(core_place(), size)], held[1]),
            (2, cots.at[1 - mp_place()], held[2]),
        ]

    shapes = ((length, width), (size, width), (length, width))
    return bounce("cut_next", jobs, shapes, (inputs, cotangent, down_one), earlier)


def select_rows(rows, count):
    index = lax.broadcasted_iota(jnp.int32, (count, rows[0].shape[0]), 0)
    total = jnp.zeros(index.shape, wide_type)
    for place, row in enumerate(rows):
        total = jnp.where(index == place, row.astype(wide_type)[None], total)
    return total


def core_groups():
    return [
        [place for place in range(lax.axis_size("dp")) if place % 2 == which] for which in (0, 1)
    ]


def total_plain(part, hidden_axis):
    own = lax.psum_scatter(part, "mp", scatter_dimension=hidden_axis, tiled=True)
    return lax.psum(own, "dp").astype(wide_type)


def total_small(vector):
    for bit in dp_bits():
        vector = vector + dp_swap(vector, bit)
    if lax.axis_size("mp") == 2:
        return vector + mp_swap(vector)
    return lax.psum(vector, "mp")


def given_row(array):
    return lax.dynamic_index_in_dim(array, 1 - lax.axis_index("mp"), 0, keepdims=False)


def gathered_row(array):
    return lax.all_to_all(array, "mp", split_axis=0, concat_axis=1, tiled=True)[0]


def return_rows(array):
    return lax.all_to_all(array[None], "mp", split_axis=1, concat_axis=0, tiled=True)


def staged(name, body, loads, outs, earlier=(), scratch=(), flops=0, stress=0):
    count, late, given = len(loads), len(earlier), len(outs)

    def kernel(*refs):
        sources = refs[1 : 1 + count]
        targets = refs[1 + count + late : 1 + count + late + given]
        rest = refs[1 + count + late + given :]
        held, made = rest[:count], rest[count : count + given]
        in_sems, out_sems, *extra = rest[count + given :]
        copies, begun, sent = {}, set(), []
        for index, load in enumerate(loads):
            view = load[2](sources[index])
            copies[index] = pltpu.make_async_copy(view, held[index], in_sems.at[index])
        queue = sorted(range(count), key=lambda index: math.prod(loads[index][1]) > 2**16)

        def begin(index):
            if index not in begun:
                copies[index].start()
                begun.add(index)

        def get(index):
            begin(index)
            if index in copies:
                copies.pop(index).wait()
                while sum(place in copies for place in begun) < window and len(begun) < count:
                    begin(next(place for place in queue if place not in begun))
            return held[index]

        for index in queue:
            if math.prod(loads[index][1]) <= 2**16 or len(begun) < window:
                begin(index)

        def done(*indices):
            for index in indices:
                slot = len(sent)
                if isinstance(index, tuple):
                    index, place = index
                    source, target = made[index].at[place], targets[index].at[place]
                else:
                    source, target = made[index], targets[index]
                copy = pltpu.make_async_copy(source, target, out_sems.at[slot])
                copy.start()
                sent.append((index, copy))

        body(get, made, done, extra, refs[0])
        for index in list(copies):
            get(index)
        left = {index for index, _ in sent}
        done(*[index for index in range(given) if index not in left])
        for _, copy in sent:
            copy.wait()

    space = pl.BlockSpec(memory_space=pltpu.HBM)
    moved = sum(math.prod(load[1]) * load[0].dtype.itemsize for load in loads)
    moved += sum(math.prod(out[0]) * jnp.dtype(out[1]).itemsize for out in outs)
    call = pl.pallas_call(
        kernel,
        out_shape=[jax.ShapeDtypeStruct(*out) for out in outs],
        in_specs=[pl.BlockSpec(memory_space=pltpu.SMEM)]
        + [space] * count
        + [pl.BlockSpec(memory_space=pl.ANY)] * late,
        out_specs=[space] * given,
        cost_estimate=pl.CostEstimate(
            flops=1 + stress * flops, bytes_accessed=1 + stress * moved, transcendentals=0
        ),
        scratch_shapes=[pltpu.VMEM(load[1], load[0].dtype) for load in loads]
        + [pltpu.VMEM(*out) for out in outs]
        + [pltpu.SemaphoreType.DMA((count,)), pltpu.SemaphoreType.DMA((2 * given,))]
        + list(scratch),
        compiler_params=pltpu.CompilerParams(vmem_limit_bytes=vmem_bytes),
        name=name,
    )
    return lambda pads: call(pads, *[load[0] for load in loads], *earlier)


def whole(array):
    return (array, array.shape, lambda ref: ref)


def part(array, index):
    return (array, array.shape[1:], lambda ref: ref.at[index()])


def mp_place():
    return lax.axis_index("mp")


def core_place():
    return lax.rem(lax.axis_index("dp"), 2)


def share(flip):
    return (core_place() + flip) % 2


def own_block(up_weight, down_weight, flip):
    width, size = up_weight.shape[0], up_weight.shape[1] // 2

    def span():
        return pl.ds(pl.multiple_of(share(flip) * size, size), size)

    return (
        (up_weight, (width, size), lambda ref: ref.at[:, span()]),
        (down_weight, (size, width), lambda ref: ref.at[span()]),
    )


def far_columns(pieces, flip):
    places, rows, size = pieces.shape
    half = rows // 2
    return (
        pieces,
        (places, half, size),
        lambda ref: ref.at[:, pl.ds(pl.multiple_of(share(flip) * half, half), half)],
    )


def matrix(ref):
    return ref[...].reshape(-1, ref.shape[-1])


def tiles(total, size):
    return [slice(start, start + size) for start in range(0, total, size)]


def live_rows(pads_ref, rows, length):
    place = lax.broadcasted_iota(jnp.int32, (rows.stop - rows.start, 1), 0) + rows.start
    place = lax.rem(place + mp_place() * (length // 2), length)
    return (place < length - pads_ref[mp_place()]).astype(wide_type)


def row_of(ref, index):
    return ref[index : index + 1, :]


row_tile = 128


def mix_rows(summed, normed, low, spectra, wide_table, pair_table, vectors):
    length, width = summed.shape
    low[...] = summed[...].astype(low_type)
    wide = wide_table()
    for columns in tiles(2 * width, width):
        spectra[:, columns] = dot(low[...], wide[:, columns]).astype(low_type)
    pair = pair_table()
    summed[...] += dot(pair[:, :length], spectra[:, :width])
    summed[...] += dot(pair[:, length:], spectra[:, width:])
    for rows in tiles(length, row_tile):
        normal, _ = normalize(summed[rows, :])
        value = normal * row_of(vectors, 0) + row_of(vectors, 1)
        normed[rows, :] = value
        low[rows, :] = value.astype(low_type)


def feed_block(low, up_weight, bias, down_weight, hidden, slope):
    hidden[...], slope[...] = gate_pair(dot(low[...], matrix(up_weight())) + bias)
    return dot(hidden[...], matrix(down_weight()))


def out_norm(residual, normed, parts, vectors):
    for rows in tiles(residual.shape[0], row_tile):
        value = normed[rows, :]
        for item in parts:
            value = value + item[rows, :]
        value = value + row_of(vectors, 2)
        residual[rows, :] = value
        normal, _ = normalize(value)
        yield rows, normal * row_of(vectors, 3) + row_of(vectors, 4)


def enter_body(get, made, done, extra, pads_ref):
    summed, normed, low, partial, hidden, slope = made
    (spectra,) = extra
    length, width = summed.shape
    half = length // 2
    for rows in tiles(length, row_tile):
        start = rows.start % half
        piece = get(rows.start // half)[start : start + row_tile, :].astype(wide_type)
        summed[rows, :] = piece * live_rows(pads_ref, rows, length)
    vectors = get(4)
    mix_rows(summed, normed, low, spectra, lambda: get(2), lambda: get(3), vectors)
    done(0, 1, 2)
    for block in range(2):
        value = feed_block(
            low,
            lambda: get(5 + 2 * block),
            row_of(vectors, 5 + block),
            lambda: get(6 + 2 * block),
            hidden.at[block],
            slope.at[block],
        )
        done((4, block), (5, block))
        partial[...] = value if block == 0 else partial[...] + value


def enter(inputs, received, tables, vectors, blocks, pads):
    pair_table, wide_table, _ = tables
    length, width = 2 * received.shape[0], received.shape[1]
    size = blocks[0][0][1][1]
    loads = [part(inputs, mp_place), whole(received), whole(wide_table)]
    loads += [part(pair_table, mp_place), whole(vectors), *blocks[0], *blocks[1]]
    rows = (length, width)
    return staged(
        "enter",
        enter_body,
        loads,
        [(rows, wide_type), (rows, wide_type), (rows, low_type), (rows, wide_type)]
        + [((2, length, size), low_type)] * 2,
        (),
        [pltpu.VMEM((length, 2 * width), low_type)],
        4 * length * width * (length + width + 2 * size),
    )(pads)


def middle_body(get, made, done, extra, pads_ref):
    hidden, slope, residual, summed, normed, low, partial, hidden_two, slope_two = made
    spectra, total = extra
    length = summed.shape[0]
    low_one, vectors = get(0), get(5)
    for block in range(2):
        value = feed_block(
            low_one,
            lambda: get(1 + 2 * block),
            row_of(vectors, 7 + block),
            lambda: get(2 + 2 * block),
            hidden.at[block],
            slope.at[block],
        )
        done((0, block), (1, block))
        total[...] = value if block == 0 else total[...] + value
    for rows, value in out_norm(residual, get(6), (total, get(7)), vectors):
        summed[rows, :] = value * live_rows(pads_ref, rows, length)
    done(2)
    vectors = get(10)
    mix_rows(summed, normed, low, spectra, lambda: get(8), lambda: get(9), vectors)
    done(3, 4, 5)
    for block in range(2):
        value = feed_block(
            low,
            lambda: get(11 + 2 * block),
            row_of(vectors, 5 + block),
            lambda: get(12 + 2 * block),
            hidden_two.at[block],
            slope_two.at[block],
        )
        done((7, block), (8, block))
        partial[...] = value if block == 0 else partial[...] + value


def middle(low, normed, partial, tables, vectors, far_blocks, own_blocks, pads, earlier=()):
    pair_table, wide_table, _ = tables
    length, width = rows = low.shape
    size = own_blocks[0][0][1][1]
    loads = [whole(low), *far_blocks[0], *far_blocks[1], whole(vectors[0])]
    loads += [whole(normed), whole(partial), whole(wide_table), part(pair_table, mp_place)]
    loads += [whole(vectors[1]), *own_blocks[0], *own_blocks[1]]
    hidden = ((2, length, size), low_type)
    return staged(
        "middle",
        middle_body,
        loads,
        [hidden, hidden, (rows, wide_type), (rows, wide_type), (rows, wide_type)]
        + [(rows, low_type), (rows, wide_type), hidden, hidden],
        earlier,
        [pltpu.VMEM((length, 2 * width), low_type), pltpu.VMEM(rows, wide_type)],
        4 * length * width * (length + width + 4 * size),
    )(pads)


def down_grads(hiddens, cot, made, done, keep, send):
    for step, index in ((1, send), (0, keep)):
        target = made[index]
        for half in range(2):
            value = dot_tn(hiddens[2 * half + step][...], cot[...]).astype(low_type)
            if len(target.shape) == 4:
                target[:, half] = value.reshape(target.shape[0], *target.shape[2:])
                place = (slice(None), half)
            else:
                target[half] = value
                place = half
            done((index, place))


def leave_body(get, made, done, extra, pads_ref):
    out_own, out_given, resid, cot, small, slope, keep, send = made
    hidden, total, residual = extra
    length, width = resid.shape
    half = length // 2
    low, vectors = get(0), get(5)
    for block in range(2):
        value = feed_block(
            low,
            lambda: get(1 + 2 * block),
            row_of(vectors, 7 + block),
            lambda: get(2 + 2 * block),
            hidden.at[block],
            slope.at[block],
        )
        done((5, block))
        total[...] = value if block == 0 else total[...] + value
    sums = [jnp.zeros((1, width), wide_type)] * 3
    for rows, value in out_norm(residual, get(6), (total, get(7)), vectors):
        live = live_rows(pads_ref, rows, length)
        start = rows.start % half
        target = (out_own, out_given)[rows.start // half]
        target[start : start + row_tile, :] = (value * live).astype(low_type)
        grad = get(8 + rows.start // half)[start : start + row_tile, :].astype(wide_type) * live
        resid[rows, :], cot[rows, :] = out_rows(grad, residual[rows, :], row_of(vectors, 3), sums)
    small[...] = jnp.zeros_like(small)
    for index, value in enumerate(sums):
        small[index : index + 1, :] = value
    done(0, 1, 2, 3, 4)
    own = get(10)
    down_grads((own.at[0], own.at[1], hidden.at[0], hidden.at[1]), cot, made, done, 6, 7)


def leave(low, normed, partial, vectors, blocks, cotangent, received, hidden, pads, earlier=()):
    length, width = rows = low.shape
    size = hidden.shape[2]
    shares = lax.axis_size("dp") // 2
    loads = [whole(low), *blocks[0], *blocks[1], whole(vectors), whole(normed), whole(partial)]
    loads += [part(cotangent, mp_place), whole(received), whole(hidden)]
    half, grads = (length // 2, width), ((shares, 2, size // shares, width), low_type)
    return staged(
        "leave",
        leave_body,
        loads,
        [(half, low_type), (half, low_type), (rows, wide_type), (rows, low_type)]
        + [((8, width), wide_type), ((2, length, size), low_type), grads, grads],
        earlier,
        [pltpu.VMEM((2, length, size), low_type)] + [pltpu.VMEM(rows, wide_type)] * 2,
        16 * length * width * size,
    )(pads)


def out_rows(grad, residual, gain, sums):
    normal, inverse = normalize(residual)
    resid_grad = norm_backward(grad, normal, inverse, gain)
    low = resid_grad.astype(low_type)
    parts = (grad * normal, grad, low.astype(wide_type))
    for index, value in enumerate(parts):
        sums[index] = sums[index] + jnp.sum(value, axis=0, keepdims=True)
    return resid_grad, low


def cot_body(get, made, done, extra, pads_ref):
    grads, total, small = made
    (cots,) = extra
    branch_cot = get(0)
    small[...] = jnp.zeros_like(small)
    places = ((1, 2, 5), (6, 7, 8))
    for half in range(2):
        down_weight, slope, up_weight = places[half]
        value = dot_nt(branch_cot[...], matrix(get(down_weight)))
        value = (value * get(slope)[...].astype(wide_type)).astype(low_type)
        cots[...] = value
        small[half : half + 1, :] = jnp.sum(value.astype(wide_type), axis=0, keepdims=True)
        value = dot_tn(get(3)[...], cots[...]).astype(low_type)
        if len(grads.shape) == 4:
            grads[:, half] = value.reshape(grads.shape[0], *grads.shape[2:])
            done((0, (slice(None), half)))
        else:
            grads[half] = value
            done((0, half))
        before, up_weight = (get(4) if half == 0 else total), get(up_weight)
        count = 1 + half
        for rows in tiles(total.shape[0], total.shape[0] // count):
            total[rows, :] = before[rows, :] + dot_nt(cots[rows, :], matrix(up_weight))
            if half:
                done((1, pl.ds(rows.start, rows.stop - rows.start)))


def cot_rows(branch_cot, low, before, slopes, blocks, pads, earlier=(), shares=0):
    length, width = rows = low.shape
    (up_a, down_a), (up_b, down_b) = blocks
    loads = [whole(branch_cot), down_a, slopes[0], whole(low), whole(before), up_a]
    loads += [down_b, slopes[1], up_b]
    size = slopes[0][1][1]
    return staged(
        "cot_rows",
        cot_body,
        loads,
        [
            ((shares, 2, width // shares, size) if shares else (2, width, size), low_type),
            (rows, wide_type),
            ((8, size), wide_type),
        ],
        earlier,
        [pltpu.VMEM((length, size), low_type)],
        12 * length * width * size,
        20,
    )(pads)


def small_body(get, made, done, extra, pads_ref):
    total = made[0]
    width = total.shape[1]
    index = lax.broadcasted_iota(jnp.int32, (4, 1), 0)
    for level in range(2):
        mix, out, *biases = (get(4 * level + step) for step in range(4))
        start = 9 * level
        total[start : start + 2, :] = mix[0:2, :]
        first = 0 if level else 2
        total[start + 2 : start + 3, :] = out[first + 2 : first + 3, :]
        total[start + 3 : start + 5, :] = out[first : first + 2, :]
        rows = jnp.zeros((4, width), wide_type)
        for block in range(4):
            half = (mp_place() + block // 2) % 2
            rows = rows + jnp.where(
                index == 2 * half + share(block % 2),
                biases[block % 2][block // 2 : block // 2 + 1, :],
                0.0,
            )
        total[start + 5 : start + 9, :] = rows
    total[18:, :] = jnp.zeros((total.shape[0] - 18, width), wide_type)


def small_matrix(parts, pads, earlier=()):
    loads = [whole(array) for level in parts for array in level]
    width = parts[0][0].shape[1]
    outs = [((32, width), wide_type)]
    return staged("small_matrix", small_body, loads, outs, earlier)(pads)[0]


def pack_pieces(groups, smalls, earlier):
    arrays = [array for group in groups for array in group]
    width = arrays[0].shape[1]
    heights = [group[0].shape[0] for group in groups]
    small_rows = smalls[0].shape[0] if smalls else 0
    count, late = len(arrays), len(earlier)
    size = sum(heights) + 2 * small_rows

    def kernel(*refs):
        sources, small_refs = refs[:count], refs[count : count + len(smalls)]
        target, packed, *held = refs[count + len(smalls) + late : -1]
        sems = refs[-1]
        copies = [
            pltpu.make_async_copy(source, room, sems.at[index])
            for index, (source, room) in enumerate(zip((*sources, *small_refs), held))
        ]
        for copy in copies:
            copy.start()
        leaving, first = [], 0
        for place, group in enumerate(groups):
            span = slice(sum(heights[:place]), sum(heights[: place + 1]))
            value = 0.0
            for index in range(first, first + len(group)):
                copies[index].wait()
                value = value + held[index][...].astype(wide_type)
            packed[span, :] = value.astype(low_type)
            first += len(group)
        if smalls:
            for copy in copies[count:]:
                copy.wait()
            total = held[count][...] + held[count + 1][...]
            high = total.astype(low_type)
            start = sum(heights)
            packed[start : start + small_rows, :] = high
            packed[start + small_rows :, :] = (total - high.astype(wide_type)).astype(low_type)
        copy = pltpu.make_async_copy(packed, target, sems.at[count + 2])
        copy.start()
        copy.wait()

    space = pl.BlockSpec(memory_space=pl.ANY)
    return pl.pallas_call(
        kernel,
        out_shape=jax.ShapeDtypeStruct((size, width), low_type),
        in_specs=[space] * (count + len(smalls)) + [pl.BlockSpec(memory_space=pl.ANY)] * late,
        out_specs=space,
        scratch_shapes=[pltpu.VMEM((size, width), low_type)]
        + [pltpu.VMEM(array.shape, low_type) for array in arrays]
        + [pltpu.VMEM((small_rows, width), wide_type) for _ in smalls]
        + [pltpu.SemaphoreType.DMA((count + 3,))],
        compiler_params=pltpu.CompilerParams(vmem_limit_bytes=24 * 2**20),
        cost_estimate=pl.CostEstimate(flops=weight[0], bytes_accessed=1, transcendentals=0),
        name="pack_pieces",
    )(*arrays, *smalls, *earlier)


def unpack_pair(mine, theirs):
    shares, rows, width = mine.shape
    size = shares * rows

    def kernel(own, near, down, low, held, sems):
        copies = [
            pltpu.make_async_copy(source, low.at[side], sems.at[side])
            for side, source in enumerate((own, near))
        ]
        for copy in copies:
            copy.start()
        leaving = []
        for side in range(2):
            copies[side].wait()
            held[side] = low[side].reshape(size, width).astype(wide_type)
            where = down.at[pl.ds(pl.multiple_of(share(side) * size, size), size)]
            leaving.append(pltpu.make_async_copy(held.at[side], where, sems.at[2 + side]))
            leaving[-1].start()
        for copy in leaving:
            copy.wait()

    return pl.pallas_call(
        kernel,
        out_shape=jax.ShapeDtypeStruct((2 * size, width), wide_type),
        in_specs=[pl.BlockSpec(memory_space=pl.ANY)] * 2,
        out_specs=pl.BlockSpec(memory_space=pltpu.HBM),
        scratch_shapes=[
            pltpu.VMEM((2, shares, rows, width), low_type),
            pltpu.VMEM((2, size, width), wide_type),
            pltpu.SemaphoreType.DMA((4,)),
        ],
        compiler_params=pltpu.CompilerParams(vmem_limit_bytes=24 * 2**20),
        cost_estimate=pl.CostEstimate(flops=weight[0], bytes_accessed=1, transcendentals=0),
        name="unpack_pair",
    )(mine, theirs)


def unpack_pieces(gathered, small_rows, earlier):
    shares, width = gathered.shape[0] // 2, gathered.shape[2]
    rising = (False, True, True)
    kinds = len(rising)
    rows = (gathered.shape[1] - 2 * small_rows) // kinds
    size = shares * rows
    pieces = gathered.reshape(shares, 2, -1, width)

    def kernel(source, *refs):
        refs = refs[len(earlier) :]
        targets, results = refs[:kinds], refs[kinds : kinds + 12]
        low, held, small, sems = refs[kinds + 12 :]
        jobs = [(kind, core) for kind in range(kinds) for core in range(2)]
        copies = [
            pltpu.make_async_copy(
                source.at[:, core, pl.ds(kind * rows, rows)], low.at[slot], sems.at[slot]
            )
            for slot, (kind, core) in enumerate(jobs)
        ]
        copies.append(
            pltpu.make_async_copy(
                source.at[:, :, pl.ds(kinds * rows, 2 * small_rows)], small, sems.at[4 * kinds]
            )
        )
        for copy in copies:
            copy.start()
        leaving = []
        for slot, (kind, core) in enumerate(jobs):
            copies[slot].wait()
            held[slot] = low[slot].reshape(size, width).astype(wide_type)
            if rising[kind]:
                where = targets[kind].at[:, pl.ds(core * width, width)]
            else:
                where = targets[kind].at[pl.ds(core * size, size)]
            leaving.append(pltpu.make_async_copy(held.at[slot], where, sems.at[2 * kinds + slot]))
            leaving[-1].start()
        copies[-1].wait()
        total = jnp.zeros((2 * small_rows, width), wide_type)
        for place in range(shares):
            for core in range(2):
                total = total + small[place, core].astype(wide_type)
        total = total[:small_rows] + total[small_rows:]
        for level in range(2):
            start = 9 * level
            for step in range(5):
                results[6 * level + step][...] = total[start + step]
            for step in range(2):
                own = jnp.where(
                    mp_place() == 0, total[start + 5 + step], total[start + 7 + step]
                )
                results[6 * level + 5][step * width : (step + 1) * width] = own
        for copy in leaving:
            copy.wait()

    space, inside = pl.BlockSpec(memory_space=pltpu.HBM), pl.BlockSpec(memory_space=pltpu.VMEM)
    shapes = [(size, 2 * width) if up else (2 * size, width) for up in rising]
    shapes += ([(width,)] * 5 + [(2 * width,)]) * 2
    return pl.pallas_call(
        kernel,
        out_shape=[jax.ShapeDtypeStruct(shape, wide_type) for shape in shapes],
        in_specs=[space] + [pl.BlockSpec(memory_space=pl.ANY)] * len(earlier),
        out_specs=[space] * kinds + [inside] * 12,
        scratch_shapes=[
            pltpu.VMEM((2 * kinds, shares, rows, width), low_type),
            pltpu.VMEM((2 * kinds, size, width), wide_type),
            pltpu.VMEM((shares, 2, 2 * small_rows, width), low_type),
            pltpu.SemaphoreType.DMA((4 * kinds + 1,)),
        ],
        compiler_params=pltpu.CompilerParams(vmem_limit_bytes=vmem_bytes),
        cost_estimate=pl.CostEstimate(flops=weight[0], bytes_accessed=1, transcendentals=0),
        name="unpack_pieces",
    )(pieces, *earlier)


def place_rows(own, received, kind, earlier=()):
    length, width = own.shape

    def kernel(mine, theirs, *refs):
        target, low_mine, low_theirs, first, second, sems = refs[len(earlier) :]
        copies = [
            pltpu.make_async_copy(source, room, sems.at[index])
            for index, (source, room) in enumerate(((mine, low_mine), (theirs, low_theirs)))
        ]
        for copy in copies:
            copy.start()
        leaving = []
        for index, (room, made, place) in enumerate(
            ((low_mine, first, mp_place()), (low_theirs, second, 1 - mp_place()))
        ):
            copies[index].wait()
            made[...] = room[...].astype(kind)
            leaving.append(pltpu.make_async_copy(made, target.at[place], sems.at[2 + index]))
            leaving[-1].start()
        for copy in leaving:
            copy.wait()

    space = pl.BlockSpec(memory_space=pltpu.HBM)
    return pl.pallas_call(
        kernel,
        out_shape=jax.ShapeDtypeStruct((2, length, width), kind),
        in_specs=[pl.BlockSpec(memory_space=pl.ANY)] * 2 + [pl.BlockSpec(memory_space=pl.ANY)] * len(earlier),
        out_specs=space,
        scratch_shapes=[pltpu.VMEM(own.shape, own.dtype), pltpu.VMEM(own.shape, received.dtype)]
        + [pltpu.VMEM(own.shape, kind)] * 2
        + [pltpu.SemaphoreType.DMA((4,))],
        compiler_params=pltpu.CompilerParams(vmem_limit_bytes=24 * 2**20),
        cost_estimate=pl.CostEstimate(flops=weight[0], bytes_accessed=1, transcendentals=0),
        name="place_rows",
    )(own, received, *earlier)


def mix_back_body(last, get, made, done, extra, pads_ref):
    low, flat, work = extra
    normed_grad, summed, vectors = (get(index) for index in range(3))
    length, width = summed.shape
    half = length // 2
    sums = [jnp.zeros((1, width), wide_type)] * 2
    for rows in tiles(length, row_tile):
        grad = normed_grad[rows, :]
        normal, inverse = normalize(summed[rows, :])
        value = norm_backward(grad, normal, inverse, row_of(vectors, 0))
        work[rows, :] = value
        low[rows, :] = value.astype(low_type)
        sums[0] = sums[0] + jnp.sum(grad * normal, axis=0, keepdims=True)
        sums[1] = sums[1] + jnp.sum(grad, axis=0, keepdims=True)
    pair_table = get(3)
    for step in range(2):
        flat[:, step * width : (step + 1) * width] = dot(
            pair_table[:, step * length : (step + 1) * length], low[...]
        ).astype(low_type)
    work[...] += dot(flat[...], get(4)[...])
    small = made[0]
    small[...] = jnp.zeros_like(small)
    if last:
        for rows in tiles(length, row_tile):
            value = work[rows, :] * live_rows(pads_ref, rows, length)
            start = rows.start % half
            target = made[1 + rows.start // half]
            target[start : start + row_tile, :] = value.astype(target.dtype)
    else:
        residual, below = get(5), get(6)
        out_sums = [jnp.zeros((1, width), wide_type)] * 3
        for rows in tiles(length, row_tile):
            grad = work[rows, :] * live_rows(pads_ref, rows, length)
            made[1][rows, :], made[2][rows, :] = out_rows(
                grad, residual[rows, :], row_of(below, 3), out_sums
            )
        sums = sums + out_sums
        done(1, 2)
        own, other = get(7), get(8)
        hiddens = (own.at[0], own.at[1], other.at[0], other.at[1])
        down_grads(hiddens, made[2], made, done, 3, 4)
    for index, value in enumerate(sums):
        small[index : index + 1, :] = value


def mix_back(normed_grad, summed, vectors, tables, pads, below=None, earlier=()):
    pair_table, _, stack_table = tables
    length, width = rows = summed.shape
    loads = [whole(array) for array in (normed_grad, summed, vectors)]
    loads += [part(pair_table, mp_place), whole(stack_table)]
    outs = [((8, width), wide_type)]
    flops = 4 * length * width * (length + width)
    if below is None:
        half = (length // 2, width)
        outs += [(half, wide_type), (half, low_type)]
    else:
        loads += [whole(array) for array in below]
        size = below[2].shape[2]
        outs += [(rows, wide_type), (rows, low_type)] + [((2, size, width), low_type)] * 2
        flops += 8 * length * width * size
    return staged(
        "mix_back",
        functools.partial(mix_back_body, below is None),
        loads,
        outs,
        earlier,
        [
            pltpu.VMEM(rows, low_type),
            pltpu.VMEM((length, 2 * width), low_type),
            pltpu.VMEM(rows, wide_type),
        ],
        flops,
        20,
    )(pads)


def layer_mix(layer_in, live_mask, params, tables):
    gain_mix, shift_mix = params[:2]
    pair_table, wide_table, stack_table = tables
    width = layer_in.shape[1]
    masked = layer_in * live_mask
    spectra = dot(masked.astype(low_type), wide_table).astype(low_type)
    stacked = jnp.concatenate([spectra[:, :width], spectra[:, width:]], axis=0)
    summed = masked + dot(pair_table, stacked)
    normal, inverse = normalize(summed)
    normed = normal * gain_mix + shift_mix
    return summed, normed, normed.astype(low_type)


def layer_hidden(normed_low, up_weight, up_bias):
    return gate_pair(dot(normed_low, up_weight) + up_bias.astype(wide_type))


def layer_out(normed, branch, live_mask, params):
    down_bias, gain_out, shift_out = params[2:]
    residual = normed + branch + down_bias
    out_normal, out_inverse = normalize(residual)
    result = (out_normal * gain_out + shift_out) * live_mask
    return result, residual


def out_backward(result_cot, live_mask, gain_out, residual):
    out_grad = result_cot * live_mask
    out_normal, out_inverse = normalize(residual)
    resid_grad = norm_backward(out_grad, out_normal, out_inverse, gain_out)
    gainout_grad = jnp.sum(out_grad * out_normal, axis=0)
    shiftout_grad = jnp.sum(out_grad, axis=0)
    branch_cot = resid_grad.astype(low_type)
    downbias_grad = jnp.sum(branch_cot, axis=0, dtype=wide_type)
    return resid_grad, branch_cot, (downbias_grad, gainout_grad, shiftout_grad)


def cot_of(branch_cot, down_weight, slope):
    return (dot_nt(branch_cot, down_weight) * slope.astype(wide_type)).astype(low_type)


def mix_backward(normed_grad, live_mask, gain_mix, summed, tables):
    pair_table, wide_table, stack_table = tables
    length = summed.shape[0]
    normal, inverse = normalize(summed)
    summed_grad = norm_backward(normed_grad, normal, inverse, gain_mix)
    gainmix_grad = jnp.sum(normed_grad * normal, axis=0)
    shiftmix_grad = jnp.sum(normed_grad, axis=0)
    summed_low = summed_grad.astype(low_type)
    flat_grad = jnp.concatenate(
        [
            dot(pair_table[:, :length], summed_low).astype(low_type),
            dot(pair_table[:, length:], summed_low).astype(low_type),
        ],
        axis=1,
    )
    masked_grad = (summed_grad + dot(flat_grad, stack_table)) * live_mask
    return masked_grad, (gainmix_grad, shiftmix_grad)


def paired(first, second):
    return dot_tn(*first) + dot_tn(*second)


def core_swap(array):
    return dp_swap(array, dp_bits()[0])


def cut(ref, axis, index):
    return ref.at[(slice(None),) * axis + (index,)]


def moved(name, body, arrays, shapes, scratch, copies, earlier):
    space = pl.BlockSpec(memory_space=pl.ANY if weight[0] > 1 else pltpu.HBM)
    count, late, given = len(arrays), len(earlier), len(shapes)

    def kernel(*refs):
        rest = refs[count + late + given :]
        body(refs[:count], refs[count + late : count + late + given], rest[:-1], rest[-1])

    return pl.pallas_call(
        kernel,
        out_shape=[jax.ShapeDtypeStruct(shape, low_type) for shape in shapes],
        in_specs=[space] * count + [pl.BlockSpec(memory_space=pl.ANY)] * late,
        out_specs=[space] * given,
        cost_estimate=pl.CostEstimate(flops=weight[0], bytes_accessed=1, transcendentals=0),
        scratch_shapes=[pltpu.VMEM(shape, low_type) for shape in scratch]
        + [pltpu.SemaphoreType.DMA((copies,))],
        compiler_params=pltpu.CompilerParams(vmem_limit_bytes=24 * 2**20 if weight[0] > 1 else vmem_bytes),
        name=name,
    )(*arrays, *earlier)


def sum_parts(arrays, views, targets, shapes, part_shape, earlier):
    count, terms = len(views), len(arrays)

    def body(sources, results, held, sems):
        loads = [
            [
                pltpu.make_async_copy(
                    view(source), held[terms * index + side], sems.at[terms * index + side]
                )
                for side, source in enumerate(sources)
            ]
            for index, view in enumerate(views)
        ]
        for group in loads:
            for copy in group:
                copy.start()
        leaving = []
        for index, group in enumerate(loads):
            for copy in group:
                copy.wait()
            rooms = held[terms * index : terms * (index + 1)]
            value = sum(room[...].astype(wide_type) for room in rooms)
            rooms[0][...] = value.astype(low_type)
            leaving.append(
                pltpu.make_async_copy(
                    rooms[0], targets[index](results), sems.at[terms * count + index]
                )
            )
            leaving[-1].start()
        for copy in leaving:
            copy.wait()

    return moved(
        "sum_parts",
        body,
        arrays,
        shapes,
        [part_shape] * (terms * count),
        (terms + 1) * count,
        earlier,
    )


def sum_split(arrays, axis, place, earlier=()):
    shape, count = arrays[0].shape, arrays[0].shape[axis]
    shape = shape[:axis] + shape[axis + 1 :]
    order = [*range(1, count), 0]
    return sum_parts(
        arrays,
        [lambda ref, step=step: cut(ref, axis, place() ^ step) for step in order],
        [lambda refs, step=step: refs[step] for step in order],
        [shape] * count,
        shape,
        earlier,
    )


def sum_whole(arrays, earlier=()):
    shape = arrays[0].shape
    parts = 2 if shape[0] % 2 == 0 and len(shape) > 2 else 1
    size = shape[0] // parts
    spans = [pl.ds(step * size, size) for step in range(parts)]
    return sum_parts(
        arrays,
        [lambda ref, at=at: ref.at[at] for at in spans],
        [lambda refs, at=at: refs[0].at[at] for at in spans],
        [shape],
        (size, *shape[1:]),
        earlier,
    )[0]


def sum_both(first, second, earlier):
    shares, halves, rows, width = first[0].shape
    arrays = (*first, *second)
    jobs = [(kind, half) for half in range(halves) for kind in range(2)]
    part_shape = (shares, rows, width)

    def body(sources, results, held, sems):
        loads = []
        for slot, (kind, half) in enumerate(jobs):
            loads.append(
                [
                    pltpu.make_async_copy(
                        sources[2 * kind + side].at[:, half],
                        held[2 * slot + side],
                        sems.at[2 * slot + side],
                    )
                    for side in range(2)
                ]
            )
            for copy in loads[-1]:
                copy.start()
        leaving = []
        for slot, group in enumerate(loads):
            for copy in group:
                copy.wait()
            left, right = held[2 * slot], held[2 * slot + 1]
            value = left[...].astype(wide_type) + right[...].astype(wide_type)
            left[...] = value.astype(low_type)
            target = results[0].at[:, pl.ds(slot * rows, rows)]
            leaving.append(pltpu.make_async_copy(left, target, sems.at[8 + slot]))
            leaving[-1].start()
        for copy in leaving:
            copy.wait()

    return moved(
        "sum_both",
        body,
        arrays,
        [(shares, 2 * halves * rows, width)],
        [part_shape] * 8,
        12,
        earlier,
    )[0]


def join_parts(arrays, axis, place, earlier=()):
    shape, count = arrays[0].shape, len(arrays)
    whole_shape = shape[:axis] + (count,) + shape[axis:]

    def body(sources, results, held, sems):
        copies = [
            pltpu.make_async_copy(source, room, sems.at[step])
            for step, (source, room) in enumerate(zip(sources, held))
        ]
        for copy in copies:
            copy.start()
        leaving = [
            pltpu.make_async_copy(
                room, cut(results[0], axis, place() ^ step), sems.at[count + step]
            )
            for step, room in enumerate(held)
        ]
        for copy, after in zip(copies, leaving):
            copy.wait()
            after.start()
        for copy in leaving:
            copy.wait()

    return moved(
        "join_parts", body, arrays, [whole_shape], [shape] * count, 2 * count, earlier
    )[0]


def axis_place(axis):
    if axis == "mp":
        return lambda: 0
    if axis == "near":
        return lambda: lax.rem(lax.axis_index("dp") // 2, 2)
    return lambda: lax.axis_index("dp") // 4


def axis_count(axis):
    return lax.axis_size("dp") // 4 if axis == "far" else 2


def axis_swap(array, axis, step):
    if axis == "mp":
        return mp_swap(array)
    return dp_swap(array, (2 if axis == "near" else 4) * step)


class FarTotal:
    def __init__(self, own, received, steps, earlier=()):
        self.axes = ["mp", "far", "near"]
        shape = tuple(axis_count(axis) for axis in self.axes) + (-1, own.shape[-1])
        self.arrays = [own.reshape(shape), received.reshape(shape)]
        self.steps, self.gone = list(steps), []
        self.finish(*earlier)

    def finish(self, *earlier):
        if not self.steps:
            self.total = self.last = sum_whole(self.arrays, earlier)
            return self.last
        name = self.steps.pop(0)
        axis = self.axes.index(name)
        self.axes.pop(axis)
        if name != "mp":
            self.gone.append((name, axis - ("mp" in self.axes)))
        own, *given = sum_split(self.arrays, axis, axis_place(name), earlier)
        self.arrays = [own] + [
            axis_swap(array, name, step + 1) for step, array in enumerate(given)
        ]
        self.last = own
        return own

    def turn(self):
        name, _ = self.gone[-1]
        self.arrays = [self.total] + [
            axis_swap(self.total, name, step) for step in range(1, axis_count(name))
        ]

    def gather(self, *earlier):
        name, axis = self.gone.pop()
        self.total = self.last = join_parts(self.arrays, axis, axis_place(name), earlier)
        if self.gone:
            self.turn()
        else:
            self.total = self.total.reshape(-1, self.total.shape[-1])
        return self.last


def sum_jobs(arrays, jobs, shapes, earlier):
    count = sum(len(sources) for sources, _, _, _ in jobs)

    def body(sources, results, held, sems):
        loads, slot = [], 0
        for views, _, _, _ in jobs:
            loads.append([])
            for index, view in views:
                copy = pltpu.make_async_copy(view(sources[index]), held[slot], sems.at[slot])
                copy.start()
                loads[-1].append((copy, held[slot]))
                slot += 1
        leaving = []
        for place, (group, (_, out, where, _)) in enumerate(zip(loads, jobs)):
            for copy, _ in group:
                copy.wait()
            room = group[0][1]
            value = sum(term[...].astype(wide_type) for _, term in group)
            room[...] = value.astype(low_type)
            leaving.append(
                pltpu.make_async_copy(room, where(results[out]), sems.at[count + place])
            )
            leaving[-1].start()
        for copy in leaving:
            copy.wait()

    scratch = [shape for views, _, _, shape in jobs for _ in views]
    return moved("sum_jobs", body, arrays, shapes, scratch, count + len(jobs), earlier)


def every(ref):
    return ref


class PairTotal:
    def __init__(self, own, received, earlier=()):
        far, width = axis_count("far"), own.shape[-1]
        shape = (2, far, 2, -1, width)
        own, received = own.reshape(shape), received.reshape(shape)
        self.far, self.width, self.half = far, width, own.shape[3] // 2
        top, below = pl.ds(0, self.half), pl.ds(self.half, self.half)
        near = axis_place("near")
        views = (
            lambda ref: ref.at[:, :, near(), top],
            lambda ref: ref.at[:, :, 1 - near(), top],
            lambda ref: ref.at[0, :, :, below],
            lambda ref: ref.at[1, :, :, below],
        )
        shapes = [(2, far, self.half, width)] * 2 + [(far, 2, self.half, width)] * 2
        jobs = [
            ([(0, views[out]), (1, views[out])], out, every, shapes[out]) for out in (1, 3, 0, 2)
        ]
        parts = sum_jobs((own, received), jobs, shapes, earlier)
        self.arrays = (
            parts[0],
            axis_swap(parts[1], "near", 1),
            parts[2],
            mp_swap(parts[3]),
        )
        self.last = parts[0]

    def second(self, *earlier):
        near = axis_place("near")
        views = (
            lambda ref: ref.at[0],
            lambda ref: ref.at[1],
            lambda ref: ref.at[:, near()],
            lambda ref: ref.at[:, 1 - near()],
        )
        shape = (self.far, self.half, self.width)
        jobs = []
        for out in (1, 3, 0, 2):
            first = 2 * (out // 2)
            jobs.append(([(first, views[out]), (first + 1, views[out])], out, every, shape))
        parts = sum_jobs(self.arrays, jobs, [shape] * 4, earlier)
        self.arrays = (
            parts[0],
            mp_swap(parts[1]),
            parts[2],
            axis_swap(parts[3], "near", 1),
        )
        return parts[0]

    def third(self, *earlier):
        place = axis_place("far")
        jobs = []
        for step in (*range(1, self.far), 0):
            for side in range(2):
                jobs.append(
                    (
                        [
                            (2 * side + term, lambda ref, step=step: ref.at[place() ^ step])
                            for term in range(2)
                        ],
                        step,
                        lambda ref, side=side: ref.at[pl.ds(side * self.half, self.half)],
                        (self.half, self.width),
                    )
                )
        shapes = [(2 * self.half, self.width)] * self.far
        own, *given = sum_jobs(self.arrays, jobs, shapes, earlier)
        self.arrays = [own] + [
            axis_swap(array, "far", step + 1) for step, array in enumerate(given)
        ]
        return own


def backward_overlapped(leaving, forward_parts, vectors, tables, blocks, pads, final_out):
    resid, cot, small_out, down_keep, down_send = leaving
    (summed_one, low_one, residual_one, hiddens_one, slopes_one), (summed, low, slopes) = (
        forward_parts
    )
    width = low.shape[1]
    shares = lax.axis_size("dp") // 2
    down_near = core_swap(down_send)
    up_send, total, bias_send = cot_rows(
        cot, low, resid, slopes[1::2], blocks[1][1::2], pads, (), shares
    )
    up_near = core_swap(up_send)
    up_keep, normed_grad, bias_keep = cot_rows(
        cot, low, total, slopes[0::2], blocks[1][0::2], pads, (), shares
    )
    bias_two = (bias_keep, bias_send)
    layer_two = sum_both((down_keep, down_near), (up_keep, up_near), (normed_grad,))
    scattered = lax.psum_scatter(
        layer_two, "dp", scatter_dimension=0, axis_index_groups=core_groups(), tiled=False
    )
    small_mix, resid, cot, down_keep, down_send = mix_back(
        normed_grad,
        summed,
        vectors[1],
        tables,
        pads,
        (residual_one, vectors[0], *hiddens_one),
        (layer_two,),
    )
    down_near = core_swap(down_send)
    up_send, total, bias_send = cot_rows(
        cot, low_one, resid, slopes_one[1::2], blocks[0][1::2], pads
    )
    up_near = core_swap(up_send)
    down_one = FarTotal(down_keep, down_near, ("mp", "far", "near"), (total,))
    up_keep, normed_grad, bias_keep = cot_rows(
        cot, low_one, total, slopes_one[0::2], blocks[0][0::2], pads, (down_one.last,)
    )
    bias_one = (bias_keep, bias_send)
    up_one = PairTotal(up_keep, up_near, (normed_grad,))
    last = down_one.finish(up_one.last)
    small_last, grad_own, grad_given = mix_back(
        normed_grad, summed_one, vectors[0], tables, pads, None, (last,)
    )
    weight[0] = heavy
    last = up_one.second(grad_given)
    small = small_matrix(
        ((small_last, small_mix, *bias_one), (small_mix, small_out, *bias_two)), pads, (last,)
    )
    small_other = mp_swap(small)
    last = down_one.finish(small)
    last = up_one.third(last)
    grad_received = mp_swap(gate(grad_given, last))
    scattered = gate(scattered, last)
    half = scattered.shape[0] // 2
    packed = pack_pieces(
        [[scattered[:half], mp_swap(scattered[half:])], up_one.arrays],
        [small, small_other],
        (last,),
    )
    both = lax.all_gather(packed, "dp", axis=0, tiled=False)
    piece = pack_pieces([down_one.arrays], [], (packed,))
    pieces = [piece] + [axis_swap(piece, "far", step) for step in range(1, axis_count("far"))]
    final_out = place_rows(*final_out, low_type, (piece,))
    input_grad = place_rows(grad_own, grad_received, wide_type, (final_out,))
    joined = join_parts(pieces, 0, axis_place("far"), (input_grad,))
    joined = join_parts([joined, axis_swap(joined, "near", 1)], 1, axis_place("near"))
    joined = joined.reshape(-1, *piece.shape)
    down_one = unpack_pair(joined, core_swap(joined))
    down_two, up_two, up_one, *small = unpack_pieces(both, small.shape[0], (down_one,))
    weight[0] = 1
    return final_out, input_grad, ((up_one, down_one), (up_two, down_two)), small


def backward_plain(grad, live_mask, params, weights, tables, saved):
    large, small, bias = [None] * 2, [None] * 2, [None] * 2
    for level in (1, 0):
        gain_mix, _, _, gain_out, _ = params[level]
        summed, normed_low, residual, kept = saved[level]
        ((up_weight, down_weight),) = weights[level]
        ((hidden, slope),) = kept
        resid_grad, branch_cot, small_out = out_backward(grad, live_mask, gain_out, residual)
        down_grad = dot_tn(hidden, branch_cot).astype(low_type)
        cot = cot_of(branch_cot, down_weight, slope)
        up_grad = dot_tn(normed_low, cot).astype(low_type)
        bias[level] = [jnp.sum(cot, axis=0, dtype=wide_type)]
        grad, small_mix = mix_backward(
            resid_grad + dot_nt(cot, up_weight), live_mask, gain_mix, summed, tables
        )
        small[level] = small_mix + small_out
        large[level] = (total_plain(up_grad, 1), total_plain(down_grad, 0))
    return grad, large, small, bias


def on_device(*arguments):
    inputs, pad_counts = arguments[:2]
    layer_args = (arguments[2:10], arguments[10:18])
    cotangent = arguments[18]
    mp_count = lax.axis_size("mp")
    mine = lax.axis_index("mp")
    feature_width = inputs.shape[2]
    row_length = inputs.shape[1] * mp_count
    cos_seq, sin_seq = fourier_table(row_length)
    pair_full = np.concatenate([cos_seq, -sin_seq], axis=1)
    turned = 1 - 2 * ((np.arange(row_length)[:, None] + np.arange(2 * row_length)[None, :]) % 2)
    if mp_count == 2:
        pair_table = jnp.asarray(np.stack([pair_full, pair_full * turned]), low_type)
    else:
        pair_table = jnp.asarray(pair_full, low_type)
    wide_table = jnp.asarray(np.concatenate(fourier_table(feature_width), axis=1), low_type)
    stack_table = jnp.asarray(np.concatenate(fourier_table(feature_width), axis=0), low_type)
    tables = (pair_table, wide_table, stack_table)
    (up_one, down_one), (up_two, down_two) = [(args[2], args[4]) for args in layer_args]
    biases = jnp.stack([args[3] for args in layer_args])
    if mp_count == 2:
        core, near, far = dp_bits()[:3]
        core_bit = bit_of(core)
        own_rows, up_part, down_part = cut_first(up_one, up_two, down_two)
        own_rows = mp_swap(own_rows)
        given, block, given_cot = cut_next(inputs, cotangent, down_one, (own_rows,))
        up_part, down_part = mp_swap(up_part), mp_swap(down_part)
        received = mp_swap(given)
        far_rows = lax.all_gather(own_rows, "dp", axis=0, tiled=False)
        up_part = fetch_join(up_part, far)
        down_part = fetch_join(down_part, near)
        down_first = mp_swap(gate(block, received))
        other_biases = mp_swap(biases)
        vectors = []
        for level in range(2):
            args = layer_args[level]
            members = [args[0], args[1], args[5], args[6], args[7]]
            members += [
                take_block(array[level], (core_bit + flip) % 2)
                for array in (biases, other_biases)
                for flip in range(2)
            ]
            vectors.append(select_rows(members, 16))
        own_blocks = [
            [own_block(up, down, flip) for flip in range(2)]
            for up, down in ((up_one, down_one), (up_two, down_two))
        ]
        summed_one, normed, low_one, partial, hidden_a, slope_a = enter(
            inputs, received, tables, vectors[0], own_blocks[0], pad_counts
        )
        up_part = fetch_join(gate(up_part, low_one), near)
        down_part = fetch_join(gate(down_part, low_one), far)
        up_near, down_near = core_swap(up_part), core_swap(down_part)
        received_cot = mp_swap(gate(given_cot, down_part))
        down_second = core_swap(down_first)
        far_blocks = [
            (far_columns(far_rows, flip), whole(array))
            for flip, array in enumerate((down_first, down_second))
        ]
        hidden_b, slope_b, residual_one, summed, normed, low, partial, hidden_c, slope_c = middle(
            low_one,
            normed,
            partial,
            tables,
            vectors,
            far_blocks,
            own_blocks[1],
            pad_counts,
        )
        late_blocks = [(whole(up_part), whole(down_part)), (whole(up_near), whole(down_near))]
        out_own, out_given, resid, cot, small_out, slope_d, down_keep, down_send = leave(
            low,
            normed,
            partial,
            vectors[1],
            late_blocks,
            cotangent,
            received_cot,
            hidden_c,
            pad_counts,
        )
        blocks = [own_blocks[0] + far_blocks, own_blocks[1] + late_blocks]
        slopes_one, slopes_two = (
            [part(array, lambda at=at: at) for array in arrays for at in (0, 1)]
            for arrays in ((slope_a, slope_b), (slope_c, slope_d))
        )
        out_received = mp_swap(out_given)
        final_out = (out_own, out_received)
        final_out, input_grad, large, small = backward_overlapped(
            (resid, cot, small_out, down_keep, down_send),
            (
                (summed_one, low_one, residual_one, (hidden_a, hidden_b), slopes_one),
                (summed, low, slopes_two),
            ),
            vectors,
            tables,
            blocks,
            pad_counts,
            final_out,
        )
    else:
        params = [
            tuple(args[step].astype(wide_type) for step in (0, 1, 5, 6, 7)) for args in layer_args
        ]
        position = jnp.arange(row_length, dtype=jnp.int32)
        pads = lax.dynamic_index_in_dim(pad_counts, mine, 0, False)
        live_mask = (position < row_length - pads).astype(wide_type)[:, None]
        weights, saved = [], []
        biases = lax.all_gather(biases, "mp", axis=1, tiled=True)
        current = gathered_row(inputs).astype(wide_type)
        for level, (up_weight, down_weight) in enumerate(((up_one, down_one), (up_two, down_two))):
            up_weight = lax.all_gather(up_weight, "mp", axis=1, tiled=True)
            down_weight = lax.all_gather(down_weight, "mp", axis=0, tiled=True)
            weights.append(((up_weight, down_weight),))
            summed, normed, normed_low = layer_mix(current, live_mask, params[level], tables)
            kept = layer_hidden(normed_low, up_weight, biases[level])
            current, residual = layer_out(
                normed, dot(kept[0], down_weight), live_mask, params[level]
            )
            saved.append((summed, normed_low, residual, (kept,)))
        grad = gathered_row(cotangent).astype(wide_type)
        final_out = return_rows(current.astype(low_type))
        grad, large, small, bias = backward_plain(grad, live_mask, params, weights, tables, saved)
        input_grad = return_rows(grad.astype(low_type)).astype(wide_type)
    hidden_own = layer_args[0][3].shape[0]
    if mp_count != 2:
        rows = []
        for level in range(2):
            rows.extend(small[level])
            rows.extend(bias[level][0].reshape(-1, feature_width))
        total = total_small(select_rows(rows, 8 * -(-len(rows) // 8)))
        count, small = len(rows) // 2, []
        for level in range(2):
            block = total[level * count : (level + 1) * count]
            small += [block[step] for step in range(5)]
            small.append(
                lax.dynamic_slice_in_dim(block[5:].reshape(-1), mine * hidden_own, hidden_own, 0)
            )
    results = [final_out, input_grad]
    for level in range(2):
        gainmix, shiftmix, downbias, gainout, shiftout, bias_total = small[6 * level : 6 * level + 6]
        up_total, down_total = large[level]
        results += [gainmix, shiftmix, up_total, bias_total, down_total, downbias, gainout, shiftout]
    return tuple(results)


def solution(mesh):
    layer_specs = (P(), P(), P(None, "mp"), P("mp"), P("mp", None), P(), P(), P())
    rows = P("dp", "mp", None)
    return jax.shard_map(
        on_device,
        mesh=mesh,
        in_specs=(rows, P("dp"), *layer_specs, *layer_specs, rows),
        out_specs=(rows, rows, *layer_specs, *layer_specs),
        check_vma=False,
    )
```

```python
import functools
import math

import jax
import jax.numpy as jnp
import numpy as np
from jax import lax
from jax.experimental import pallas as pl
from jax.experimental.pallas import tpu as pltpu
from jax.sharding import PartitionSpec as P

norm_eps = 1e-05
low_type = jnp.bfloat16
wide_type = jnp.float32
vmem_bytes = 62 * 2**20
window = 4
heavy = 6 * 10**10
weight = [1]


def fourier_table(points):
    indices = np.arange(points, dtype=np.int64)
    phases = (indices[:, None] * indices[None, :]) % points
    angles = phases.astype(np.float32) * np.float32(2.0 * math.pi / points)
    factor = np.float32(points ** (-0.5))
    return (np.cos(angles) * factor, np.sin(angles) * factor)


def dot(left, right):
    return jnp.dot(left, right, preferred_element_type=wide_type)


def dot_tn(left, right):
    return lax.dot_general(left, right, (((0,), (0,)), ((), ())), preferred_element_type=wide_type)


def dot_nt(left, right):
    return lax.dot_general(left, right, (((1,), (1,)), ((), ())), preferred_element_type=wide_type)


def normalize(activity):
    center = jnp.mean(activity, axis=-1, keepdims=True)
    centered = activity - center
    spread = jnp.mean(centered * centered, axis=-1, keepdims=True)
    inverse = lax.rsqrt(spread + norm_eps)
    return centered * inverse, inverse


def norm_backward(grad, normal, inverse, gain):
    pulled = grad * gain
    first = jnp.mean(pulled, axis=-1, keepdims=True)
    second = jnp.mean(pulled * normal, axis=-1, keepdims=True)
    return inverse * (pulled - first - normal * second)


def gate_pair(preact):
    scale = math.sqrt(2.0 / math.pi)
    square = preact * preact
    turn = jnp.tanh(preact * (scale + (0.044715 * scale) * square))
    half = 0.5 + 0.5 * turn
    hidden = preact * half
    slope = half + hidden * (1.0 - turn) * (scale + (3 * 0.044715 * scale) * square)
    return hidden.astype(low_type), slope.astype(low_type)


def flip_pairs(size, bit):
    return [(index, index ^ bit) for index in range(size)]


def order_halves(bit_value, mine, theirs, axis=0):
    return jnp.where(
        bit_value == 0,
        jnp.concatenate([mine, theirs], axis=axis),
        jnp.concatenate([theirs, mine], axis=axis),
    )


def take_block(array, which, count=2, axis=0):
    size = array.shape[axis] // count
    return lax.dynamic_slice_in_dim(array, which * size, size, axis)


def dp_bits():
    return [1 << level for level in range(lax.axis_size("dp").bit_length() - 1)]


def bit_of(bit):
    return (lax.axis_index("dp") // bit) % 2


def dp_swap(array, bit):
    return lax.ppermute(array, "dp", flip_pairs(lax.axis_size("dp"), bit))


def mp_swap(array):
    return lax.ppermute(array, "mp", [(0, 1), (1, 0)])


def add_low(left, right):
    return (left.astype(wide_type) + right.astype(wide_type)).astype(low_type)


def gate(value, *earlier):
    def kernel(*refs):
        pass

    anywhere = pl.BlockSpec(memory_space=pl.ANY)
    return pl.pallas_call(
        kernel,
        out_shape=jax.ShapeDtypeStruct(value.shape, value.dtype),
        in_specs=[anywhere] * (1 + len(earlier)),
        out_specs=anywhere,
        input_output_aliases={0: 0},
        name="gate",
    )(value, *earlier)


def fetch_join(piece, bit):
    return order_halves(bit_of(bit), piece, dp_swap(piece, bit))


def bounce(name, jobs, shapes, arrays, earlier=()):
    count, late, given = len(arrays), len(earlier), len(shapes)

    def kernel(*refs):
        targets = refs[count + late : count + late + given]
        held, sems = refs[count + late + given : -1], refs[-1]
        work = jobs(refs[:count], held)
        copies = [
            pltpu.make_async_copy(source, target, sems.at[given + index])
            for index, (_, source, target) in enumerate(work)
        ]
        for copy in copies:
            copy.start()
        leaving = [
            pltpu.make_async_copy(source, target, sems.at[index])
            for index, (source, target) in enumerate(zip(held, targets))
        ]
        for slot in range(given):
            for (place, _, _), copy in zip(work, copies):
                if place == slot:
                    copy.wait()
            leaving[slot].start()
        for copy in leaving:
            copy.wait()

    space = pl.BlockSpec(memory_space=pltpu.HBM)
    return pl.pallas_call(
        kernel,
        out_shape=[jax.ShapeDtypeStruct(shape, low_type) for shape in shapes],
        in_specs=[space] * count + [pl.BlockSpec(memory_space=pl.ANY)] * late,
        out_specs=[space] * given,
        scratch_shapes=[pltpu.VMEM(shape, low_type) for shape in shapes]
        + [pltpu.SemaphoreType.DMA((4 * given,))],
        compiler_params=pltpu.CompilerParams(vmem_limit_bytes=vmem_bytes),
        name=name,
    )(*arrays, *earlier)


def span(index, count):
    return pl.ds(pl.multiple_of(index * count, count), count)


def cut_first(up_one, up_two, down_two):
    width, size = up_one.shape[0], up_one.shape[1] // 2
    rows = width // lax.axis_size("dp")
    quarter = (width // 4, size // 4)

    def jobs(sources, held):
        place, core = lax.axis_index("dp"), core_place()
        near, away = lax.rem(place // 2, 2), lax.rem(place // 4, 2)
        own = sources[0].at[span(place, rows)]
        return [
            (0, own.at[:, pl.ds(0, size)], held[0].at[pl.ds(0, rows)]),
            (0, own.at[:, pl.ds(size, size)], held[0].at[pl.ds(rows, rows)]),
            (1, sources[1].at[span(2 * near + away, quarter[0]), span(core, size)], held[1]),
            (2, sources[2].at[span(core * 4 + 2 * away + near, quarter[1])], held[2]),
        ]

    shapes = ((2 * rows, size), (quarter[0], size), (quarter[1], width))
    return bounce("cut_first", jobs, shapes, (up_one, up_two, down_two))


def cut_next(inputs, cotangent, down_one, earlier):
    length, width = cotangent.shape[1:]
    size = down_one.shape[0] // 2

    def jobs(sources, held):
        rows, cots, down = sources
        return [
            (0, rows.at[1 - mp_place()], held[0]),
            (1, down.at[span(core_place(), size)], held[1]),
            (2, cots.at[1 - mp_place()], held[2]),
        ]

    shapes = ((length, width), (size, width), (length, width))
    return bounce("cut_next", jobs, shapes, (inputs, cotangent, down_one), earlier)


def select_rows(rows, count):
    index = lax.broadcasted_iota(jnp.int32, (count, rows[0].shape[0]), 0)
    total = jnp.zeros(index.shape, wide_type)
    for place, row in enumerate(rows):
        total = jnp.where(index == place, row.astype(wide_type)[None], total)
    return total


def core_groups():
    return [
        [place for place in range(lax.axis_size("dp")) if place % 2 == which] for which in (0, 1)
    ]


def total_plain(part, hidden_axis):
    own = lax.psum_scatter(part, "mp", scatter_dimension=hidden_axis, tiled=True)
    return lax.psum(own, "dp").astype(wide_type)


def total_small(vector):
    for bit in dp_bits():
        vector = vector + dp_swap(vector, bit)
    if lax.axis_size("mp") == 2:
        return vector + mp_swap(vector)
    return lax.psum(vector, "mp")


def given_row(array):
    return lax.dynamic_index_in_dim(array, 1 - lax.axis_index("mp"), 0, keepdims=False)


def gathered_row(array):
    return lax.all_to_all(array, "mp", split_axis=0, concat_axis=1, tiled=True)[0]


def return_rows(array):
    return lax.all_to_all(array[None], "mp", split_axis=1, concat_axis=0, tiled=True)


def staged(name, body, loads, outs, earlier=(), scratch=(), flops=0, stress=0):
    count, late, given = len(loads), len(earlier), len(outs)

    def kernel(*refs):
        sources = refs[1 : 1 + count]
        targets = refs[1 + count + late : 1 + count + late + given]
        rest = refs[1 + count + late + given :]
        held, made = rest[:count], rest[count : count + given]
        in_sems, out_sems, *extra = rest[count + given :]
        copies, begun, sent = {}, set(), []
        for index, load in enumerate(loads):
            view = load[2](sources[index])
            copies[index] = pltpu.make_async_copy(view, held[index], in_sems.at[index])
        queue = sorted(range(count), key=lambda index: math.prod(loads[index][1]) > 2**16)

        def begin(index):
            if index not in begun:
                copies[index].start()
                begun.add(index)

        def get(index):
            begin(index)
            if index in copies:
                copies.pop(index).wait()
                while sum(place in copies for place in begun) < window and len(begun) < count:
                    begin(next(place for place in queue if place not in begun))
            return held[index]

        for index in queue:
            if math.prod(loads[index][1]) <= 2**16 or len(begun) < window:
                begin(index)

        def done(*indices):
            for index in indices:
                slot = len(sent)
                if isinstance(index, tuple):
                    index, place = index
                    source, target = made[index].at[place], targets[index].at[place]
                else:
                    source, target = made[index], targets[index]
                copy = pltpu.make_async_copy(source, target, out_sems.at[slot])
                copy.start()
                sent.append((index, copy))

        body(get, made, done, extra, refs[0])
        for index in list(copies):
            get(index)
        left = {index for index, _ in sent}
        done(*[index for index in range(given) if index not in left])
        for _, copy in sent:
            copy.wait()

    space = pl.BlockSpec(memory_space=pltpu.HBM)
    moved = sum(math.prod(load[1]) * load[0].dtype.itemsize for load in loads)
    moved += sum(math.prod(out[0]) * jnp.dtype(out[1]).itemsize for out in outs)
    call = pl.pallas_call(
        kernel,
        out_shape=[jax.ShapeDtypeStruct(*out) for out in outs],
        in_specs=[pl.BlockSpec(memory_space=pltpu.SMEM)]
        + [space] * count
        + [pl.BlockSpec(memory_space=pl.ANY)] * late,
        out_specs=[space] * given,
        cost_estimate=pl.CostEstimate(
            flops=1 + stress * flops, bytes_accessed=1 + stress * moved, transcendentals=0
        ),
        scratch_shapes=[pltpu.VMEM(load[1], load[0].dtype) for load in loads]
        + [pltpu.VMEM(*out) for out in outs]
        + [pltpu.SemaphoreType.DMA((count,)), pltpu.SemaphoreType.DMA((2 * given,))]
        + list(scratch),
        compiler_params=pltpu.CompilerParams(vmem_limit_bytes=vmem_bytes),
        name=name,
    )
    return lambda pads: call(pads, *[load[0] for load in loads], *earlier)


def whole(array):
    return (array, array.shape, lambda ref: ref)


def part(array, index):
    return (array, array.shape[1:], lambda ref: ref.at[index()])


def mp_place():
    return lax.axis_index("mp")


def core_place():
    return lax.rem(lax.axis_index("dp"), 2)


def share(flip):
    return (core_place() + flip) % 2


def own_block(up_weight, down_weight, flip):
    width, size = up_weight.shape[0], up_weight.shape[1] // 2

    def span():
        return pl.ds(pl.multiple_of(share(flip) * size, size), size)

    return (
        (up_weight, (width, size), lambda ref: ref.at[:, span()]),
        (down_weight, (size, width), lambda ref: ref.at[span()]),
    )


def far_columns(pieces, flip):
    places, rows, size = pieces.shape
    half = rows // 2
    return (
        pieces,
        (places, half, size),
        lambda ref: ref.at[:, pl.ds(pl.multiple_of(share(flip) * half, half), half)],
    )


def matrix(ref):
    return ref[...].reshape(-1, ref.shape[-1])


def tiles(total, size):
    return [slice(start, start + size) for start in range(0, total, size)]


def live_rows(pads_ref, rows, length):
    place = lax.broadcasted_iota(jnp.int32, (rows.stop - rows.start, 1), 0) + rows.start
    place = lax.rem(place + mp_place() * (length // 2), length)
    return (place < length - pads_ref[mp_place()]).astype(wide_type)


def row_of(ref, index):
    return ref[index : index + 1, :]


row_tile = 128


def mix_rows(summed, normed, low, spectra, wide_table, pair_table, vectors):
    length, width = summed.shape
    low[...] = summed[...].astype(low_type)
    wide = wide_table()
    for columns in tiles(2 * width, width):
        spectra[:, columns] = dot(low[...], wide[:, columns]).astype(low_type)
    pair = pair_table()
    summed[...] += dot(pair[:, :length], spectra[:, :width])
    summed[...] += dot(pair[:, length:], spectra[:, width:])
    for rows in tiles(length, row_tile):
        normal, _ = normalize(summed[rows, :])
        value = normal * row_of(vectors, 0) + row_of(vectors, 1)
        normed[rows, :] = value
        low[rows, :] = value.astype(low_type)


def feed_block(low, up_weight, bias, down_weight, hidden, slope):
    hidden[...], slope[...] = gate_pair(dot(low[...], matrix(up_weight())) + bias)
    return dot(hidden[...], matrix(down_weight()))


def out_norm(residual, normed, parts, vectors):
    for rows in tiles(residual.shape[0], row_tile):
        value = normed[rows, :]
        for item in parts:
            value = value + item[rows, :]
        value = value + row_of(vectors, 2)
        residual[rows, :] = value
        normal, _ = normalize(value)
        yield rows, normal * row_of(vectors, 3) + row_of(vectors, 4)


def enter_body(get, made, done, extra, pads_ref):
    summed, normed, low, partial, hidden, slope = made
    (spectra,) = extra
    length, width = summed.shape
    half = length // 2
    for rows in tiles(length, row_tile):
        start = rows.start % half
        piece = get(rows.start // half)[start : start + row_tile, :].astype(wide_type)
        summed[rows, :] = piece * live_rows(pads_ref, rows, length)
    vectors = get(4)
    mix_rows(summed, normed, low, spectra, lambda: get(2), lambda: get(3), vectors)
    done(0, 1, 2)
    for block in range(2):
        value = feed_block(
            low,
            lambda: get(5 + 2 * block),
            row_of(vectors, 5 + block),
            lambda: get(6 + 2 * block),
            hidden.at[block],
            slope.at[block],
        )
        done((4, block), (5, block))
        partial[...] = value if block == 0 else partial[...] + value


def enter(inputs, received, tables, vectors, blocks, pads):
    pair_table, wide_table, _ = tables
    length, width = 2 * received.shape[0], received.shape[1]
    size = blocks[0][0][1][1]
    loads = [part(inputs, mp_place), whole(received), whole(wide_table)]
    loads += [part(pair_table, mp_place), whole(vectors), *blocks[0], *blocks[1]]
    rows = (length, width)
    return staged(
        "enter",
        enter_body,
        loads,
        [(rows, wide_type), (rows, wide_type), (rows, low_type), (rows, wide_type)]
        + [((2, length, size), low_type)] * 2,
        (),
        [pltpu.VMEM((length, 2 * width), low_type)],
        4 * length * width * (length + width + 2 * size),
    )(pads)


def middle_body(get, made, done, extra, pads_ref):
    hidden, slope, residual, summed, normed, low, partial, hidden_two, slope_two = made
    spectra, total = extra
    length = summed.shape[0]
    low_one, vectors = get(0), get(5)
    for block in range(2):
        value = feed_block(
            low_one,
            lambda: get(1 + 2 * block),
            row_of(vectors, 7 + block),
            lambda: get(2 + 2 * block),
            hidden.at[block],
            slope.at[block],
        )
        done((0, block), (1, block))
        total[...] = value if block == 0 else total[...] + value
    for rows, value in out_norm(residual, get(6), (total, get(7)), vectors):
        summed[rows, :] = value * live_rows(pads_ref, rows, length)
    done(2)
    vectors = get(10)
    mix_rows(summed, normed, low, spectra, lambda: get(8), lambda: get(9), vectors)
    done(3, 4, 5)
    for block in range(2):
        value = feed_block(
            low,
            lambda: get(11 + 2 * block),
            row_of(vectors, 5 + block),
            lambda: get(12 + 2 * block),
            hidden_two.at[block],
            slope_two.at[block],
        )
        done((7, block), (8, block))
        partial[...] = value if block == 0 else partial[...] + value


def middle(low, normed, partial, tables, vectors, far_blocks, own_blocks, pads, earlier=()):
    pair_table, wide_table, _ = tables
    length, width = rows = low.shape
    size = own_blocks[0][0][1][1]
    loads = [whole(low), *far_blocks[0], *far_blocks[1], whole(vectors[0])]
    loads += [whole(normed), whole(partial), whole(wide_table), part(pair_table, mp_place)]
    loads += [whole(vectors[1]), *own_blocks[0], *own_blocks[1]]
    hidden = ((2, length, size), low_type)
    return staged(
        "middle",
        middle_body,
        loads,
        [hidden, hidden, (rows, wide_type), (rows, wide_type), (rows, wide_type)]
        + [(rows, low_type), (rows, wide_type), hidden, hidden],
        earlier,
        [pltpu.VMEM((length, 2 * width), low_type), pltpu.VMEM(rows, wide_type)],
        4 * length * width * (length + width + 4 * size),
    )(pads)


def down_grads(hiddens, cot, made, done, keep, send):
    for step, index in ((1, send), (0, keep)):
        target = made[index]
        for half in range(2):
            value = dot_tn(hiddens[2 * half + step][...], cot[...]).astype(low_type)
            if len(target.shape) == 4:
                target[:, half] = value.reshape(target.shape[0], *target.shape[2:])
                place = (slice(None), half)
            else:
                target[half] = value
                place = half
            done((index, place))


def leave_body(get, made, done, extra, pads_ref):
    out_own, out_given, resid, cot, small, slope, keep, send = made
    hidden, total, residual = extra
    length, width = resid.shape
    half = length // 2
    low, vectors = get(0), get(5)
    for block in range(2):
        value = feed_block(
            low,
            lambda: get(1 + 2 * block),
            row_of(vectors, 7 + block),
            lambda: get(2 + 2 * block),
            hidden.at[block],
            slope.at[block],
        )
        done((5, block))
        total[...] = value if block == 0 else total[...] + value
    sums = [jnp.zeros((1, width), wide_type)] * 3
    for rows, value in out_norm(residual, get(6), (total, get(7)), vectors):
        live = live_rows(pads_ref, rows, length)
        start = rows.start % half
        target = (out_own, out_given)[rows.start // half]
        target[start : start + row_tile, :] = (value * live).astype(low_type)
        grad = get(8 + rows.start // half)[start : start + row_tile, :].astype(wide_type) * live
        resid[rows, :], cot[rows, :] = out_rows(grad, residual[rows, :], row_of(vectors, 3), sums)
    small[...] = jnp.zeros_like(small)
    for index, value in enumerate(sums):
        small[index : index + 1, :] = value
    done(0, 1, 2, 3, 4)
    own = get(10)
    down_grads((own.at[0], own.at[1], hidden.at[0], hidden.at[1]), cot, made, done, 6, 7)


def leave(low, normed, partial, vectors, blocks, cotangent, received, hidden, pads, earlier=()):
    length, width = rows = low.shape
    size = hidden.shape[2]
    shares = lax.axis_size("dp") // 2
    loads = [whole(low), *blocks[0], *blocks[1], whole(vectors), whole(normed), whole(partial)]
    loads += [part(cotangent, mp_place), whole(received), whole(hidden)]
    half, grads = (length // 2, width), ((shares, 2, size // shares, width), low_type)
    return staged(
        "leave",
        leave_body,
        loads,
        [(half, low_type), (half, low_type), (rows, wide_type), (rows, low_type)]
        + [((8, width), wide_type), ((2, length, size), low_type), grads, grads],
        earlier,
        [pltpu.VMEM((2, length, size), low_type)] + [pltpu.VMEM(rows, wide_type)] * 2,
        16 * length * width * size,
    )(pads)


def out_rows(grad, residual, gain, sums):
    normal, inverse = normalize(residual)
    resid_grad = norm_backward(grad, normal, inverse, gain)
    low = resid_grad.astype(low_type)
    parts = (grad * normal, grad, low.astype(wide_type))
    for index, value in enumerate(parts):
        sums[index] = sums[index] + jnp.sum(value, axis=0, keepdims=True)
    return resid_grad, low


def cot_body(get, made, done, extra, pads_ref):
    grads, total, small = made
    (cots,) = extra
    branch_cot = get(0)
    small[...] = jnp.zeros_like(small)
    places = ((1, 2, 5), (6, 7, 8))
    for half in range(2):
        down_weight, slope, up_weight = places[half]
        value = dot_nt(branch_cot[...], matrix(get(down_weight)))
        value = (value * get(slope)[...].astype(wide_type)).astype(low_type)
        cots[...] = value
        small[half : half + 1, :] = jnp.sum(value.astype(wide_type), axis=0, keepdims=True)
        value = dot_tn(get(3)[...], cots[...]).astype(low_type)
        if len(grads.shape) == 4:
            grads[:, half] = value.reshape(grads.shape[0], *grads.shape[2:])
            done((0, (slice(None), half)))
        else:
            grads[half] = value
            done((0, half))
        before, up_weight = (get(4) if half == 0 else total), get(up_weight)
        count = 1 + half
        for rows in tiles(total.shape[0], total.shape[0] // count):
            total[rows, :] = before[rows, :] + dot_nt(cots[rows, :], matrix(up_weight))
            if half:
                done((1, pl.ds(rows.start, rows.stop - rows.start)))


def cot_rows(branch_cot, low, before, slopes, blocks, pads, earlier=(), shares=0):
    length, width = rows = low.shape
    (up_a, down_a), (up_b, down_b) = blocks
    loads = [whole(branch_cot), down_a, slopes[0], whole(low), whole(before), up_a]
    loads += [down_b, slopes[1], up_b]
    size = slopes[0][1][1]
    return staged(
        "cot_rows",
        cot_body,
        loads,
        [
            ((shares, 2, width // shares, size) if shares else (2, width, size), low_type),
            (rows, wide_type),
            ((8, size), wide_type),
        ],
        earlier,
        [pltpu.VMEM((length, size), low_type)],
        12 * length * width * size,
        60,
    )(pads)


def small_body(get, made, done, extra, pads_ref):
    total = made[0]
    width = total.shape[1]
    index = lax.broadcasted_iota(jnp.int32, (4, 1), 0)
    for level in range(2):
        mix, out, *biases = (get(4 * level + step) for step in range(4))
        start = 9 * level
        total[start : start + 2, :] = mix[0:2, :]
        first = 0 if level else 2
        total[start + 2 : start + 3, :] = out[first + 2 : first + 3, :]
        total[start + 3 : start + 5, :] = out[first : first + 2, :]
        rows = jnp.zeros((4, width), wide_type)
        for block in range(4):
            half = (mp_place() + block // 2) % 2
            rows = rows + jnp.where(
                index == 2 * half + share(block % 2),
                biases[block % 2][block // 2 : block // 2 + 1, :],
                0.0,
            )
        total[start + 5 : start + 9, :] = rows
    total[18:, :] = jnp.zeros((total.shape[0] - 18, width), wide_type)


def small_matrix(parts, pads, earlier=()):
    loads = [whole(array) for level in parts for array in level]
    width = parts[0][0].shape[1]
    outs = [((32, width), wide_type)]
    return staged("small_matrix", small_body, loads, outs, earlier)(pads)[0]


def pack_pieces(groups, smalls, earlier):
    arrays = [array for group in groups for array in group]
    width = arrays[0].shape[1]
    heights = [group[0].shape[0] for group in groups]
    small_rows = smalls[0].shape[0] if smalls else 0
    count, late = len(arrays), len(earlier)
    size = sum(heights) + 2 * small_rows

    def kernel(*refs):
        sources, small_refs = refs[:count], refs[count : count + len(smalls)]
        target, packed, *held = refs[count + len(smalls) + late : -1]
        sems = refs[-1]
        copies = [
            pltpu.make_async_copy(source, room, sems.at[index])
            for index, (source, room) in enumerate(zip((*sources, *small_refs), held))
        ]
        for copy in copies:
            copy.start()
        leaving, first = [], 0
        for place, group in enumerate(groups):
            span = slice(sum(heights[:place]), sum(heights[: place + 1]))
            value = 0.0
            for index in range(first, first + len(group)):
                copies[index].wait()
                value = value + held[index][...].astype(wide_type)
            packed[span, :] = value.astype(low_type)
            first += len(group)
        if smalls:
            for copy in copies[count:]:
                copy.wait()
            total = held[count][...] + held[count + 1][...]
            high = total.astype(low_type)
            start = sum(heights)
            packed[start : start + small_rows, :] = high
            packed[start + small_rows :, :] = (total - high.astype(wide_type)).astype(low_type)
        copy = pltpu.make_async_copy(packed, target, sems.at[count + 2])
        copy.start()
        copy.wait()

    space = pl.BlockSpec(memory_space=pl.ANY)
    return pl.pallas_call(
        kernel,
        out_shape=jax.ShapeDtypeStruct((size, width), low_type),
        in_specs=[space] * (count + len(smalls)) + [pl.BlockSpec(memory_space=pl.ANY)] * late,
        out_specs=space,
        scratch_shapes=[pltpu.VMEM((size, width), low_type)]
        + [pltpu.VMEM(array.shape, low_type) for array in arrays]
        + [pltpu.VMEM((small_rows, width), wide_type) for _ in smalls]
        + [pltpu.SemaphoreType.DMA((count + 3,))],
        compiler_params=pltpu.CompilerParams(vmem_limit_bytes=24 * 2**20),
        cost_estimate=pl.CostEstimate(flops=weight[0], bytes_accessed=1, transcendentals=0),
        name="pack_pieces",
    )(*arrays, *smalls, *earlier)


def unpack_pair(mine, theirs):
    shares, rows, width = mine.shape
    size = shares * rows

    def kernel(own, near, down, low, held, sems):
        copies = [
            pltpu.make_async_copy(source, low.at[side], sems.at[side])
            for side, source in enumerate((own, near))
        ]
        for copy in copies:
            copy.start()
        leaving = []
        for side in range(2):
            copies[side].wait()
            held[side] = low[side].reshape(size, width).astype(wide_type)
            where = down.at[pl.ds(pl.multiple_of(share(side) * size, size), size)]
            leaving.append(pltpu.make_async_copy(held.at[side], where, sems.at[2 + side]))
            leaving[-1].start()
        for copy in leaving:
            copy.wait()

    return pl.pallas_call(
        kernel,
        out_shape=jax.ShapeDtypeStruct((2 * size, width), wide_type),
        in_specs=[pl.BlockSpec(memory_space=pl.ANY)] * 2,
        out_specs=pl.BlockSpec(memory_space=pltpu.HBM),
        scratch_shapes=[
            pltpu.VMEM((2, shares, rows, width), low_type),
            pltpu.VMEM((2, size, width), wide_type),
            pltpu.SemaphoreType.DMA((4,)),
        ],
        compiler_params=pltpu.CompilerParams(vmem_limit_bytes=24 * 2**20),
        cost_estimate=pl.CostEstimate(flops=weight[0], bytes_accessed=1, transcendentals=0),
        name="unpack_pair",
    )(mine, theirs)


def unpack_pieces(gathered, small_rows, earlier):
    shares, width = gathered.shape[0] // 2, gathered.shape[2]
    rising = (False, True, True)
    kinds = len(rising)
    rows = (gathered.shape[1] - 2 * small_rows) // kinds
    size = shares * rows
    pieces = gathered.reshape(shares, 2, -1, width)

    def kernel(source, *refs):
        refs = refs[len(earlier) :]
        targets, results = refs[:kinds], refs[kinds : kinds + 12]
        low, held, small, sems = refs[kinds + 12 :]
        jobs = [(kind, core) for kind in range(kinds) for core in range(2)]
        copies = [
            pltpu.make_async_copy(
                source.at[:, core, pl.ds(kind * rows, rows)], low.at[slot], sems.at[slot]
            )
            for slot, (kind, core) in enumerate(jobs)
        ]
        copies.append(
            pltpu.make_async_copy(
                source.at[:, :, pl.ds(kinds * rows, 2 * small_rows)], small, sems.at[4 * kinds]
            )
        )
        for copy in copies:
            copy.start()
        leaving = []
        for slot, (kind, core) in enumerate(jobs):
            copies[slot].wait()
            held[slot] = low[slot].reshape(size, width).astype(wide_type)
            if rising[kind]:
                where = targets[kind].at[:, pl.ds(core * width, width)]
            else:
                where = targets[kind].at[pl.ds(core * size, size)]
            leaving.append(pltpu.make_async_copy(held.at[slot], where, sems.at[2 * kinds + slot]))
            leaving[-1].start()
        copies[-1].wait()
        total = jnp.zeros((2 * small_rows, width), wide_type)
        for place in range(shares):
            for core in range(2):
                total = total + small[place, core].astype(wide_type)
        total = total[:small_rows] + total[small_rows:]
        for level in range(2):
            start = 9 * level
            for step in range(5):
                results[6 * level + step][...] = total[start + step]
            for step in range(2):
                own = jnp.where(
                    mp_place() == 0, total[start + 5 + step], total[start + 7 + step]
                )
                results[6 * level + 5][step * width : (step + 1) * width] = own
        for copy in leaving:
            copy.wait()

    space, inside = pl.BlockSpec(memory_space=pltpu.HBM), pl.BlockSpec(memory_space=pltpu.VMEM)
    shapes = [(size, 2 * width) if up else (2 * size, width) for up in rising]
    shapes += ([(width,)] * 5 + [(2 * width,)]) * 2
    return pl.pallas_call(
        kernel,
        out_shape=[jax.ShapeDtypeStruct(shape, wide_type) for shape in shapes],
        in_specs=[space] + [pl.BlockSpec(memory_space=pl.ANY)] * len(earlier),
        out_specs=[space] * kinds + [inside] * 12,
        scratch_shapes=[
            pltpu.VMEM((2 * kinds, shares, rows, width), low_type),
            pltpu.VMEM((2 * kinds, size, width), wide_type),
            pltpu.VMEM((shares, 2, 2 * small_rows, width), low_type),
            pltpu.SemaphoreType.DMA((4 * kinds + 1,)),
        ],
        compiler_params=pltpu.CompilerParams(vmem_limit_bytes=vmem_bytes),
        cost_estimate=pl.CostEstimate(flops=weight[0], bytes_accessed=1, transcendentals=0),
        name="unpack_pieces",
    )(pieces, *earlier)


def place_rows(own, received, kind, earlier=()):
    length, width = own.shape

    def kernel(mine, theirs, *refs):
        target, low_mine, low_theirs, first, second, sems = refs[len(earlier) :]
        copies = [
            pltpu.make_async_copy(source, room, sems.at[index])
            for index, (source, room) in enumerate(((mine, low_mine), (theirs, low_theirs)))
        ]
        for copy in copies:
            copy.start()
        leaving = []
        for index, (room, made, place) in enumerate(
            ((low_mine, first, mp_place()), (low_theirs, second, 1 - mp_place()))
        ):
            copies[index].wait()
            made[...] = room[...].astype(kind)
            leaving.append(pltpu.make_async_copy(made, target.at[place], sems.at[2 + index]))
            leaving[-1].start()
        for copy in leaving:
            copy.wait()

    space = pl.BlockSpec(memory_space=pltpu.HBM)
    return pl.pallas_call(
        kernel,
        out_shape=jax.ShapeDtypeStruct((2, length, width), kind),
        in_specs=[pl.BlockSpec(memory_space=pl.ANY)] * 2 + [pl.BlockSpec(memory_space=pl.ANY)] * len(earlier),
        out_specs=space,
        scratch_shapes=[pltpu.VMEM(own.shape, own.dtype), pltpu.VMEM(own.shape, received.dtype)]
        + [pltpu.VMEM(own.shape, kind)] * 2
        + [pltpu.SemaphoreType.DMA((4,))],
        compiler_params=pltpu.CompilerParams(vmem_limit_bytes=24 * 2**20),
        cost_estimate=pl.CostEstimate(flops=weight[0], bytes_accessed=1, transcendentals=0),
        name="place_rows",
    )(own, received, *earlier)


def mix_back_body(last, get, made, done, extra, pads_ref):
    low, flat, work = extra
    normed_grad, summed, vectors = (get(index) for index in range(3))
    length, width = summed.shape
    half = length // 2
    sums = [jnp.zeros((1, width), wide_type)] * 2
    for rows in tiles(length, row_tile):
        grad = normed_grad[rows, :]
        normal, inverse = normalize(summed[rows, :])
        value = norm_backward(grad, normal, inverse, row_of(vectors, 0))
        work[rows, :] = value
        low[rows, :] = value.astype(low_type)
        sums[0] = sums[0] + jnp.sum(grad * normal, axis=0, keepdims=True)
        sums[1] = sums[1] + jnp.sum(grad, axis=0, keepdims=True)
    pair_table = get(3)
    for step in range(2):
        flat[:, step * width : (step + 1) * width] = dot(
            pair_table[:, step * length : (step + 1) * length], low[...]
        ).astype(low_type)
    work[...] += dot(flat[...], get(4)[...])
    small = made[0]
    small[...] = jnp.zeros_like(small)
    if last:
        for rows in tiles(length, row_tile):
            value = work[rows, :] * live_rows(pads_ref, rows, length)
            start = rows.start % half
            target = made[1 + rows.start // half]
            target[start : start + row_tile, :] = value.astype(target.dtype)
    else:
        residual, below = get(5), get(6)
        out_sums = [jnp.zeros((1, width), wide_type)] * 3
        for rows in tiles(length, row_tile):
            grad = work[rows, :] * live_rows(pads_ref, rows, length)
            made[1][rows, :], made[2][rows, :] = out_rows(
                grad, residual[rows, :], row_of(below, 3), out_sums
            )
        sums = sums + out_sums
        done(1, 2)
        own, other = get(7), get(8)
        hiddens = (own.at[0], own.at[1], other.at[0], other.at[1])
        down_grads(hiddens, made[2], made, done, 3, 4)
    for index, value in enumerate(sums):
        small[index : index + 1, :] = value


def mix_back(normed_grad, summed, vectors, tables, pads, below=None, earlier=()):
    pair_table, _, stack_table = tables
    length, width = rows = summed.shape
    loads = [whole(array) for array in (normed_grad, summed, vectors)]
    loads += [part(pair_table, mp_place), whole(stack_table)]
    outs = [((8, width), wide_type)]
    flops = 4 * length * width * (length + width)
    if below is None:
        half = (length // 2, width)
        outs += [(half, wide_type), (half, low_type)]
    else:
        loads += [whole(array) for array in below]
        size = below[2].shape[2]
        outs += [(rows, wide_type), (rows, low_type)] + [((2, size, width), low_type)] * 2
        flops += 8 * length * width * size
    return staged(
        "mix_back",
        functools.partial(mix_back_body, below is None),
        loads,
        outs,
        earlier,
        [
            pltpu.VMEM(rows, low_type),
            pltpu.VMEM((length, 2 * width), low_type),
            pltpu.VMEM(rows, wide_type),
        ],
        flops,
        60,
    )(pads)


def layer_mix(layer_in, live_mask, params, tables):
    gain_mix, shift_mix = params[:2]
    pair_table, wide_table, stack_table = tables
    width = layer_in.shape[1]
    masked = layer_in * live_mask
    spectra = dot(masked.astype(low_type), wide_table).astype(low_type)
    stacked = jnp.concatenate([spectra[:, :width], spectra[:, width:]], axis=0)
    summed = masked + dot(pair_table, stacked)
    normal, inverse = normalize(summed)
    normed = normal * gain_mix + shift_mix
    return summed, normed, normed.astype(low_type)


def layer_hidden(normed_low, up_weight, up_bias):
    return gate_pair(dot(normed_low, up_weight) + up_bias.astype(wide_type))


def layer_out(normed, branch, live_mask, params):
    down_bias, gain_out, shift_out = params[2:]
    residual = normed + branch + down_bias
    out_normal, out_inverse = normalize(residual)
    result = (out_normal * gain_out + shift_out) * live_mask
    return result, residual


def out_backward(result_cot, live_mask, gain_out, residual):
    out_grad = result_cot * live_mask
    out_normal, out_inverse = normalize(residual)
    resid_grad = norm_backward(out_grad, out_normal, out_inverse, gain_out)
    gainout_grad = jnp.sum(out_grad * out_normal, axis=0)
    shiftout_grad = jnp.sum(out_grad, axis=0)
    branch_cot = resid_grad.astype(low_type)
    downbias_grad = jnp.sum(branch_cot, axis=0, dtype=wide_type)
    return resid_grad, branch_cot, (downbias_grad, gainout_grad, shiftout_grad)


def cot_of(branch_cot, down_weight, slope):
    return (dot_nt(branch_cot, down_weight) * slope.astype(wide_type)).astype(low_type)


def mix_backward(normed_grad, live_mask, gain_mix, summed, tables):
    pair_table, wide_table, stack_table = tables
    length = summed.shape[0]
    normal, inverse = normalize(summed)
    summed_grad = norm_backward(normed_grad, normal, inverse, gain_mix)
    gainmix_grad = jnp.sum(normed_grad * normal, axis=0)
    shiftmix_grad = jnp.sum(normed_grad, axis=0)
    summed_low = summed_grad.astype(low_type)
    flat_grad = jnp.concatenate(
        [
            dot(pair_table[:, :length], summed_low).astype(low_type),
            dot(pair_table[:, length:], summed_low).astype(low_type),
        ],
        axis=1,
    )
    masked_grad = (summed_grad + dot(flat_grad, stack_table)) * live_mask
    return masked_grad, (gainmix_grad, shiftmix_grad)


def paired(first, second):
    return dot_tn(*first) + dot_tn(*second)


def core_swap(array):
    return dp_swap(array, dp_bits()[0])


def cut(ref, axis, index):
    return ref.at[(slice(None),) * axis + (index,)]


def moved(name, body, arrays, shapes, scratch, copies, earlier):
    space = pl.BlockSpec(memory_space=pl.ANY if weight[0] > 1 else pltpu.HBM)
    count, late, given = len(arrays), len(earlier), len(shapes)

    def kernel(*refs):
        rest = refs[count + late + given :]
        body(refs[:count], refs[count + late : count + late + given], rest[:-1], rest[-1])

    return pl.pallas_call(
        kernel,
        out_shape=[jax.ShapeDtypeStruct(shape, low_type) for shape in shapes],
        in_specs=[space] * count + [pl.BlockSpec(memory_space=pl.ANY)] * late,
        out_specs=[space] * given,
        cost_estimate=pl.CostEstimate(flops=weight[0], bytes_accessed=1, transcendentals=0),
        scratch_shapes=[pltpu.VMEM(shape, low_type) for shape in scratch]
        + [pltpu.SemaphoreType.DMA((copies,))],
        compiler_params=pltpu.CompilerParams(vmem_limit_bytes=24 * 2**20 if weight[0] > 1 else vmem_bytes),
        name=name,
    )(*arrays, *earlier)


def sum_parts(arrays, views, targets, shapes, part_shape, earlier):
    count, terms = len(views), len(arrays)

    def body(sources, results, held, sems):
        loads = [
            [
                pltpu.make_async_copy(
                    view(source), held[terms * index + side], sems.at[terms * index + side]
                )
                for side, source in enumerate(sources)
            ]
            for index, view in enumerate(views)
        ]
        for group in loads:
            for copy in group:
                copy.start()
        leaving = []
        for index, group in enumerate(loads):
            for copy in group:
                copy.wait()
            rooms = held[terms * index : terms * (index + 1)]
            value = sum(room[...].astype(wide_type) for room in rooms)
            rooms[0][...] = value.astype(low_type)
            leaving.append(
                pltpu.make_async_copy(
                    rooms[0], targets[index](results), sems.at[terms * count + index]
                )
            )
            leaving[-1].start()
        for copy in leaving:
            copy.wait()

    return moved(
        "sum_parts",
        body,
        arrays,
        shapes,
        [part_shape] * (terms * count),
        (terms + 1) * count,
        earlier,
    )


def sum_split(arrays, axis, place, earlier=()):
    shape, count = arrays[0].shape, arrays[0].shape[axis]
    shape = shape[:axis] + shape[axis + 1 :]
    order = [*range(1, count), 0]
    return sum_parts(
        arrays,
        [lambda ref, step=step: cut(ref, axis, place() ^ step) for step in order],
        [lambda refs, step=step: refs[step] for step in order],
        [shape] * count,
        shape,
        earlier,
    )


def sum_whole(arrays, earlier=()):
    shape = arrays[0].shape
    parts = 2 if shape[0] % 2 == 0 and len(shape) > 2 else 1
    size = shape[0] // parts
    spans = [pl.ds(step * size, size) for step in range(parts)]
    return sum_parts(
        arrays,
        [lambda ref, at=at: ref.at[at] for at in spans],
        [lambda refs, at=at: refs[0].at[at] for at in spans],
        [shape],
        (size, *shape[1:]),
        earlier,
    )[0]


def sum_both(first, second, earlier):
    shares, halves, rows, width = first[0].shape
    arrays = (*first, *second)
    jobs = [(kind, half) for half in range(halves) for kind in range(2)]
    part_shape = (shares, rows, width)

    def body(sources, results, held, sems):
        loads = []
        for slot, (kind, half) in enumerate(jobs):
            loads.append(
                [
                    pltpu.make_async_copy(
                        sources[2 * kind + side].at[:, half],
                        held[2 * slot + side],
                        sems.at[2 * slot + side],
                    )
                    for side in range(2)
                ]
            )
            for copy in loads[-1]:
                copy.start()
        leaving = []
        for slot, group in enumerate(loads):
            for copy in group:
                copy.wait()
            left, right = held[2 * slot], held[2 * slot + 1]
            value = left[...].astype(wide_type) + right[...].astype(wide_type)
            left[...] = value.astype(low_type)
            target = results[0].at[:, pl.ds(slot * rows, rows)]
            leaving.append(pltpu.make_async_copy(left, target, sems.at[8 + slot]))
            leaving[-1].start()
        for copy in leaving:
            copy.wait()

    return moved(
        "sum_both",
        body,
        arrays,
        [(shares, 2 * halves * rows, width)],
        [part_shape] * 8,
        12,
        earlier,
    )[0]


def join_parts(arrays, axis, place, earlier=()):
    shape, count = arrays[0].shape, len(arrays)
    whole_shape = shape[:axis] + (count,) + shape[axis:]

    def body(sources, results, held, sems):
        copies = [
            pltpu.make_async_copy(source, room, sems.at[step])
            for step, (source, room) in enumerate(zip(sources, held))
        ]
        for copy in copies:
            copy.start()
        leaving = [
            pltpu.make_async_copy(
                room, cut(results[0], axis, place() ^ step), sems.at[count + step]
            )
            for step, room in enumerate(held)
        ]
        for copy, after in zip(copies, leaving):
            copy.wait()
            after.start()
        for copy in leaving:
            copy.wait()

    return moved(
        "join_parts", body, arrays, [whole_shape], [shape] * count, 2 * count, earlier
    )[0]


def axis_place(axis):
    if axis == "mp":
        return lambda: 0
    if axis == "near":
        return lambda: lax.rem(lax.axis_index("dp") // 2, 2)
    return lambda: lax.axis_index("dp") // 4


def axis_count(axis):
    return lax.axis_size("dp") // 4 if axis == "far" else 2


def axis_swap(array, axis, step):
    if axis == "mp":
        return mp_swap(array)
    return dp_swap(array, (2 if axis == "near" else 4) * step)


class FarTotal:
    def __init__(self, own, received, steps, earlier=()):
        self.axes = ["mp", "far", "near"]
        shape = tuple(axis_count(axis) for axis in self.axes) + (-1, own.shape[-1])
        self.arrays = [own.reshape(shape), received.reshape(shape)]
        self.steps, self.gone = list(steps), []
        self.finish(*earlier)

    def finish(self, *earlier):
        if not self.steps:
            self.total = self.last = sum_whole(self.arrays, earlier)
            return self.last
        name = self.steps.pop(0)
        axis = self.axes.index(name)
        self.axes.pop(axis)
        if name != "mp":
            self.gone.append((name, axis - ("mp" in self.axes)))
        own, *given = sum_split(self.arrays, axis, axis_place(name), earlier)
        self.arrays = [own] + [
            axis_swap(array, name, step + 1) for step, array in enumerate(given)
        ]
        self.last = own
        return own

    def turn(self):
        name, _ = self.gone[-1]
        self.arrays = [self.total] + [
            axis_swap(self.total, name, step) for step in range(1, axis_count(name))
        ]

    def gather(self, *earlier):
        name, axis = self.gone.pop()
        self.total = self.last = join_parts(self.arrays, axis, axis_place(name), earlier)
        if self.gone:
            self.turn()
        else:
            self.total = self.total.reshape(-1, self.total.shape[-1])
        return self.last


def sum_jobs(arrays, jobs, shapes, earlier):
    count = sum(len(sources) for sources, _, _, _ in jobs)

    def body(sources, results, held, sems):
        loads, slot = [], 0
        for views, _, _, _ in jobs:
            loads.append([])
            for index, view in views:
                copy = pltpu.make_async_copy(view(sources[index]), held[slot], sems.at[slot])
                copy.start()
                loads[-1].append((copy, held[slot]))
                slot += 1
        leaving = []
        for place, (group, (_, out, where, _)) in enumerate(zip(loads, jobs)):
            for copy, _ in group:
                copy.wait()
            room = group[0][1]
            value = sum(term[...].astype(wide_type) for _, term in group)
            room[...] = value.astype(low_type)
            leaving.append(
                pltpu.make_async_copy(room, where(results[out]), sems.at[count + place])
            )
            leaving[-1].start()
        for copy in leaving:
            copy.wait()

    scratch = [shape for views, _, _, shape in jobs for _ in views]
    return moved("sum_jobs", body, arrays, shapes, scratch, count + len(jobs), earlier)


def every(ref):
    return ref


class PairTotal:
    def __init__(self, own, received, earlier=()):
        far, width = axis_count("far"), own.shape[-1]
        shape = (2, far, 2, -1, width)
        own, received = own.reshape(shape), received.reshape(shape)
        self.far, self.width, self.half = far, width, own.shape[3] // 2
        top, below = pl.ds(0, self.half), pl.ds(self.half, self.half)
        near = axis_place("near")
        views = (
            lambda ref: ref.at[:, :, near(), top],
            lambda ref: ref.at[:, :, 1 - near(), top],
            lambda ref: ref.at[0, :, :, below],
            lambda ref: ref.at[1, :, :, below],
        )
        shapes = [(2, far, self.half, width)] * 2 + [(far, 2, self.half, width)] * 2
        jobs = [
            ([(0, views[out]), (1, views[out])], out, every, shapes[out]) for out in (1, 3, 0, 2)
        ]
        parts = sum_jobs((own, received), jobs, shapes, earlier)
        self.arrays = (
            parts[0],
            axis_swap(parts[1], "near", 1),
            parts[2],
            mp_swap(parts[3]),
        )
        self.last = parts[0]

    def second(self, *earlier):
        near = axis_place("near")
        views = (
            lambda ref: ref.at[0],
            lambda ref: ref.at[1],
            lambda ref: ref.at[:, near()],
            lambda ref: ref.at[:, 1 - near()],
        )
        shape = (self.far, self.half, self.width)
        jobs = []
        for out in (1, 3, 0, 2):
            first = 2 * (out // 2)
            jobs.append(([(first, views[out]), (first + 1, views[out])], out, every, shape))
        parts = sum_jobs(self.arrays, jobs, [shape] * 4, earlier)
        self.arrays = (
            parts[0],
            mp_swap(parts[1]),
            parts[2],
            axis_swap(parts[3], "near", 1),
        )
        return parts[0]

    def third(self, *earlier):
        place = axis_place("far")
        jobs = []
        for step in (*range(1, self.far), 0):
            for side in range(2):
                jobs.append(
                    (
                        [
                            (2 * side + term, lambda ref, step=step: ref.at[place() ^ step])
                            for term in range(2)
                        ],
                        step,
                        lambda ref, side=side: ref.at[pl.ds(side * self.half, self.half)],
                        (self.half, self.width),
                    )
                )
        shapes = [(2 * self.half, self.width)] * self.far
        own, *given = sum_jobs(self.arrays, jobs, shapes, earlier)
        self.arrays = [own] + [
            axis_swap(array, "far", step + 1) for step, array in enumerate(given)
        ]
        return own


def backward_overlapped(leaving, forward_parts, vectors, tables, blocks, pads, final_out):
    resid, cot, small_out, down_keep, down_send = leaving
    (summed_one, low_one, residual_one, hiddens_one, slopes_one), (summed, low, slopes) = (
        forward_parts
    )
    width = low.shape[1]
    shares = lax.axis_size("dp") // 2
    down_near = core_swap(down_send)
    up_send, total, bias_send = cot_rows(
        cot, low, resid, slopes[1::2], blocks[1][1::2], pads, (), shares
    )
    up_near = core_swap(up_send)
    up_keep, normed_grad, bias_keep = cot_rows(
        cot, low, total, slopes[0::2], blocks[1][0::2], pads, (), shares
    )
    bias_two = (bias_keep, bias_send)
    layer_two = sum_both((down_keep, down_near), (up_keep, up_near), (normed_grad,))
    scattered = lax.psum_scatter(
        layer_two, "dp", scatter_dimension=0, axis_index_groups=core_groups(), tiled=False
    )
    small_mix, resid, cot, down_keep, down_send = mix_back(
        normed_grad,
        summed,
        vectors[1],
        tables,
        pads,
        (residual_one, vectors[0], *hiddens_one),
        (layer_two,),
    )
    down_near = core_swap(down_send)
    up_send, total, bias_send = cot_rows(
        cot, low_one, resid, slopes_one[1::2], blocks[0][1::2], pads
    )
    up_near = core_swap(up_send)
    down_one = FarTotal(down_keep, down_near, ("mp", "far", "near"), (total,))
    up_keep, normed_grad, bias_keep = cot_rows(
        cot, low_one, total, slopes_one[0::2], blocks[0][0::2], pads, (down_one.last,)
    )
    bias_one = (bias_keep, bias_send)
    up_one = PairTotal(up_keep, up_near, (normed_grad,))
    last = down_one.finish(up_one.last)
    small_last, grad_own, grad_given = mix_back(
        normed_grad, summed_one, vectors[0], tables, pads, None, (last,)
    )
    weight[0] = heavy
    last = up_one.second(grad_given)
    small = small_matrix(
        ((small_last, small_mix, *bias_one), (small_mix, small_out, *bias_two)), pads, (last,)
    )
    small_other = mp_swap(small)
    last = down_one.finish(small)
    last = up_one.third(last)
    grad_received = mp_swap(gate(grad_given, last))
    scattered = gate(scattered, last)
    half = scattered.shape[0] // 2
    packed = pack_pieces(
        [[scattered[:half], mp_swap(scattered[half:])], up_one.arrays],
        [small, small_other],
        (last,),
    )
    both = lax.all_gather(packed, "dp", axis=0, tiled=False)
    piece = pack_pieces([down_one.arrays], [], (packed,))
    pieces = [piece] + [axis_swap(piece, "far", step) for step in range(1, axis_count("far"))]
    final_out = place_rows(*final_out, low_type, (piece,))
    input_grad = place_rows(grad_own, grad_received, wide_type, (final_out,))
    joined = join_parts(pieces, 0, axis_place("far"), (input_grad,))
    joined = join_parts([joined, axis_swap(joined, "near", 1)], 1, axis_place("near"))
    joined = joined.reshape(-1, *piece.shape)
    down_one = unpack_pair(joined, core_swap(joined))
    down_two, up_two, up_one, *small = unpack_pieces(both, small.shape[0], (down_one,))
    weight[0] = 1
    return final_out, input_grad, ((up_one, down_one), (up_two, down_two)), small


def backward_plain(grad, live_mask, params, weights, tables, saved):
    large, small, bias = [None] * 2, [None] * 2, [None] * 2
    for level in (1, 0):
        gain_mix, _, _, gain_out, _ = params[level]
        summed, normed_low, residual, kept = saved[level]
        ((up_weight, down_weight),) = weights[level]
        ((hidden, slope),) = kept
        resid_grad, branch_cot, small_out = out_backward(grad, live_mask, gain_out, residual)
        down_grad = dot_tn(hidden, branch_cot).astype(low_type)
        cot = cot_of(branch_cot, down_weight, slope)
        up_grad = dot_tn(normed_low, cot).astype(low_type)
        bias[level] = [jnp.sum(cot, axis=0, dtype=wide_type)]
        grad, small_mix = mix_backward(
            resid_grad + dot_nt(cot, up_weight), live_mask, gain_mix, summed, tables
        )
        small[level] = small_mix + small_out
        large[level] = (total_plain(up_grad, 1), total_plain(down_grad, 0))
    return grad, large, small, bias


def on_device(*arguments):
    inputs, pad_counts = arguments[:2]
    layer_args = (arguments[2:10], arguments[10:18])
    cotangent = arguments[18]
    mp_count = lax.axis_size("mp")
    mine = lax.axis_index("mp")
    feature_width = inputs.shape[2]
    row_length = inputs.shape[1] * mp_count
    cos_seq, sin_seq = fourier_table(row_length)
    pair_full = np.concatenate([cos_seq, -sin_seq], axis=1)
    turned = 1 - 2 * ((np.arange(row_length)[:, None] + np.arange(2 * row_length)[None, :]) % 2)
    if mp_count == 2:
        pair_table = jnp.asarray(np.stack([pair_full, pair_full * turned]), low_type)
    else:
        pair_table = jnp.asarray(pair_full, low_type)
    wide_table = jnp.asarray(np.concatenate(fourier_table(feature_width), axis=1), low_type)
    stack_table = jnp.asarray(np.concatenate(fourier_table(feature_width), axis=0), low_type)
    tables = (pair_table, wide_table, stack_table)
    (up_one, down_one), (up_two, down_two) = [(args[2], args[4]) for args in layer_args]
    biases = jnp.stack([args[3] for args in layer_args])
    if mp_count == 2:
        core, near, far = dp_bits()[:3]
        core_bit = bit_of(core)
        own_rows, up_part, down_part = cut_first(up_one, up_two, down_two)
        own_rows = mp_swap(own_rows)
        given, block, given_cot = cut_next(inputs, cotangent, down_one, (own_rows,))
        up_part, down_part = mp_swap(up_part), mp_swap(down_part)
        received = mp_swap(given)
        far_rows = lax.all_gather(own_rows, "dp", axis=0, tiled=False)
        up_part = fetch_join(up_part, far)
        down_part = fetch_join(down_part, near)
        down_first = mp_swap(gate(block, received))
        other_biases = mp_swap(biases)
        vectors = []
        for level in range(2):
            args = layer_args[level]
            members = [args[0], args[1], args[5], args[6], args[7]]
            members += [
                take_block(array[level], (core_bit + flip) % 2)
                for array in (biases, other_biases)
                for flip in range(2)
            ]
            vectors.append(select_rows(members, 16))
        own_blocks = [
            [own_block(up, down, flip) for flip in range(2)]
            for up, down in ((up_one, down_one), (up_two, down_two))
        ]
        summed_one, normed, low_one, partial, hidden_a, slope_a = enter(
            inputs, received, tables, vectors[0], own_blocks[0], pad_counts
        )
        up_part = fetch_join(gate(up_part, low_one), near)
        down_part = fetch_join(gate(down_part, low_one), far)
        up_near, down_near = core_swap(up_part), core_swap(down_part)
        received_cot = mp_swap(gate(given_cot, down_part))
        down_second = core_swap(down_first)
        far_blocks = [
            (far_columns(far_rows, flip), whole(array))
            for flip, array in enumerate((down_first, down_second))
        ]
        hidden_b, slope_b, residual_one, summed, normed, low, partial, hidden_c, slope_c = middle(
            low_one,
            normed,
            partial,
            tables,
            vectors,
            far_blocks,
            own_blocks[1],
            pad_counts,
        )
        late_blocks = [(whole(up_part), whole(down_part)), (whole(up_near), whole(down_near))]
        out_own, out_given, resid, cot, small_out, slope_d, down_keep, down_send = leave(
            low,
            normed,
            partial,
            vectors[1],
            late_blocks,
            cotangent,
            received_cot,
            hidden_c,
            pad_counts,
        )
        blocks = [own_blocks[0] + far_blocks, own_blocks[1] + late_blocks]
        slopes_one, slopes_two = (
            [part(array, lambda at=at: at) for array in arrays for at in (0, 1)]
            for arrays in ((slope_a, slope_b), (slope_c, slope_d))
        )
        out_received = mp_swap(out_given)
        final_out = (out_own, out_received)
        final_out, input_grad, large, small = backward_overlapped(
            (resid, cot, small_out, down_keep, down_send),
            (
                (summed_one, low_one, residual_one, (hidden_a, hidden_b), slopes_one),
                (summed, low, slopes_two),
            ),
            vectors,
            tables,
            blocks,
            pad_counts,
            final_out,
        )
    else:
        params = [
            tuple(args[step].astype(wide_type) for step in (0, 1, 5, 6, 7)) for args in layer_args
        ]
        position = jnp.arange(row_length, dtype=jnp.int32)
        pads = lax.dynamic_index_in_dim(pad_counts, mine, 0, False)
        live_mask = (position < row_length - pads).astype(wide_type)[:, None]
        weights, saved = [], []
        biases = lax.all_gather(biases, "mp", axis=1, tiled=True)
        current = gathered_row(inputs).astype(wide_type)
        for level, (up_weight, down_weight) in enumerate(((up_one, down_one), (up_two, down_two))):
            up_weight = lax.all_gather(up_weight, "mp", axis=1, tiled=True)
            down_weight = lax.all_gather(down_weight, "mp", axis=0, tiled=True)
            weights.append(((up_weight, down_weight),))
            summed, normed, normed_low = layer_mix(current, live_mask, params[level], tables)
            kept = layer_hidden(normed_low, up_weight, biases[level])
            current, residual = layer_out(
                normed, dot(kept[0], down_weight), live_mask, params[level]
            )
            saved.append((summed, normed_low, residual, (kept,)))
        grad = gathered_row(cotangent).astype(wide_type)
        final_out = return_rows(current.astype(low_type))
        grad, large, small, bias = backward_plain(grad, live_mask, params, weights, tables, saved)
        input_grad = return_rows(grad.astype(low_type)).astype(wide_type)
    hidden_own = layer_args[0][3].shape[0]
    if mp_count != 2:
        rows = []
        for level in range(2):
            rows.extend(small[level])
            rows.extend(bias[level][0].reshape(-1, feature_width))
        total = total_small(select_rows(rows, 8 * -(-len(rows) // 8)))
        count, small = len(rows) // 2, []
        for level in range(2):
            block = total[level * count : (level + 1) * count]
            small += [block[step] for step in range(5)]
            small.append(
                lax.dynamic_slice_in_dim(block[5:].reshape(-1), mine * hidden_own, hidden_own, 0)
            )
    results = [final_out, input_grad]
    for level in range(2):
        gainmix, shiftmix, downbias, gainout, shiftout, bias_total = small[6 * level : 6 * level + 6]
        up_total, down_total = large[level]
        results += [gainmix, shiftmix, up_total, bias_total, down_total, downbias, gainout, shiftout]
    return tuple(results)


def solution(mesh):
    layer_specs = (P(), P(), P(None, "mp"), P("mp"), P("mp", None), P(), P(), P())
    rows = P("dp", "mp", None)
    return jax.shard_map(
        on_device,
        mesh=mesh,
        in_specs=(rows, P("dp"), *layer_specs, *layer_specs, rows),
        out_specs=(rows, rows, *layer_specs, *layer_specs),
        check_vma=False,
    )
```
